32 devices in a mesh: section: 4 (over y, x), wide: 8 (over z, core).
Axes of the slice: x: 2, y: 2, z: 4, core: 2. Of those that a mesh axis runs over, the one named last changes fastest.
Arguments:
- patches_in: bfloat16 [4, 6272, 384], P(None, 'wide'), may hold values from -6 to 6
- cotangent: bfloat16 [4, 6272, 384], P(None, 'wide'), may hold values from -6 to 6
- task_ids: int32 [4, 32], P(None, 'wide'), may hold values from 0 to 1
- routes: int32 [4, 6272, 2], P(None, 'wide'), may hold values from 0 to 3, as said below
- keep_mask: int32 [4, 6272, 2], P(None, 'wide'), may hold values from 0 to 1, as said below
- first_gain: float32 [384], replicated, may hold values from 0.5 to 1.5
- first_shift: float32 [384], replicated, may hold values from -1.25 to 1.25
- first_proj: bfloat16 [384, 1152], P('section'), may hold values from -0.3125 to 0.3125
- first_out: bfloat16 [384, 384], P('section'), may hold values from -1.75 to 1.75
- first_bias: float32 [384], replicated, may hold values from -1.25 to 1.25
- dense_gain: float32 [384], replicated, may hold values from 0.5 to 1.5
- dense_shift: float32 [384], replicated, may hold values from -1.25 to 1.25
- dense_up: bfloat16 [384, 1536], P('section'), may hold values from -0.3125 to 0.3125
- hidden_bias: float32 [1536], replicated, may hold values from -3 to 3
- dense_down: bfloat16 [1536, 384], P('section'), may hold values from -0.15625 to 0.15625
- dense_bias: float32 [384], replicated, may hold values from -1.25 to 1.25
- second_gain: float32 [384], replicated, may hold values from 0.5 to 1.5
- second_shift: float32 [384], replicated, may hold values from -1.25 to 1.25
- second_proj: bfloat16 [384, 1152], P('section'), may hold values from -0.3125 to 0.3125
- second_out: bfloat16 [384, 384], P('section'), may hold values from -1.75 to 1.75
- second_bias: float32 [384], replicated, may hold values from -1.25 to 1.25
- mixture_gain: float32 [384], replicated, may hold values from 0.5 to 1.5
- mixture_shift: float32 [384], replicated, may hold values from -1.25 to 1.25
- router: bfloat16 [384, 8], P('section'), may hold values from -0.21875 to 0.21875
- expert_up: bfloat16 [4, 384, 1536], P('section'), may hold values from -0.3125 to 0.3125
- expert_down: bfloat16 [4, 1536, 384], P('section'), may hold values from -0.3125 to 0.3125
Outputs:
- block_output: bfloat16 [4, 6272, 384], P('section', 'wide')
- input_grad: bfloat16 [4, 6272, 384], P('section', 'wide')
- grad_first_gain: float32 [384], P('section')
- grad_first_shift: float32 [384], P('section')
- grad_first_proj: float32 [384, 1152], P('section')
- grad_first_out: float32 [384, 384], P('section')
- grad_first_bias: float32 [384], P('section')
- grad_dense_gain: float32 [384], P('section')
- grad_dense_shift: float32 [384], P('section')
- grad_dense_up: float32 [384, 1536], P('section')
- grad_hidden_bias: float32 [1536], P('section')
- grad_dense_down: float32 [1536, 384], P('section')
- grad_dense_bias: float32 [384], P('section')
- grad_second_gain: float32 [384], P('section')
- grad_second_shift: float32 [384], P('section')
- grad_second_proj: float32 [384, 1152], P('section')
- grad_second_out: float32 [384, 384], P('section')
- grad_second_bias: float32 [384], P('section')
- grad_mixture_gain: float32 [384], P('section')
- grad_mixture_shift: float32 [384], P('section')
- grad_router: float32 [384, 8], P('section')
- grad_expert_up: float32 [4, 384, 1536], P('section')
- grad_expert_down: float32 [4, 1536, 384], P('section')
The draws below stay inside these ranges and needn't reach their ends.
Inputs may be any that keep to these rules, and one draw needn't show every extreme that they name: `routes`: each row names 2 different experts. keep_mask[m, r, k] = 1 exactly when fewer than 488 earlier routes of the same micro-batch and the same 4 * 196 rows of one index of wide (earlier rows, or a smaller k of the same row) name the same expert; in each such block some expert has 488 kept routes.
All inputs are finite; a program needn't handle non-finite values.
Results may differ from the reference program's by a relative error of at most 0.02.
Values may be sent and summed in bfloat16 or wider, within the bound.
A program may use at most 320 MiB of HBM per device.

```python
import jax
import jax.numpy as jnp
from jax import lax

D = 384
HEADS = 6
HEAD_DIM = 64
FF = 1536
PATCHES = 196
EXPERTS = 4
TOPK = 2
TASKS = 2
MICRO = 4
IMG_DEV = 4
IMAGES = 32
ROWS = 6272
CAPACITY = 488


def route_table(key):
    blocks = MICRO * (IMAGES // IMG_DEV)
    length = IMG_DEV * PATCHES
    hot_key, other_key, coin_key, second_key = jax.random.split(key, 4)
    hottest = jax.random.randint(hot_key, (blocks, 1), 0, EXPERTS)
    coin = jax.random.randint(coin_key, (blocks, length), 0, 8)
    other = jax.random.randint(other_key, (blocks, length), 0, EXPERTS)
    first = jnp.where(coin < 7, hottest, other)
    step_ahead = jax.random.randint(second_key, (blocks, length), 1, EXPERTS)
    second = (first + step_ahead) % EXPERTS
    table = jnp.stack([first, second], axis=-1).astype(jnp.int32)
    expert_ids = jnp.arange(EXPERTS, dtype=jnp.int32)
    hits = (table.reshape(blocks, length * 2, 1) == expert_ids[None, None, :]).astype(jnp.int32)
    before = jnp.cumsum(hits, axis=1) - hits
    count_before = jnp.sum(before * hits, axis=-1)
    kept = (count_before < CAPACITY).astype(jnp.int32)
    return (table.reshape(MICRO, ROWS, 2), kept.reshape(MICRO, ROWS, 2))


def draw_routes(key, part):
    table, kept = route_table(key)
    return table


def draw_keep_mask(key, part):
    table, kept = route_table(key)
    return kept


def set_ends(entries, rng, smallest, largest):
    dims = entries.shape
    index_at = [jax.random.randint(jax.random.fold_in(rng, axis), (), 0, dims[axis]) for axis in range(len(dims))]
    entries = entries.at[tuple(index_at)].set(smallest)
    longest = dims.index(max(dims))
    index_at[longest] = (index_at[longest] + 1) % dims[longest]
    return entries.at[tuple(index_at)].set(largest)


def levels(key, dims, cuts, smallest, high):
    level, own = 1.0, jax.random.fold_in(key, 6)
    for dim, shards_of in cuts:
        draws = jnp.exp(jax.random.uniform(jax.random.fold_in(own, dim), (shards_of,), jnp.float32, smallest / len(cuts), high / len(cuts)))
        level = level * jnp.repeat(draws, dims[dim] // shards_of).reshape([-1 if axis == dim else 1 for axis in range(len(dims))])
    return level


def gaussian(stream_key, extent, scale, bound, cuts=(), kind=jnp.bfloat16):
    gain = levels(stream_key, extent, cuts, -0.22, 0.18) if cuts else 1.0
    values = jax.random.normal(stream_key, extent, jnp.float32) * scale * gain
    return jnp.minimum(jnp.maximum(values, -bound), bound).astype(kind)


def setup_inputs(seed: int = 0) -> dict:
    key_list = jax.random.split(jax.random.key(seed), 27)
    patches_in = gaussian(key_list[0], (MICRO, ROWS, D), 1.0, 6.0, ((1, 8),))
    cotangent = gaussian(key_list[1], (MICRO, ROWS, D), 1.0, 6.0, ((1, 8),))
    task_ids = set_ends(jax.random.randint(key_list[2], (MICRO, IMAGES), 0, TASKS), jax.random.fold_in(key_list[2], 1), 0, TASKS - 1).astype(jnp.int32)
    routes = draw_routes(jax.random.fold_in(key_list[26], 71), 0)
    keep_mask = draw_keep_mask(jax.random.fold_in(key_list[26], 71), 0)
    first_gain = jnp.clip(1.0 + 0.1 * jax.random.normal(key_list[5], (D,), jnp.float32), 0.5, 1.5)
    first_shift = gaussian(key_list[6], (D,), 0.2, 1.25, (), jnp.float32)
    first_proj = gaussian(key_list[7], (D, 3 * D), D ** -0.5, 0.3125, ((0, 4),))
    first_out = gaussian(key_list[8], (D, D), (D // 32) ** -0.5, 1.75, ((0, 4),))
    first_bias = gaussian(key_list[9], (D,), 0.2, 1.25, (), jnp.float32)
    dense_gain = jnp.clip(1.0 + 0.1 * jax.random.normal(key_list[10], (D,), jnp.float32), 0.5, 1.5)
    dense_shift = gaussian(key_list[11], (D,), 0.2, 1.25, (), jnp.float32)
    dense_up = gaussian(key_list[12], (D, FF), D ** -0.5, 0.3125, ((0, 4),))
    hidden_bias = gaussian(key_list[13], (FF,), 0.5, 3.0, (), jnp.float32)
    dense_down = gaussian(key_list[14], (FF, D), FF ** -0.5, 0.15625, ((0, 4),))
    dense_bias = gaussian(key_list[15], (D,), 0.2, 1.25, (), jnp.float32)
    second_gain = jnp.clip(1.0 + 0.1 * jax.random.normal(key_list[16], (D,), jnp.float32), 0.5, 1.5)
    second_shift = gaussian(key_list[17], (D,), 0.2, 1.25, (), jnp.float32)
    second_proj = gaussian(key_list[18], (D, 3 * D), D ** -0.5, 0.3125, ((0, 4),))
    second_out = gaussian(key_list[19], (D, D), (D // 32) ** -0.5, 1.75, ((0, 4),))
    second_bias = gaussian(key_list[20], (D,), 0.2, 1.25, (), jnp.float32)
    mixture_gain = jnp.clip(1.0 + 0.1 * jax.random.normal(key_list[21], (D,), jnp.float32), 0.5, 1.5)
    mixture_shift = gaussian(key_list[22], (D,), 0.2, 1.25, (), jnp.float32)
    router = gaussian(key_list[23], (D, TASKS * EXPERTS), (2 * D) ** -0.5, 0.21875, ((0, 4),))
    expert_up = gaussian(key_list[24], (EXPERTS, D, FF), D ** -0.5, 0.3125, ((0, 4),))
    expert_down = gaussian(key_list[25], (EXPERTS, FF, D), (FF // 4) ** -0.5, 0.3125, ((0, 4),))
    return dict(patches_in=patches_in, cotangent=cotangent, task_ids=task_ids, routes=routes, keep_mask=keep_mask, first_gain=first_gain, first_shift=first_shift, first_proj=first_proj, first_out=first_out, first_bias=first_bias, dense_gain=dense_gain, dense_shift=dense_shift, dense_up=dense_up, hidden_bias=hidden_bias, dense_down=dense_down, dense_bias=dense_bias, second_gain=second_gain, second_shift=second_shift, second_proj=second_proj, second_out=second_out, second_bias=second_bias, mixture_gain=mixture_gain, mixture_shift=mixture_shift, router=router, expert_up=expert_up, expert_down=expert_down)


EPSILON = 1e-06
HIGHEST = lax.Precision.HIGHEST

@jax.custom_vjp
def low(v):
    return lax.optimization_barrier(v.astype(jnp.bfloat16)).astype(jnp.float32)

@jax.custom_vjp
def low_back(v):
    return v

def low_keep(v):
    return (low(v), None)

def low_pass(kept, grad):
    return (grad,)

def back_keep(v):
    return (v, None)

def back_low(kept, grad):
    return (low(grad),)
low.defvjp(low_keep, low_pass)
low_back.defvjp(back_keep, back_low)

def layer_norm(residual, norm_gain, norm_shift):
    middle = lax.optimization_barrier(jnp.mean(residual, axis=-1, keepdims=True))
    centered = residual - middle
    spread = lax.optimization_barrier(jnp.mean(centered * centered, axis=-1, keepdims=True))
    return centered * lax.rsqrt(spread + EPSILON) * norm_gain + norm_shift

def matmul(left, right):
    return jnp.dot(left, right, precision=HIGHEST, preferred_element_type=jnp.float32)

def attention(residual, norm_gain, norm_shift, in_weight, out_weight, out_bias):
    images = residual.shape[0] // PATCHES
    normed = low(layer_norm(residual, norm_gain, norm_shift))
    projected = low(low_back(matmul(normed, in_weight)))
    shaped = projected.reshape(images, PATCHES, 3, HEADS, HEAD_DIM)
    scores = jnp.einsum('iqhd,ikhd->ihqk', shaped[:, :, 0], shaped[:, :, 1], precision=HIGHEST)
    scores = low_back(scores * HEAD_DIM ** (-0.5))
    softened = jax.nn.softmax(scores, axis=-1)
    context = jnp.einsum('ihqk,ikhd->iqhd', low(softened), shaped[:, :, 2], precision=HIGHEST)
    context = low(low_back(context.reshape(residual.shape[0], HEADS * HEAD_DIM)))
    return low_back(low(residual + matmul(context, out_weight) + out_bias))

def feed_forward(residual, norm_gain, norm_shift, up_weight, up_bias, down_weight, down_bias):
    normed = low(layer_norm(residual, norm_gain, norm_shift))
    hidden = low_back(matmul(normed, up_weight) + up_bias)
    active = low(jax.nn.gelu(hidden, approximate=False))
    return low_back(low(residual + matmul(active, down_weight) + down_bias))

def mixture(residual, task_rows, route_rows, keep_rows, norm_gain, norm_shift, router, up_weight, down_weight):
    normed = low(layer_norm(residual, norm_gain, norm_shift))
    logits_all = low_back(matmul(normed, router)).reshape(-1, TASKS, EXPERTS)
    picked = (task_rows[:, None] == jnp.arange(TASKS, dtype=jnp.int32)[None, :]).astype(jnp.float32)
    logits = jnp.einsum('rt,rte->re', picked, logits_all, precision=HIGHEST)
    expert_ids = jnp.arange(EXPERTS, dtype=jnp.int32)
    chosen = (route_rows[:, :, None] == expert_ids[None, None, :]) & (keep_rows[:, :, None] == 1)
    selected = lax.optimization_barrier(jnp.sum(chosen.astype(jnp.float32), axis=1))
    combine = jax.nn.softmax(logits, axis=-1) * selected

    def expert_step(total, member):
        single_up, single_down, column = member
        hidden = low_back(matmul(normed, single_up))
        active = low(jax.nn.gelu(hidden, approximate=False))
        result = low(low_back(matmul(active, single_down)))
        weight = lax.optimization_barrier(jnp.sum(combine * column[None, :], axis=1))
        return (total + weight[:, None] * result, None)
    total, _ = lax.scan(expert_step, jnp.zeros_like(residual), (up_weight, down_weight, jnp.eye(EXPERTS, dtype=jnp.float32)))
    return low_back(low(residual + total))

def block(params, residual, task_rows, route_rows, keep_rows):
    residual = attention(residual, *params[0:5])
    residual = feed_forward(residual, *params[5:11])
    residual = attention(residual, *params[11:16])
    return mixture(residual, task_rows, route_rows, keep_rows, *params[16:21])

def reference(patches_in, cotangent, task_ids, routes, keep_mask, first_gain, first_shift, first_proj, first_out, first_bias, dense_gain, dense_shift, dense_up, hidden_bias, dense_down, dense_bias, second_gain, second_shift, second_proj, second_out, second_bias, mixture_gain, mixture_shift, router, expert_up, expert_down):
    params = tuple((member.astype(jnp.float32) for member in (first_gain, first_shift, first_proj, first_out, first_bias, dense_gain, dense_shift, dense_up, hidden_bias, dense_down, dense_bias, second_gain, second_shift, second_proj, second_out, second_bias, mixture_gain, mixture_shift, router, expert_up, expert_down)))
    blocks = MICRO * (IMAGES // IMG_DEV)
    length = IMG_DEV * PATCHES
    inputs = patches_in.astype(jnp.float32).reshape(blocks, length, D)
    task_rows = jnp.repeat(task_ids.reshape(blocks, IMG_DEV), PATCHES, axis=1)
    route_rows = routes.reshape(blocks, length, TOPK)
    keep_rows = keep_mask.reshape(blocks, length, TOPK)
    checked = jax.checkpoint(block)

    def forward(weights_now, inputs_now):

        def block_step(carried, member):
            residual, tasks_here, routes_here, keep_here = member
            return (carried, checked(weights_now, residual, tasks_here, routes_here, keep_here))
        _, outputs = lax.scan(block_step, jnp.zeros((), jnp.float32), (inputs_now, task_rows, route_rows, keep_rows))
        return outputs
    outputs, pullback = jax.vjp(forward, params, inputs)
    weight_grads, input_grads = pullback(cotangent.astype(jnp.float32).reshape(blocks, length, D))
    block_output = outputs.reshape(MICRO, ROWS, D).astype(jnp.bfloat16)
    input_grad = input_grads.reshape(MICRO, ROWS, D).astype(jnp.bfloat16)
    return (block_output, input_grad, weight_grads[0], weight_grads[1], weight_grads[2], weight_grads[3], weight_grads[4], weight_grads[5], weight_grads[6], weight_grads[7], weight_grads[8], weight_grads[9], weight_grads[10], weight_grads[11], weight_grads[12], weight_grads[13], weight_grads[14], weight_grads[15], weight_grads[16], weight_grads[17], weight_grads[18], weight_grads[19], weight_grads[20])
```

```python
import functools

import jax
import jax.numpy as jnp
from jax import lax
from jax.experimental import pallas as pl
from jax.experimental.pallas import tpu as pltpu
from jax.sharding import PartitionSpec as P

HEADS = 6
HEAD_DIM = 64
PATCHES = 196
EXPERTS = 4
TASKS = 2
CAPACITY = 488
EPSILON = 1e-06
MESH = pl.DeviceIdType.MESH
bf16 = jnp.bfloat16
f32 = jnp.float32

RP = 208
SL = 496
VROWS = 32
NSEM = 120


def dot(left, right):
    return jnp.dot(left, right, preferred_element_type=f32)


def nt(left, right):
    return lax.dot_general(left, right, (((1,), (1,)), ((), ())), preferred_element_type=f32)


def tn(left, right):
    return lax.dot_general(left, right, (((0,), (0,)), ((), ())), preferred_element_type=f32)


def iota(shape, dim):
    return lax.broadcasted_iota(jnp.int32, shape, dim)


def onehot(cond):
    return jnp.where(cond, 1.0, 0.0).astype(bf16)


def normed(x):
    centered = x - jnp.mean(x, axis=-1, keepdims=True)
    scale = lax.rsqrt(jnp.mean(centered * centered, axis=-1, keepdims=True) + EPSILON)
    return centered * scale, scale


def norm_back(grad, xhat, scale, gain):
    inner = grad * gain
    mean_inner = jnp.mean(inner, axis=-1, keepdims=True)
    mean_cross = jnp.mean(inner * xhat, axis=-1, keepdims=True)
    return scale * (inner - mean_inner - xhat * mean_cross)


def gelu_both(u):
    cdf = 0.5 * (1.0 + lax.erf(u * 0.7071067811865476))
    return u * cdf, cdf + u * (jnp.exp(u * u * -0.5) * 0.3989422804014327)


def column_sum(v):
    return jnp.sum(v, axis=0, keepdims=True)


V_A1, V_D, V_HB, V_A2, V_M, V_R = 0, 3, 6, 10, 13, 16


class Links:
    def __init__(self, send_sems, recv_sems):
        self.send_sems, self.recv_sems, self.used, self.sent = send_sems, recv_sems, 0, []

    def take(self, count=1):
        first = self.used
        self.used += count
        return first

    def copy(self, number, src, dst, device):
        return pltpu.make_async_remote_copy(
            src_ref=src,
            dst_ref=dst,
            send_sem=self.send_sems.at[number],
            recv_sem=self.recv_sems.at[number],
            device_id=device,
            device_id_type=MESH,
        )

    def start(self, number, src, dst, device):
        made = self.copy(number, src, dst, device)
        made.start()
        self.sent.append(made)
        return made

    def forget(self, made):
        self.sent = [other for other in self.sent if other is not made]


def block_kernel(bits, refs):
    r = refs
    R, D = r.patches.shape[1:]
    FF = r.up.shape[1]
    xraw = r.h3.at[pl.ds(0, R)]
    IMG = R // PATCHES
    RT = IMG * RP
    FC = D
    NF = FF // FC
    sec = lax.axis_index("section")
    wide = lax.axis_index("wide")
    core = lax.rem(wide, 2)
    chip = wide // 2
    NS = 4
    links = Links(r.send, r.recv)

    def section_peer(j):
        hi, lo = sec // 2, lax.rem(sec, 2)
        jh, jl = j // 2, j % 2 if isinstance(j, int) else lax.rem(j, 2)
        return (hi + jh - 2 * hi * jh) * 2 + (lo + jl - 2 * lo * jl)

    def at_section(j):
        return (section_peer(j), wide)

    mate = (sec, wide + 1 - 2 * core)

    def bit_of(b):
        return lax.rem(chip // (1 << b), 2)

    def at_chip(b):
        return (sec, wide + (1 - 2 * bit_of(b)) * (2 << b))

    local = []

    def fetch(src, dst):
        c = pltpu.make_async_copy(src, dst, r.local.at[len(local)])
        c.start()
        local.append(c)
        return c

    fetch_x = fetch(r.patches.at[sec], xraw)
    fetch_c = [fetch(r.cotangent.at[m], r.pool.at[pl.ds(m * R, R)]) for m in range(NS)]
    shards = [
        (r.s_p1, r.w_p1),
        (r.s_o1, r.w_o1),
        (r.s_up, r.w_up),
        (r.s_dn, r.w_dn),
        (r.s_p2, r.w_p2),
        (r.s_o2, r.w_o2),
        (r.s_rt, r.w_rt),
    ]
    fetch_w = []
    for shard, whole in shards:
        n = shard.shape[0]
        fetch_w.append(fetch(shard, whole.at[pl.ds(pl.multiple_of(sec * n, n), n)]))
    fetch_up = fetch(r.expert_up.at[0], r.up)
    fetch_dn = fetch(r.expert_down.at[0], r.down)

    barrier = pltpu.get_barrier_semaphore()
    partners = [at_section(j) for j in range(1, NS)] + [mate] + [at_chip(b) for b in range(bits)]
    for device in partners:
        pl.semaphore_signal(barrier, inc=1, device_id=device, device_id_type=MESH)
    pl.semaphore_wait(barrier, len(partners))

    direct, passed = [], []
    for shard, whole in shards:
        n = shard.shape[0]
        h = n // 2
        numbers = []
        for j in range(1, NS):
            number = links.take()
            links.start(
                number,
                shard.at[pl.ds(pl.multiple_of(core * h, h), h)],
                whole.at[pl.ds(pl.multiple_of(sec * n + core * h, h), h)],
                at_section(j),
            )
            numbers.append(number)
        direct.append(numbers)
        passed.append([links.take() for _ in range(1, NS)])

    def pass_on(group):
        for t in group:
            shard, whole = shards[t]
            n = shard.shape[0]
            h = n // 2
            for j in range(1, NS):
                here = whole.at[pl.ds(pl.multiple_of(section_peer(j) * n + core * h, h), h)]
                links.copy(direct[t][j - 1], here, here, at_section(j)).wait_recv()
                links.start(passed[t][j - 1], here, here, mate)

    def landed(group):
        for t in group:
            shard, whole = shards[t]
            n = shard.shape[0]
            h = n // 2
            fetch_w[t].wait()
            for j in range(1, NS):
                there = whole.at[pl.ds(pl.multiple_of(section_peer(j) * n + (1 - core) * h, h), h)]
                links.copy(passed[t][j - 1], there, there, mate).wait_recv()

    expert_rows = []
    for j in range(NS):
        other = section_peer(j)
        r0 = jnp.zeros((1, R), jnp.int32)
        r1, k0, k1 = r0, r0, r0
        for m in range(NS):
            mine = jnp.where(sec == m, 1, 0)
            r0 = r0 + mine * r.routes[m, 0:1, :]
            r1 = r1 + mine * r.routes[m, 1:2, :]
            k0 = k0 + mine * r.keep[m, 0:1, :]
            k1 = k1 + mine * r.keep[m, 1:2, :]
        expert_rows.append(((r0 == other) & (k0 == 1)) | ((r1 == other) & (k1 == 1)))
    for j in range(NS):
        other = section_peer(j)
        r0 = jnp.zeros((1, R), jnp.int32)
        r1, k0, k1 = r0, r0, r0
        for m in range(NS):
            mine = jnp.where(other == m, 1, 0)
            r0 = r0 + mine * r.routes[m, 0:1, :]
            r1 = r1 + mine * r.routes[m, 1:2, :]
            k0 = k0 + mine * r.keep[m, 0:1, :]
            k1 = k1 + mine * r.keep[m, 1:2, :]
        expert_rows.append(((r0 == sec) & (k0 == 1)) | ((r1 == sec) & (k1 == 1)))
    for k in range(16):
        if k < 8:
            r.chosen[k : k + 1, :] = jnp.where(expert_rows[k], 1.0, 0.0)
        else:
            r.chosen[k : k + 1, :] = jnp.zeros((1, R), f32)

    def slots_of(limit, valid):
        chosen = r.chosen[...].astype(bf16)
        column = iota((limit.shape[0], R), 1)
        before = nt(onehot(column < limit), chosen)
        upto = nt(onehot((column <= limit) & valid), chosen)
        return jnp.where(upto > before, before, -1.0)

    def slots_padded(i, carry):
        off = iota((RP, 1), 0)
        r.pos_pad[pl.ds(pl.multiple_of(i * RP, RP), RP), :] = slots_of(i * PATCHES + off, off < PATCHES)
        return carry

    lax.fori_loop(0, IMG, slots_padded, 0)
    RC = R // 7

    def slots_raw(i, carry):
        off = iota((RC, 1), 0)
        r.pos_raw[pl.ds(pl.multiple_of(i * RC, RC), RC), :] = slots_of(i * RC + off, off >= 0)
        return carry

    lax.fori_loop(0, 7, slots_raw, 0)

    fetch_x.wait()
    for c in fetch_c:
        c.wait()
    for i in range(IMG):
        start = (PATCHES * i) // 16 * 16
        gap = PATCHES * i - start
        a, b = iota((RP, RP), 0), iota((RP, RP), 1)
        shift = onehot((b == a + gap) & (a < PATCHES))
        r.h0[i * RP : (i + 1) * RP, :] = dot(shift, xraw[start : start + RP, :]).astype(bf16)
        first = pl.multiple_of(sec * R + start, 16)
        r.g3[i * RP : (i + 1) * RP, :] = dot(shift, r.pool[pl.ds(first, RP), :]).astype(bf16)

    slot_lane = iota((1, SL), 1).astype(f32)
    for j in range(NS):
        m = section_peer(j)
        pick = onehot(r.pos_raw[:, 4 + j : 5 + j] == slot_lane)
        first = pl.multiple_of(m * R, 16)
        r.gslot[j] = tn(pick, r.pool[pl.ds(first, R), :]).astype(bf16)
        row = iota((R, 128), 0)
        task = jnp.zeros((R, 128), jnp.int32)
        for i in range(IMG):
            task = jnp.where((row >= i * PATCHES) & (row < (i + 1) * PATCHES), r.task[m, i], task)
        r.tslot[j] = tn(pick, task.astype(f32).astype(bf16)).astype(bf16)

    low_half = iota((1, 128), 1) < 64
    half_masks = [onehot(low_half), onehot(jnp.logical_not(low_half))]
    low_half_rows = iota((RP, 128), 1) < 64
    key_ok = iota((RP, RP), 0) < PATCHES

    def attend(h_in, h_out, vecs, w_p, w_o, qkv_s, p_s, ctx_s):
        gain, shift, bias = vecs

        def image(i, carry):
            rows = pl.ds(pl.multiple_of(i * RP, RP), RP)
            x = h_in[rows, :].astype(f32)
            a = (normed(x)[0] * gain[...] + shift[...]).astype(bf16)
            qkv = dot(a, w_p[...]).astype(bf16)
            qkv_s[rows, :] = qkv
            parts = []
            for pair in range(HEADS // 2):
                at = 128 * pair
                q2 = qkv[:, at : at + 128]
                k2 = qkv[:, D + at : D + at + 128]
                v2 = qkv[:, 2 * D + at : 2 * D + at + 128]
                outs = []
                for half in range(2):
                    scores = nt(k2 * half_masks[half], q2)
                    scores = jnp.where(key_ok, scores, -1e30)
                    top = jnp.max(scores, axis=0, keepdims=True)
                    e = jnp.exp((scores - top) * HEAD_DIM**-0.5)
                    p = (e * (1.0 / jnp.sum(e, axis=0, keepdims=True))).astype(bf16)
                    p_s[i * HEADS + 2 * pair + half] = p
                    outs.append(tn(p, v2))
                parts.append(jnp.where(low_half_rows, outs[0], outs[1]).astype(bf16))
            ctx = jnp.concatenate(parts, axis=1)
            ctx_s[rows, :] = ctx
            h_out[rows, :] = (x + dot(ctx, w_o[...]) + bias[...]).astype(bf16)
            return carry

        lax.fori_loop(0, IMG, image, 0)

    def attend_back(h_in, g_in, g_out, vecs, w_p, w_o, qkv_s, p_s, ctx_s, vrow):
        gain, shift, _ = vecs

        def image(i, carry):
            rows = pl.ds(pl.multiple_of(i * RP, RP), RP)
            g = g_in[rows, :]
            gf = g.astype(f32)
            xhat, scale = normed(h_in[rows, :].astype(f32))
            r.a_s[rows, :] = (xhat * gain[...] + shift[...]).astype(bf16)
            gc = nt(g, w_o[...]).astype(bf16)
            qkv = qkv_s[rows, :]
            gq, gk, gv = [], [], []
            for pair in range(HEADS // 2):
                at = 128 * pair
                q2 = qkv[:, at : at + 128]
                k2 = qkv[:, D + at : D + at + 128]
                v2 = qkv[:, 2 * D + at : 2 * D + at + 128]
                gc2 = gc[:, at : at + 128]
                two = []
                for half in range(2):
                    p = p_s[i * HEADS + 2 * pair + half]
                    pf = p.astype(f32)
                    gp = nt(v2 * half_masks[half], gc2)
                    t = pf * gp
                    gs = (t - pf * jnp.sum(t, axis=0, keepdims=True)).astype(bf16)
                    two.append((tn(gs, k2), dot(gs, q2), dot(p, gc2)))
                gq.append((jnp.where(low_half_rows, two[0][0], two[1][0]) * HEAD_DIM**-0.5).astype(bf16))
                gk.append((jnp.where(low_half_rows, two[0][1], two[1][1]) * HEAD_DIM**-0.5).astype(bf16))
                gv.append(jnp.where(low_half_rows, two[0][2], two[1][2]).astype(bf16))
            gqkv = jnp.concatenate(gq + gk + gv, axis=1)
            qkv_s[rows, :] = gqkv
            ga = nt(gqkv, w_p[...])
            r.vec[vrow : vrow + 1, :] += column_sum(ga * xhat)
            r.vec[vrow + 1 : vrow + 2, :] += column_sum(ga)
            r.vec[vrow + 2 : vrow + 3, :] += column_sum(gf)
            g_out[rows, :] = (gf + norm_back(ga, xhat, scale, gain[...])).astype(bf16)
            return carry

        lax.fori_loop(0, IMG, image, 0)

    r.vec[...] = jnp.zeros(r.vec.shape, f32)
    att1 = (r.first_gain, r.first_shift, r.first_bias)
    att2 = (r.second_gain, r.second_shift, r.second_bias)

    pass_on((0, 1))
    landed((0, 1))
    attend(r.h0, r.h1, att1, r.w_p1, r.w_o1, r.qkv1, r.p1, r.ctx1)

    pass_on((2, 3))
    landed((2, 3))
    HR = RT // 2

    def dense_step(i, carry):
        rows = pl.ds(pl.multiple_of(i * HR, HR), HR)
        x = r.h1[rows, :].astype(f32)
        a = (normed(x)[0] * r.dense_gain[...] + r.dense_shift[...]).astype(bf16)
        total = x + r.dense_bias[...]
        for f in range(NF):
            cols = slice(f * FC, (f + 1) * FC)
            u = dot(a, r.w_up[:, cols]) + r.hidden_bias[:, cols]
            z, slope = gelu_both(u)
            z = z.astype(bf16)
            r.z[rows, cols] = z
            r.slope[rows, cols] = slope.astype(bf16)
            total = total + dot(z, r.w_dn[cols, :])
        r.h2[rows, :] = total.astype(bf16)
        return carry

    lax.fori_loop(0, 2, dense_step, 0)

    pass_on((4, 5, 6))
    landed((4, 5, 6))
    attend(r.h2, r.h3, att2, r.w_p2, r.w_o2, r.qkv2, r.p2, r.ctx2)

    lane = iota((1, 128), 1)

    def gates_of(a, task):
        logits = dot(a, r.w_rt[...])
        active = (lane < TASKS * EXPERTS) & (lane // EXPERTS == task)
        top = jnp.max(jnp.where(active, logits, -1e30), axis=-1, keepdims=True)
        e = jnp.where(active, jnp.exp(jnp.minimum(logits - top, 0.0)), 0.0)
        return e / jnp.sum(e, axis=-1, keepdims=True), active

    def mix_rows(i, carry):
        rows = pl.ds(pl.multiple_of(i * RP, RP), RP)
        a = (normed(r.h3[rows, :].astype(f32))[0] * r.mixture_gain[...] + r.mixture_shift[...]).astype(bf16)
        r.a4[rows, :] = a
        task = jnp.zeros((RP, 1), jnp.int32) + r.task[sec, i]
        r.gates[rows, :] = gates_of(a, task)[0]
        return carry

    lax.fori_loop(0, IMG, mix_rows, 0)

    slots_first = links.take(NS)
    for j in (3, 1, 2, 0):
        pick = onehot(r.pos_pad[:, j : j + 1] == slot_lane)
        r.slot_out[j] = tn(pick, r.a4[...]).astype(bf16)
        if j > 0:
            links.start(slots_first + j, r.slot_out.at[j], r.slot_in.at[j], at_section(j))
        else:
            r.slot_in[0] = r.slot_out[0]

    fetch_up.wait()
    fetch_dn.wait()
    r.eg[...] = jnp.zeros(r.eg.shape, f32)
    ga_first, q_first, w_first = links.take(NS), links.take(NS), links.take(NS)

    def ga_in(j):
        return r.pool.at[pl.ds((j - 1) * SL, SL)]

    def w_in(j):
        return r.pool.at[pl.ds((j + 2) * SL, SL)]

    def expert_step(j, carry):
        there = at_section(j)

        @pl.when(j > 0)
        def _():
            links.copy(slots_first + j, r.slot_out.at[j], r.slot_in.at[j], there).wait()

        a = r.slot_in[j]
        gs = r.gslot[j]
        gates, active = gates_of(a, r.tslot[j][:, 0:1].astype(jnp.int32))
        combine = jnp.sum(jnp.where(lax.rem(lane, EXPERTS) == sec, gates, 0.0), axis=-1, keepdims=True)
        gout = (combine * gs.astype(f32)).astype(bf16)
        for f in range(NF):
            cols = slice(f * FC, (f + 1) * FC)
            z, slope = gelu_both(dot(a, r.up[:, cols]))
            z = z.astype(bf16)
            part = dot(z, r.down[cols, :])
            gv = (nt(gout, r.down[cols, :]) * slope).astype(bf16)
            gpart = nt(gv, r.up[:, cols])
            if f == 0:
                r.out_acc[...] = part
                r.ga_acc[...] = gpart
            else:
                r.out_acc[...] += part
                r.ga_acc[...] += gpart
            r.eg[0, :, cols] += tn(a, gv)
            r.eg[1, :, cols] += tn(gout, z)
        r.slot_out[j] = r.ga_acc[...].astype(bf16)
        weighted = combine * r.out_acc[...].astype(bf16).astype(f32)
        q = jnp.sum(gs.astype(f32) * weighted, axis=-1, keepdims=True)
        q_hi = q.astype(bf16).astype(f32)
        lanes = iota((SL, 128), 1)
        q2 = jnp.where(lanes == 0, q_hi, jnp.where(lanes == 1, q - q_hi, 0.0))
        r.q_out[j] = q2.T[0:16, :].astype(bf16)
        r.gslot[j] = weighted.astype(bf16)

        @pl.when(j > 0)
        def _():
            links.copy(ga_first + j, r.slot_out.at[j], ga_in(j), there).start()
            links.copy(q_first + j, r.q_out.at[j], r.q_in.at[j], there).start()
            links.copy(w_first + j, r.gslot.at[j], w_in(j), there).start()

        return carry

    lax.fori_loop(0, NS, expert_step, 0)

    def expert_copies(j):
        there = at_section(j)
        return (
            lambda: links.copy(ga_first + j, r.slot_out.at[j], ga_in(j), there),
            lambda: links.copy(q_first + j, r.q_out.at[j], r.q_in.at[j], there),
            lambda: links.copy(w_first + j, r.gslot.at[j], w_in(j), there),
        )

    links.sent = links.sent[:-3]

    e_core = links.take(NF)
    for b in range(NF):
        cols = slice(b * FC, (b + 1) * FC)
        r.up[:, cols] = r.eg[1 - core, :, cols].astype(bf16)
        links.start(e_core + b, r.up.at[:, cols], r.e_sum.at[b], mate)

    for j in range(1, NS):
        ga, q, _ = expert_copies(j)
        ga().wait()
        q().wait()

    def mix_back(i, carry):
        rows = pl.ds(pl.multiple_of(i * RP, RP), RP)
        task = jnp.zeros((RP, 1), jnp.int32) + r.task[sec, i]
        active = (lane < TASKS * EXPERTS) & (lane // EXPERTS == task)
        ga = jnp.zeros((RP, D), f32)
        q8 = jnp.zeros((RP, 128), f32)
        for j in range(NS):
            pick = onehot(r.pos_pad[rows, j : j + 1] == slot_lane)
            ga = ga + dot(pick, r.slot_out[0] if j == 0 else ga_in(j)[...])
            q = jnp.sum(nt(pick, r.q_out[0] if j == 0 else r.q_in[j]), axis=-1, keepdims=True)
            q8 = q8 + jnp.where(active & (lax.rem(lane, EXPERTS) == section_peer(j)), q, 0.0)
        gl = (q8 - r.gates[rows, :] * jnp.sum(q8, axis=-1, keepdims=True)).astype(bf16)
        ga = ga + nt(gl, r.w_rt[...])
        r.vec[V_R : V_R + 8, :] += tn(gl, r.a4[rows, :])[0:8, :]
        xhat, scale = normed(r.h3[rows, :].astype(f32))
        r.vec[V_M : V_M + 1, :] += column_sum(ga * xhat)
        r.vec[V_M + 1 : V_M + 2, :] += column_sum(ga)
        g = r.g3[rows, :].astype(f32)
        r.g2[rows, :] = (g + norm_back(ga, xhat, scale, r.mixture_gain[...])).astype(bf16)
        return carry

    lax.fori_loop(0, IMG, mix_back, 0)

    for b in range(NF):
        cols = slice(b * FC, (b + 1) * FC)
        links.copy(e_core + b, r.up.at[:, cols], r.e_sum.at[b], mate).wait_recv()
        r.e_sum[b] = (r.eg[core, :, cols] + r.e_sum[b].astype(f32)).astype(bf16)

    half_rows = D // 2
    parts = []
    for k in range(2):
        order = list(range(bits)) if k == 0 else list(range(bits))[::-1]
        parts.append(dict(rows=pl.ds(k * half_rows, half_rows), k=k, order=order, lo=0, n=NF, kept=[]))

    def chips_start(step):
        for part in parts:
            b = part["order"][step]
            v = bit_of(b)
            number = links.take()
            if part["n"] > 1:
                half = part["n"] // 2
                keep = part["lo"] + v * half
                send = part["lo"] + (1 - v) * half
            else:
                half = 1
                keep = send = part["lo"]
            land = (r.e_land, r.e_land2)[part["k"]].at[pl.ds(step + (step > 0), half)]
            made = links.start(number, r.e_sum.at[pl.ds(send, half), part["rows"]], land, at_chip(b))
            part["now"] = (made, keep, half, part["n"] > 1)
            part["made"] = made

    def chips_end(step):
        for part in parts:
            made, keep, half, halved = part["now"]
            made.wait_recv()
            if not halved:
                made.wait_send()
                links.forget(made)
            for b in range(half):
                mine = r.e_sum[keep + b, part["rows"], :].astype(f32)
                other = (r.e_land, r.e_land2)[part["k"]][step + (step > 0) + b].astype(f32)
                r.e_sum[keep + b, part["rows"], :] = (mine + other).astype(bf16)
            part["lo"], part["n"] = keep, half
            if halved:
                part["kept"].append((part["order"][step], half))

    def gather_first():
        for part in parts:
            part["at"] = part["lo"]
            for b in range(part["n"]):
                r.e_all[core, part["lo"] + b, part["rows"], :] = r.e_sum[part["lo"] + b, part["rows"], :]

    def gather_start():
        for part in parts:
            if not part["kept"]:
                part["now"] = None
                continue
            b, half = part["kept"].pop()
            number = links.take()
            here = r.e_all.at[core, pl.ds(part["at"], half), part["rows"]]
            made = links.start(number, here, here, at_chip(b))
            v = bit_of(b)
            part["now"] = (number, b, part["at"] + (1 - 2 * v) * half, half)
            part["at"] = part["at"] - v * half

    def gather_end():
        for part in parts:
            if part["now"] is None:
                continue
            number, b, first, half = part["now"]
            there = r.e_all.at[core, pl.ds(first, half), part["rows"]]
            links.copy(number, there, there, at_chip(b)).wait_recv()

    class Summed:
        def __init__(self, buffers):
            self.b = buffers

        def send_core(self):
            self.core_number = links.take()
            self.made = links.start(self.core_number, self.b.full.at[:, 1 - core], self.b.pair, mate)

        def send_section(self):
            b = self.b
            self.made.wait()
            links.forget(self.made)
            for p in range(NS):
                b.pair[p] = (b.full[p, core].astype(f32) + b.pair[p].astype(f32)).astype(bf16)
            self.numbers = [links.take() for _ in range(1, NS)]
            for j in range(1, NS):
                links.start(self.numbers[j - 1], b.pair.at[section_peer(j)], b.sec.at[j - 1], at_section(j))

        def section_sum(self):
            b = self.b
            for j in range(1, NS):
                links.copy(self.numbers[j - 1], b.sec.at[j - 1], b.sec.at[j - 1], at_section(j)).wait_recv()
            total = b.pair[sec].astype(f32)
            for j in range(1, NS):
                total = total + b.sec[j - 1].astype(f32)
            for k in range(2):
                b.fin[core, k] = self.half(total, k).astype(bf16)

        def half(self, v, k):
            if self.b.by_rows:
                h = v.shape[0] // 2
                return v[k * h : (k + 1) * h, :]
            h = v.shape[1] // 2
            return v[:, k * h : (k + 1) * h]

        def chip_start(self, step):
            self.now = []
            for k in range(2):
                bit = step if k == 0 else bits - 1 - step
                self.now.append(links.start(links.take(), self.b.fin.at[core, k], self.b.land.at[step, k], at_chip(bit)))

        def chip_end(self, step):
            for k in range(2):
                self.now[k].wait()
                links.forget(self.now[k])
                mine = self.b.fin[core, k].astype(f32)
                self.b.fin[core, k] = (mine + self.b.land[step, k].astype(f32)).astype(bf16)

        def pair_start(self):
            self.last = links.take()
            here = self.b.fin.at[core]
            links.start(self.last, here, here, mate)

        def pair_end(self):
            there = self.b.fin.at[1 - core]
            links.copy(self.last, there, there, mate).wait_recv()

    def by_section_rows(full, cols, value):
        n = D // NS // 2
        for p in range(NS):
            for c in range(2):
                full[p, c, :, cols] = value[(2 * p + c) * n : (2 * p + c + 1) * n, :].astype(bf16)

    def attention_grads(full, g_in, qkv_s, ctx_s):
        for f in range(3):
            cols = slice(f * D, (f + 1) * D)
            by_section_rows(full, cols, tn(r.a_s[...], qkv_s[:, cols]))
        by_section_rows(full, slice(3 * D, 4 * D), tn(ctx_s[...], g_in[...]))

    sum_a2, sum_du, sum_dd, sum_a1 = (Summed(b) for b in (r.t_a2, r.t_du, r.t_dd, r.t_a1))
    out_copies = []

    def send_out(src, dst):
        c = pltpu.make_async_copy(src, dst, r.out_sems.at[len(out_copies)])
        c.start()
        out_copies.append(c)

    if bits > 0:
        chips_start(0)
    attend_back(r.h2, r.g2, r.g1, att2, r.w_p2, r.w_o2, r.qkv2, r.p2, r.ctx2, V_A2)
    if bits > 0:
        chips_end(0)
    if bits > 1:
        chips_start(1)
    attention_grads(r.t_a2.full, r.g2, r.qkv2, r.ctx2)
    sum_a2.send_core()

    def dense_back(i, carry):
        rows = pl.ds(pl.multiple_of(i * HR, HR), HR)
        g = r.g1[rows, :]
        gf = g.astype(f32)
        xhat, scale = normed(r.h1[rows, :].astype(f32))
        r.a_s[rows, :] = (xhat * r.dense_gain[...] + r.dense_shift[...]).astype(bf16)
        ga = jnp.zeros((HR, D), f32)
        for f in range(NF):
            cols = slice(f * FC, (f + 1) * FC)
            gu = (nt(g, r.w_dn[cols, :]) * r.slope[rows, cols].astype(f32)).astype(bf16)
            r.slope[rows, cols] = gu
            r.vec[V_HB + f : V_HB + f + 1, :] += column_sum(gu.astype(f32))
            ga = ga + nt(gu, r.w_up[:, cols])
        r.vec[V_D : V_D + 1, :] += column_sum(ga * xhat)
        r.vec[V_D + 1 : V_D + 2, :] += column_sum(ga)
        r.vec[V_D + 2 : V_D + 3, :] += column_sum(gf)
        r.g0[rows, :] = (gf + norm_back(ga, xhat, scale, r.dense_gain[...])).astype(bf16)
        return carry

    lax.fori_loop(0, 2, dense_back, 0)
    sum_a2.send_section()
    for step in range(1, bits):
        if step > 1:
            chips_start(step)
        chips_end(step)
    gather_first()
    gather_start()

    for f in range(NF):
        cols = slice(f * FC, (f + 1) * FC)
        by_section_rows(r.t_du.full, cols, tn(r.a_s[...], r.slope[:, cols]))
    sum_du.send_core()
    for f in range(NF):
        cols = slice(f * FC, (f + 1) * FC)
        value = tn(r.g1[...], r.z[:, cols])
        n = D // 2
        for c in range(2):
            r.t_dd.full[f, c] = value[c * n : (c + 1) * n, :].astype(bf16)
    sum_dd.send_core()
    sum_a2.section_sum()
    sum_du.send_section()
    gather_end()
    gather_start()

    for j in range(1, NS):
        expert_copies(j)[2]().wait()

    def block_out(i, carry):
        rows = pl.ds(pl.multiple_of(i * RP, RP), RP)
        total = r.h3[rows, :].astype(f32)
        for j in range(NS):
            pick = onehot(r.pos_pad[rows, j : j + 1] == slot_lane)
            total = total + dot(pick, r.gslot[0] if j == 0 else w_in(j)[...])
        r.a4[rows, :] = total.astype(bf16)
        return carry

    lax.fori_loop(0, IMG, block_out, 0)
    send_out(r.a4, r.o_block)
    sum_dd.send_section()
    sum_du.section_sum()

    attend_back(r.h0, r.g0, r.g3, att1, r.w_p1, r.w_o1, r.qkv1, r.p1, r.ctx1, V_A1)
    send_out(r.g3, r.o_grad)
    sum_dd.section_sum()
    attention_grads(r.t_a1.full, r.g0, r.qkv1, r.ctx1)
    sum_a1.send_core()

    vec_core = links.take()
    made = links.start(vec_core, r.vec, r.vec_land.at[0], mate)
    gather_end()
    while any(part["kept"] for part in parts):
        gather_start()
        gather_end()
    e_last = links.take()
    here = r.e_all.at[core]
    links.start(e_last, here, here, mate)
    sum_a1.send_section()
    made.wait()
    links.forget(made)
    r.vec[...] += r.vec_land[0]
    vec_numbers = [links.take() for _ in range(1, NS)]
    vec_made = [links.start(vec_numbers[j - 1], r.vec, r.vec_land.at[j], at_section(j)) for j in range(1, NS)]
    early = (sum_a2, sum_du, sum_dd)
    for step in range(bits):
        for s in early:
            s.chip_start(step)
        for s in early:
            s.chip_end(step)
    for s in early:
        s.pair_start()
    for made in vec_made:
        made.wait()
        links.forget(made)
    r.vec[...] += r.vec_land[1] + r.vec_land[2] + r.vec_land[3]
    sum_a1.section_sum()
    for step in range(bits):
        sum_a1.chip_start(step)
        made = links.start(links.take(), r.vec, r.vec_land.at[NS + step], at_chip(step))
        sum_a1.chip_end(step)
        made.wait()
        links.forget(made)
        r.vec[...] += r.vec_land[NS + step]
    sum_a1.pair_start()
    send_out(r.vec, r.o_vec)
    there = r.e_all.at[1 - core]
    links.copy(e_last, there, there, mate).wait_recv()
    send_out(r.e_all, r.o_expert)
    for s, dst in ((sum_a2, r.o_a2), (sum_du, r.o_du), (sum_dd, r.o_dd), (sum_a1, r.o_a1)):
        s.pair_end()
        send_out(s.b.fin, dst)
    for made in links.sent:
        made.wait_send()
    for c in out_copies:
        c.wait()


class Bag:
    def __init__(self, **members):
        self.__dict__.update(members)


VECTORS = (
    "first_gain",
    "first_shift",
    "first_bias",
    "dense_gain",
    "dense_shift",
    "hidden_bias",
    "dense_bias",
    "second_gain",
    "second_shift",
    "second_bias",
    "mixture_gain",
    "mixture_shift",
)
HBM_IN = ("patches", "cotangent", "s_p1", "s_o1", "s_up", "s_dn", "s_p2", "s_o2", "s_rt", "expert_up", "expert_down")


def run_blocks(bits, arrays):
    R, D = arrays["patches"].shape[1:]
    FF = arrays["expert_up"].shape[2]
    IMG = R // PATCHES
    RT = IMG * RP
    n = D // 8
    vm = pltpu.VMEM
    scratch = dict(
        pool=vm((max(4 * R, 6 * SL), D), bf16),
        chosen=vm((16, R), f32),
        pos_pad=vm((RT, 16), f32),
        pos_raw=vm((R, 16), f32),
        w_p1=vm((D, 3 * D), bf16),
        w_o1=vm((D, D), bf16),
        w_up=vm((D, FF), bf16),
        w_dn=vm((FF, D), bf16),
        w_p2=vm((D, 3 * D), bf16),
        w_o2=vm((D, D), bf16),
        w_rt=vm((D, 128), bf16),
        up=vm((D, FF), bf16),
        down=vm((FF, D), bf16),
        h0=vm((RT, D), bf16),
        h1=vm((RT, D), bf16),
        h2=vm((RT, D), bf16),
        h3=vm((RT, D), bf16),
        g0=vm((RT, D), bf16),
        g1=vm((RT, D), bf16),
        g2=vm((RT, D), bf16),
        g3=vm((RT, D), bf16),
        a_s=vm((RT, D), bf16),
        a4=vm((RT, D), bf16),
        qkv1=vm((RT, 3 * D), bf16),
        qkv2=vm((RT, 3 * D), bf16),
        p1=vm((IMG * HEADS, RP, RP), bf16),
        p2=vm((IMG * HEADS, RP, RP), bf16),
        ctx1=vm((RT, D), bf16),
        ctx2=vm((RT, D), bf16),
        z=vm((RT, FF), bf16),
        slope=vm((RT, FF), bf16),
        gates=vm((RT, 128), f32),
        slot_out=vm((4, SL, D), bf16),
        slot_in=vm((4, SL, D), bf16),
        gslot=vm((4, SL, D), bf16),
        tslot=vm((4, SL, 128), bf16),
        q_out=vm((4, 16, SL), bf16),
        q_in=vm((4, 16, SL), bf16),
        out_acc=vm((SL, D), f32),
        ga_acc=vm((SL, D), f32),
        eg=vm((2, D, FF), f32),
        e_sum=vm((4, D, D), bf16),
        e_land=vm((bits + 1, D // 2, D), bf16),
        e_land2=vm((bits + 1, D // 2, D), bf16),
        e_all=vm((2, 4, D, D), bf16),
        vec=vm((VROWS, D), f32),
        vec_land=vm((4 + max(bits, 1), VROWS, D), f32),
        send=pltpu.SemaphoreType.DMA((NSEM,)),
        recv=pltpu.SemaphoreType.DMA((NSEM,)),
        local=pltpu.SemaphoreType.DMA((16,)),
        out_sems=pltpu.SemaphoreType.DMA((8,)),
    )
    sums = dict(t_a2=False, t_du=False, t_dd=True, t_a1=False)
    fin = {}
    for name, by_rows in sums.items():
        rows, cols = (D // 2, D) if by_rows else (n, FF)
        halved = (rows // 2, cols) if by_rows else (rows, cols // 2)
        if name in ("t_a2", "t_dd"):
            scratch[name + ".full"] = vm((4, 2, rows, cols), bf16)
        scratch[name + ".pair"] = vm((4, rows, cols), bf16)
        scratch[name + ".sec"] = vm((3, rows, cols), bf16)
        scratch[name + ".fin"] = vm((2, 2) + halved, bf16)
        scratch[name + ".land"] = vm((max(bits, 1), 2) + halved, bf16)
        fin[name] = jax.ShapeDtypeStruct((2, 2) + halved, bf16)
    outs = dict(
        o_block=jax.ShapeDtypeStruct((RT, D), bf16),
        o_grad=jax.ShapeDtypeStruct((RT, D), bf16),
        o_expert=jax.ShapeDtypeStruct((2, 4, D, D), bf16),
        o_a2=fin["t_a2"],
        o_du=fin["t_du"],
        o_dd=fin["t_dd"],
        o_a1=fin["t_a1"],
        o_vec=jax.ShapeDtypeStruct((VROWS, D), f32),
    )
    ins = list(arrays)
    names = ins + list(outs) + list(scratch)
    spaces = {name: pl.BlockSpec(memory_space=pl.ANY) for name in HBM_IN}
    spaces["task"] = pl.BlockSpec(memory_space=pltpu.SMEM)

    def body(*refs):
        members = {}
        for name, ref in zip(names, refs, strict=True):
            if "." in name:
                outer, inner = name.split(".")
                members.setdefault(outer, Bag(by_rows=sums[outer])).__dict__[inner] = ref
            else:
                members[name] = ref
        for name in ("t_du", "t_a1"):
            members[name].full = members["t_a2"].full
        block_kernel(bits, Bag(**members))

    return pl.pallas_call(
        body,
        out_shape=list(outs.values()),
        in_specs=[spaces.get(name, pl.BlockSpec(memory_space=pltpu.VMEM)) for name in ins],
        out_specs=[pl.BlockSpec(memory_space=pl.ANY)] * len(outs),
        scratch_shapes=list(scratch.values()),
        compiler_params=pltpu.CompilerParams(
            collective_id=0, has_side_effects=True, vmem_limit_bytes=64 * 2**20 - 2**18
        ),
        name="blocks",
    )(*arrays.values())


def finish_kernel(block, grad, expert, a2, du, dd, a1, vec, *outs):
    (
        o_block, o_grad, g1, s1, p1, o1, b1, gd, sd, up, hb, dn, db, g2, s2, p2, o2, b2, gm, sm, rt, eup, edn,
    ) = outs
    D = block.shape[1]
    R = o_block.shape[1]
    sec = lax.axis_index("section")
    row, col = iota((R, RP), 0), iota((R, RP), 1)
    for src, dst in ((block, o_block), (grad, o_grad)):
        total = jnp.zeros((R, D), f32)
        for i in range(R // PATCHES):
            pick = onehot((row - i * PATCHES == col) & (col < PATCHES))
            total = total + dot(pick, src[i * RP : (i + 1) * RP, :])
        dst[0] = total.astype(bf16)
    n = D // 8
    for src, dst_p, dst_o in ((a1, p1, o1), (a2, p2, o2)):
        for c in range(2):
            rows = slice(c * n, (c + 1) * n)
            dst_p[rows, 0 : 2 * D] = src[c, 0].astype(f32)
            dst_p[rows, 2 * D : 3 * D] = src[c, 1, :, 0:D].astype(f32)
            dst_o[rows, :] = src[c, 1, :, D : 2 * D].astype(f32)
    for c in range(2):
        for k in range(2):
            up[c * n : (c + 1) * n, k * 2 * D : (k + 1) * 2 * D] = du[c, k].astype(f32)
    down_t = jnp.concatenate([dd[0, 0], dd[0, 1], dd[1, 0], dd[1, 1]], axis=0)
    dn[...] = down_t.astype(f32).T
    for b in range(4):
        eup[0, :, b * D : (b + 1) * D] = expert[0, b].astype(f32)
        edn[0, b * D : (b + 1) * D, :] = expert[1, b].astype(f32).T
    q = D // 4
    mine = jnp.where(iota((D, q), 0) == iota((D, q), 1) + sec * q, 1.0, 0.0)
    cut = jnp.dot(vec[...], mine, precision=lax.Precision.HIGHEST, preferred_element_type=f32)
    for dst, at in (
        (g1, V_A1), (s1, V_A1 + 1), (b1, V_A1 + 2), (gd, V_D), (sd, V_D + 1), (db, V_D + 2),
        (g2, V_A2), (s2, V_A2 + 1), (b2, V_A2 + 2), (gm, V_M), (sm, V_M + 1),
    ):
        dst[...] = cut[at : at + 1, :]
    rt[...] = cut[V_R : V_R + 8, :]
    hb[...] = vec[pl.ds(V_HB + sec, 1), :]


def finish(parts, shape):
    R, D, FF = shape
    q = D // 4
    s = lambda *dims: jax.ShapeDtypeStruct(dims, f32)
    outs = [
        jax.ShapeDtypeStruct((1, R, D), bf16), jax.ShapeDtypeStruct((1, R, D), bf16),
        s(1, q), s(1, q), s(q, 3 * D), s(q, D), s(1, q),
        s(1, q), s(1, q), s(q, FF), s(1, FF // 4), s(FF // 4, D), s(1, q),
        s(1, q), s(1, q), s(q, 3 * D), s(q, D), s(1, q),
        s(1, q), s(1, q), s(8, q), s(1, D, FF), s(1, FF, D),
    ]
    return pl.pallas_call(
        finish_kernel,
        out_shape=outs,
        in_specs=[pl.BlockSpec(memory_space=pltpu.VMEM)] * 8,
        out_specs=[pl.BlockSpec(memory_space=pltpu.VMEM)] * len(outs),
        compiler_params=pltpu.CompilerParams(vmem_limit_bytes=48 * 2**20),
        name="finish",
    )(*parts)


def local(
    patches_in, cotangent, task_ids, routes, keep_mask,
    first_gain, first_shift, first_proj, first_out, first_bias,
    dense_gain, dense_shift, dense_up, hidden_bias, dense_down, dense_bias,
    second_gain, second_shift, second_proj, second_out, second_bias,
    mixture_gain, mixture_shift, router, expert_up, expert_down,
):
    bits = (lax.axis_size("wide") // 2).bit_length() - 1
    line = lambda v: v.reshape(1, -1)
    arrays = dict(
        patches=patches_in,
        cotangent=cotangent,
        task=task_ids,
        routes=jnp.transpose(routes, (0, 2, 1)),
        keep=jnp.transpose(keep_mask, (0, 2, 1)),
        s_p1=first_proj,
        s_o1=first_out,
        s_up=dense_up,
        s_dn=dense_down,
        s_p2=second_proj,
        s_o2=second_out,
        s_rt=jnp.pad(router, ((0, 0), (0, 128 - router.shape[1]))),
        expert_up=expert_up,
        expert_down=expert_down,
        first_gain=line(first_gain),
        first_shift=line(first_shift),
        first_bias=line(first_bias),
        dense_gain=line(dense_gain),
        dense_shift=line(dense_shift),
        hidden_bias=line(hidden_bias),
        dense_bias=line(dense_bias),
        second_gain=line(second_gain),
        second_shift=line(second_shift),
        second_bias=line(second_bias),
        mixture_gain=line(mixture_gain),
        mixture_shift=line(mixture_shift),
    )
    parts = run_blocks(bits, arrays)
    R, D = patches_in.shape[1:]
    outs = list(finish(parts, (R, D, expert_up.shape[2])))
    for at in (2, 3, 6, 7, 8, 10, 12, 13, 14, 17, 18, 19):
        outs[at] = outs[at].reshape(-1)
    outs[20] = outs[20].T
    return tuple(outs)


def solution(mesh):
    rows, vec, mat = P(None, "wide", None), P(), P("section", None)
    cube = P("section", None, None)
    in_specs = (
        rows, rows, P(None, "wide"), rows, rows,
        vec, vec, mat, mat, vec,
        vec, vec, mat, vec, mat, vec,
        vec, vec, mat, mat, vec,
        vec, vec, mat, cube, cube,
    )
    cut, moved = P("section"), P("section", "wide", None)
    out_specs = (
        moved, moved,
        cut, cut, mat, mat, cut,
        cut, cut, mat, cut, mat, cut,
        cut, cut, mat, mat, cut,
        cut, cut, mat, cube, cube,
    )
    return jax.shard_map(local, mesh=mesh, in_specs=in_specs, out_specs=out_specs, check_vma=False)
```

```python
import functools

import jax
import jax.numpy as jnp
from jax import lax
from jax.experimental import pallas as pl
from jax.experimental.pallas import tpu as pltpu
from jax.sharding import PartitionSpec as P

HEADS = 6
HEAD_DIM = 64
PATCHES = 196
EXPERTS = 4
TASKS = 2
CAPACITY = 488
EPSILON = 1e-06
MESH = pl.DeviceIdType.MESH
bf16 = jnp.bfloat16
f32 = jnp.float32

RP = 208
SL = 496
VROWS = 32
NSEM = 200


def dot(left, right):
    return jnp.dot(left, right, preferred_element_type=f32)


def nt(left, right):
    return lax.dot_general(left, right, (((1,), (1,)), ((), ())), preferred_element_type=f32)


def tn(left, right):
    return lax.dot_general(left, right, (((0,), (0,)), ((), ())), preferred_element_type=f32)


def iota(shape, dim):
    return lax.broadcasted_iota(jnp.int32, shape, dim)


def onehot(cond):
    return jnp.where(cond, 1.0, 0.0).astype(bf16)


def normed(x):
    centered = x - jnp.mean(x, axis=-1, keepdims=True)
    scale = lax.rsqrt(jnp.mean(centered * centered, axis=-1, keepdims=True) + EPSILON)
    return centered * scale, scale


def norm_back(grad, xhat, scale, gain):
    inner = grad * gain
    mean_inner = jnp.mean(inner, axis=-1, keepdims=True)
    mean_cross = jnp.mean(inner * xhat, axis=-1, keepdims=True)
    return scale * (inner - mean_inner - xhat * mean_cross)


def gelu_both(u):
    cdf = 0.5 * (1.0 + lax.erf(u * 0.7071067811865476))
    return u * cdf, cdf + u * (jnp.exp(u * u * -0.5) * 0.3989422804014327)


def column_sum(v):
    return jnp.sum(v, axis=0, keepdims=True)


V_A1, V_D, V_HB, V_A2, V_M, V_R = 0, 3, 6, 10, 13, 16


class Links:
    def __init__(self, send_sems, recv_sems):
        self.send_sems, self.recv_sems, self.used, self.sent = send_sems, recv_sems, 0, {}

    def take(self, count=1):
        first = self.used
        self.used += count
        return first

    def copy(self, number, src, dst, device):
        return pltpu.make_async_remote_copy(
            src_ref=src,
            dst_ref=dst,
            send_sem=self.send_sems.at[number],
            recv_sem=self.recv_sems.at[number],
            device_id=device,
            device_id_type=MESH,
        )

    def start(self, name, number=None):
        number = self.take() if number is None else number
        self.copy(number, *name()).start()
        self.sent[number] = name
        return number

    def arrived(self, number, there, device):
        self.copy(number, there, there, device).wait_recv()

    def left(self, number):
        self.copy(number, *self.sent.pop(number)()).wait_send()

    def drain(self):
        for number in list(self.sent):
            self.left(number)


def at_steps(hooks, i):
    for step, actions in hooks.items():

        @pl.when(i == step)
        def _():
            for action in actions:
                action()


def block_kernel(bits, r):
    R, D = r.patches.shape[1:]
    FF = r.up.shape[1]
    xraw = r.h3.at[pl.ds(0, R)]
    IMG = R // PATCHES
    RT = IMG * RP
    FC = D
    NF = FF // FC
    NS = 4
    sec = lax.axis_index("section")
    wide = lax.axis_index("wide")
    core = lax.rem(wide, 2)
    chip = wide // 2
    links = Links(r.send, r.recv)

    sec_hi, sec_lo = sec // 2, lax.rem(sec, 2)

    def flip(bit, by):
        return bit + by - 2 * bit * by

    peers = [flip(sec_hi, j // 2) * 2 + flip(sec_lo, j % 2) for j in range(NS)]
    at_section = [(peer, wide) for peer in peers]
    mate = (sec, wide + 1 - 2 * core)
    bit_of = [lax.rem(chip // (1 << b), 2) for b in range(bits)]
    near_bits = min(bits, 2)
    near = 1 << near_bits
    at_near = []
    for k in range(near):
        other = wide
        for b in range(near_bits):
            if k >> b & 1:
                other = other + (1 - 2 * bit_of[b]) * (2 << b)
        at_near.append((sec, other))
    at_chip = [at_near[1 << b] if b < near_bits else (sec, wide + (1 - 2 * bit_of[b]) * (2 << b)) for b in range(bits)]
    near_index = lax.rem(chip, near)
    near_indices = []
    for k in range(near):
        index = 0
        for b in range(near_bits):
            index = index + flip(bit_of[b], k >> b & 1) * (1 << b)
        near_indices.append(index)

    def peer_of(j):
        return flip(sec_hi, j // 2) * 2 + flip(sec_lo, lax.rem(j, 2))

    local = []

    def fetch(src, dst):
        c = pltpu.make_async_copy(src, dst, r.local.at[len(local)])
        c.start()
        local.append(c)
        return c

    small = [fetch(getattr(r, name), getattr(r, "v_" + name)) for name in SMALL_IN]
    fetch_x = fetch(r.patches.at[sec], xraw)
    fetch_c = [fetch(r.cotangent.at[m], r.pool.at[pl.ds(m * R, R)]) for m in range(NS)]

    r.rt[...] = jnp.zeros(r.rt.shape, f32)

    barrier = pltpu.get_barrier_semaphore()
    partners = at_section[1:] + [mate] + at_near[1:] + at_chip[near_bits:]
    for device in partners:
        pl.semaphore_signal(barrier, inc=1, device_id=device, device_id_type=MESH)
    pl.semaphore_wait(barrier, len(partners))

    shards = [
        (r.s_p1, r.w_p1),
        (r.s_o1, r.w_o1),
        (r.s_up, r.w_up),
        (r.s_dn, r.w_dn),
        (r.s_p2, r.w_p2),
        (r.s_o2, r.w_o2),
    ]
    SPREAD = 3
    direct, passed, spread = {}, {}, {}

    def piece(t, j, c, part=None):
        n = shards[t][0].shape[0]
        h = n // 2
        at, rows = peers[j] * n + c * h, h
        if part is not None:
            rows = h // near
            at = at + part * rows
        return shards[t][1].at[pl.ds(pl.multiple_of(at, 16), rows)]

    def own(t, part=None):
        n = shards[t][0].shape[0]
        at, rows = core * (n // 2), n // 2
        if part is not None:
            rows = rows // near
            at = at + part * rows
        return shards[t][0].at[pl.ds(pl.multiple_of(at, 16), rows)]

    for t in (SPREAD, 0, 1, 2, 4, 5):
        part = near_index if t == SPREAD else None
        for j in range(1, NS):
            direct[t, j] = links.start(
                lambda t=t, j=j, part=part: (own(t, part), piece(t, 0, core, part), at_section[j])
            )
    fetch_w = []
    for shard, whole in shards:
        n = shard.shape[0]
        fetch_w.append(fetch(shard, whole.at[pl.ds(pl.multiple_of(sec * n, n), n)]))
    fetch_up = fetch(r.expert_up.at[0], r.up)
    fetch_dn = fetch(r.expert_down.at[0], r.down)

    def spread_on():
        for j in range(1, NS):
            links.arrived(direct[SPREAD, j], piece(SPREAD, j, core, near_index), at_section[j])
            for k in range(1, near):
                spread[j, k] = links.start(
                    lambda j=j, k=k: (piece(SPREAD, j, core, near_index), piece(SPREAD, j, core, near_index), at_near[k])
                )

    def pass_on(*group):
        for t in group:
            for j in range(1, NS):
                if t == SPREAD:
                    for k in range(1, near):
                        links.arrived(spread[j, k], piece(t, j, core, near_indices[k]), at_near[k])
                else:
                    links.arrived(direct[t, j], piece(t, j, core), at_section[j])
                passed[t, j] = links.start(lambda t=t, j=j: (piece(t, j, core), piece(t, j, core), mate))

    def landed(*group):
        for t in group:
            fetch_w[t].wait()
            for j in range(1, NS):
                links.arrived(passed[t, j], piece(t, j, 1 - core), mate)

    for c in small:
        c.wait()
    q = D // NS
    r.rt[sec, 0 : TASKS * EXPERTS, 0:q] = r.v_router[...].astype(f32)
    router_numbers = {}
    for j in range(1, NS):
        router_numbers[j] = links.start(
            lambda j=j: (
                r.rt.at[sec, pl.ds(0, TASKS * EXPERTS)],
                r.rt.at[sec, pl.ds(0, TASKS * EXPERTS)],
                at_section[j],
            )
        )
    vec = Bag()
    for k, name in enumerate(VECTORS):
        line = getattr(r, "v_" + name)
        r.lines[k : k + 1, 0 : line.shape[0]] = line[...].reshape(1, -1)
        setattr(vec, name, r.lines.at[pl.ds(k, 1), pl.ds(0, line.shape[0])])

    def chosen_rows(m_is, expert):
        r0 = jnp.zeros((1, R), jnp.int32)
        r1, k0, k1 = r0, r0, r0
        for m in range(NS):
            mine = jnp.where(m_is == m, 1, 0)
            r0 = r0 + mine * r.v_routes[m, 0:1, :]
            r1 = r1 + mine * r.v_routes[m, 1:2, :]
            k0 = k0 + mine * r.v_keep[m, 0:1, :]
            k1 = k1 + mine * r.v_keep[m, 1:2, :]
        return jnp.where(((r0 == expert) & (k0 == 1)) | ((r1 == expert) & (k1 == 1)), 1.0, 0.0)

    r.chosen[...] = jnp.zeros(r.chosen.shape, f32)
    for j in range(NS):
        r.chosen[j : j + 1, :] = chosen_rows(sec, peers[j])
        r.chosen[4 + j : 5 + j, :] = chosen_rows(peers[j], sec)

    def slots_of(limit, valid):
        chosen = r.chosen[...].astype(bf16)
        column = iota((limit.shape[0], R), 1)
        before = nt(onehot(column < limit), chosen)
        upto = nt(onehot((column <= limit) & valid), chosen)
        return jnp.where(upto > before, before, -1.0)

    def slots_padded(i, carry):
        off = iota((RP, 1), 0)
        r.pos_pad[pl.ds(pl.multiple_of(i * RP, RP), RP), :] = slots_of(i * PATCHES + off, off < PATCHES)
        return carry

    lax.fori_loop(0, IMG, slots_padded, 0)
    RC = R // 7

    def slots_raw(i, carry):
        off = iota((RC, 1), 0)
        r.pos_raw[pl.ds(pl.multiple_of(i * RC, RC), RC), :] = slots_of(i * RC + off, off >= 0)
        return carry

    lax.fori_loop(0, 7, slots_raw, 0)

    fetch_x.wait()
    for c in fetch_c:
        c.wait()
    for i in range(IMG):
        start = (PATCHES * i) // 16 * 16
        gap = PATCHES * i - start
        a, b = iota((RP, RP), 0), iota((RP, RP), 1)
        shift = onehot((b == a + gap) & (a < PATCHES))
        r.h0[i * RP : (i + 1) * RP, :] = dot(shift, xraw[start : start + RP, :]).astype(bf16)
        first = pl.multiple_of(sec * R + start, 16)
        r.g3[i * RP : (i + 1) * RP, :] = dot(shift, r.pool[pl.ds(first, RP), :]).astype(bf16)

    spread_on()

    slot_lane = iota((1, SL), 1).astype(f32)
    for j in range(NS):
        pick = onehot(r.pos_raw[:, 4 + j : 5 + j] == slot_lane)
        first = pl.multiple_of(peers[j] * R, 16)
        r.gslot[j] = tn(pick, r.pool[pl.ds(first, R), :]).astype(bf16)
        row = iota((R, 128), 0)
        task = jnp.zeros((R, 128), jnp.int32)
        for i in range(IMG):
            task = jnp.where((row >= i * PATCHES) & (row < (i + 1) * PATCHES), r.v_task[peers[j], i], task)
        r.tslot[j] = tn(pick, task.astype(f32).astype(bf16)).astype(bf16)

    low_half = iota((1, 128), 1) < 64
    half_masks = [onehot(low_half), onehot(jnp.logical_not(low_half))]
    low_half_rows = iota((RP, 128), 1) < 64
    key_ok = iota((RP, RP), 0) < PATCHES

    def attend(h_in, h_out, vecs, w_p, w_o, qkv_s, p_s, ctx_s, hooks):
        gain, shift, bias = vecs

        def image(i, carry):
            rows = pl.ds(pl.multiple_of(i * RP, RP), RP)
            x = h_in[rows, :].astype(f32)
            a = (normed(x)[0] * gain[...] + shift[...]).astype(bf16)
            qkv = dot(a, w_p[...]).astype(bf16)
            qkv_s[rows, :] = qkv
            parts = []
            for pair in range(HEADS // 2):
                at = 128 * pair
                q2 = qkv[:, at : at + 128]
                k2 = qkv[:, D + at : D + at + 128]
                v2 = qkv[:, 2 * D + at : 2 * D + at + 128]
                outs = []
                for half in range(2):
                    scores = nt(k2 * half_masks[half], q2)
                    scores = jnp.where(key_ok, scores, -1e30)
                    top = jnp.max(scores, axis=0, keepdims=True)
                    e = jnp.exp((scores - top) * HEAD_DIM**-0.5)
                    p = (e * (1.0 / jnp.sum(e, axis=0, keepdims=True))).astype(bf16)
                    p_s[i * HEADS + 2 * pair + half] = p
                    outs.append(tn(p, v2))
                parts.append(jnp.where(low_half_rows, outs[0], outs[1]).astype(bf16))
            ctx = jnp.concatenate(parts, axis=1)
            ctx_s[rows, :] = ctx
            h_out[rows, :] = (x + dot(ctx, w_o[...]) + bias[...]).astype(bf16)
            at_steps(hooks, i)
            return carry

        lax.fori_loop(0, IMG, image, 0)

    def attend_back(h_in, g_in, g_out, vecs, w_p, w_o, qkv_s, p_s, ctx_s, vrow, hooks):
        gain, shift, _ = vecs

        def image(i, carry):
            rows = pl.ds(pl.multiple_of(i * RP, RP), RP)
            g = g_in[rows, :]
            gf = g.astype(f32)
            xhat, scale = normed(h_in[rows, :].astype(f32))
            r.a_s[rows, :] = (xhat * gain[...] + shift[...]).astype(bf16)
            gc = nt(g, w_o[...]).astype(bf16)
            qkv = qkv_s[rows, :]
            gq, gk, gv = [], [], []
            for pair in range(HEADS // 2):
                at = 128 * pair
                q2 = qkv[:, at : at + 128]
                k2 = qkv[:, D + at : D + at + 128]
                v2 = qkv[:, 2 * D + at : 2 * D + at + 128]
                gc2 = gc[:, at : at + 128]
                two = []
                for half in range(2):
                    p = p_s[i * HEADS + 2 * pair + half]
                    pf = p.astype(f32)
                    gp = nt(v2 * half_masks[half], gc2)
                    t = pf * gp
                    gs = (t - pf * jnp.sum(t, axis=0, keepdims=True)).astype(bf16)
                    two.append((tn(gs, k2), dot(gs, q2), dot(p, gc2)))
                gq.append((jnp.where(low_half_rows, two[0][0], two[1][0]) * HEAD_DIM**-0.5).astype(bf16))
                gk.append((jnp.where(low_half_rows, two[0][1], two[1][1]) * HEAD_DIM**-0.5).astype(bf16))
                gv.append(jnp.where(low_half_rows, two[0][2], two[1][2]).astype(bf16))
            gqkv = jnp.concatenate(gq + gk + gv, axis=1)
            qkv_s[rows, :] = gqkv
            ga = nt(gqkv, w_p[...])
            r.vec[vrow : vrow + 1, :] += column_sum(ga * xhat)
            r.vec[vrow + 1 : vrow + 2, :] += column_sum(ga)
            r.vec[vrow + 2 : vrow + 3, :] += column_sum(gf)
            g_out[rows, :] = (gf + norm_back(ga, xhat, scale, gain[...])).astype(bf16)
            at_steps(hooks, i)
            return carry

        lax.fori_loop(0, IMG, image, 0)

    r.vec[...] = jnp.zeros(r.vec.shape, f32)
    att1 = (vec.first_gain, vec.first_shift, vec.first_bias)
    att2 = (vec.second_gain, vec.second_shift, vec.second_bias)

    pass_on(0, 1)
    landed(0, 1)
    attend(r.h0, r.h1, att1, r.w_p1, r.w_o1, r.qkv1, r.p1, r.ctx1, {IMG - 1: [lambda: pass_on(3, 2)]})
    landed(3, 2)
    HR = RT // 2

    def dense_step(i, carry):
        rows = pl.ds(pl.multiple_of(i * HR, HR), HR)
        x = r.h1[rows, :].astype(f32)
        a = (normed(x)[0] * vec.dense_gain[...] + vec.dense_shift[...]).astype(bf16)
        total = x + vec.dense_bias[...]
        for f in range(NF):
            cols = slice(f * FC, (f + 1) * FC)
            u = dot(a, r.w_up[:, cols]) + vec.hidden_bias[:, cols]
            z, slope = gelu_both(u)
            z = z.astype(bf16)
            r.z[rows, cols] = z
            r.slope[rows, cols] = slope.astype(bf16)
            total = total + dot(z, r.w_dn[cols, :])
        r.h2[rows, :] = total.astype(bf16)
        at_steps({1: [lambda: pass_on(4, 5)]}, i)
        return carry

    lax.fori_loop(0, 2, dense_step, 0)
    landed(4, 5)
    attend(r.h2, r.h3, att2, r.w_p2, r.w_o2, r.qkv2, r.p2, r.ctx2, {})

    for j in range(1, NS):
        links.arrived(router_numbers[j], r.rt.at[peers[j], pl.ds(0, TASKS * EXPERTS)], at_section[j])
    for p in range(NS):
        r.w_rt[p * q : (p + 1) * q, :] = r.rt[p].T[0:q, :].astype(bf16)
    lane = iota((1, 128), 1)

    def gates_of(a, task):
        logits = dot(a, r.w_rt[...])
        active = (lane < TASKS * EXPERTS) & (lane // EXPERTS == task)
        top = jnp.max(jnp.where(active, logits, -1e30), axis=-1, keepdims=True)
        e = jnp.where(active, jnp.exp(jnp.minimum(logits - top, 0.0)), 0.0)
        return e / jnp.sum(e, axis=-1, keepdims=True)

    def mix_rows(i, carry):
        rows = pl.ds(pl.multiple_of(i * RP, RP), RP)
        a = (normed(r.h3[rows, :].astype(f32))[0] * vec.mixture_gain[...] + vec.mixture_shift[...]).astype(bf16)
        r.a4[rows, :] = a
        return carry

    lax.fori_loop(0, IMG, mix_rows, 0)

    slots_first = links.take(NS)
    for j in (1, 2, 3, 0):
        pick = onehot(r.pos_pad[:, j : j + 1] == slot_lane)
        r.slot_out[j] = tn(pick, r.a4[...]).astype(bf16)
        if j > 0:
            links.start(lambda j=j: (r.slot_out.at[j], r.slot_in.at[j], at_section[j]), slots_first + j)
        else:
            r.slot_in[0] = r.slot_out[0]

    fetch_up.wait()
    fetch_dn.wait()
    r.eg[...] = jnp.zeros(r.eg.shape, f32)
    ga_first, q_first, w_first = links.take(NS), links.take(NS), links.take(NS)
    out_acc, ga_acc = r.acc.at[pl.ds(0, SL)], r.acc.at[pl.ds(SL, SL)]

    def ga_in(j):
        return r.pool.at[pl.ds((j - 1) * SL, SL)]

    def w_in(j):
        return r.pool.at[pl.ds((j + 2) * SL, SL)]

    def expert_step(j, carry):
        there = (peer_of(j), wide)

        @pl.when(j > 0)
        def _():
            links.copy(slots_first + j, r.slot_out.at[j], r.slot_in.at[j], there).wait()

        a = r.slot_in[j]
        gs = r.gslot[j]
        gates = gates_of(a, r.tslot[j][:, 0:1].astype(jnp.int32))
        combine = jnp.sum(jnp.where(lax.rem(lane, EXPERTS) == sec, gates, 0.0), axis=-1, keepdims=True)
        gout = (combine * gs.astype(f32)).astype(bf16)
        for f in range(NF):
            cols = slice(f * FC, (f + 1) * FC)
            z, slope = gelu_both(dot(a, r.up[:, cols]))
            z = z.astype(bf16)
            part = dot(z, r.down[cols, :])
            gv = (nt(gout, r.down[cols, :]) * slope).astype(bf16)
            gpart = nt(gv, r.up[:, cols])
            if f == 0:
                out_acc[...] = part
                ga_acc[...] = gpart
            else:
                out_acc[...] += part
                ga_acc[...] += gpart
            r.eg[0, :, cols] += tn(a, gv)
            r.eg[1, :, cols] += tn(z, gout)
        r.slot_out[j] = ga_acc[...].astype(bf16)
        weighted = combine * out_acc[...].astype(bf16).astype(f32)
        q = jnp.sum(gs.astype(f32) * weighted, axis=-1, keepdims=True)
        q_hi = q.astype(bf16).astype(f32)
        lanes = iota((SL, 128), 1)
        q2 = jnp.where(lanes == 0, q_hi, jnp.where(lanes == 1, q - q_hi, 0.0))
        r.q_out[j] = q2.T[0:16, :].astype(bf16)
        r.gslot[j] = weighted.astype(bf16)

        @pl.when(j > 0)
        def _():
            links.copy(ga_first + j, r.slot_out.at[j], ga_in(j), there).start()
            links.copy(q_first + j, r.q_out.at[j], r.q_in.at[j], there).start()

        return carry

    lax.fori_loop(0, NS, expert_step, 0)

    for j in range(1, NS):
        links.sent.pop(slots_first + j)

    def grads_back(j):
        links.copy(ga_first + j, r.slot_out.at[j], ga_in(j), at_section[j]).wait()
        links.copy(q_first + j, r.q_out.at[j], r.q_in.at[j], at_section[j]).wait()

    e_core = links.take(NF)
    for b in range(NF):
        cols = slice(b * FC, (b + 1) * FC)
        r.up[:, cols] = r.eg[1 - core, :, cols].astype(bf16)
        links.start(lambda b=b, cols=cols: (r.up.at[:, cols], r.e_sum.at[b], mate), e_core + b)
    for j in range(1, NS):
        links.start(lambda j=j: (r.gslot.at[j], w_in(j), at_section[j]), w_first + j)

    half_rows = D // 2
    parts = []
    for k in range(2):
        lo, n, down, up = 0, NF, [], []
        order = list(range(bits)) if k == 0 else list(range(bits))[::-1]
        for b in order:
            v = bit_of[b]
            if n > 1:
                n = n // 2
                down.append((b, lo + v * n, lo + (1 - v) * n, n, True))
                lo = lo + v * n
            else:
                down.append((b, lo, lo, 1, False))
        at = lo
        for b, _, _, half, halved in down[::-1]:
            if halved:
                up.append((b, at, at + (1 - 2 * bit_of[b]) * half, half))
                at = at - bit_of[b] * half
        parts.append(
            Bag(k=k, rows=pl.ds(k * half_rows, half_rows), down=down, up=up, lo=lo, n=n, land=(r.e_land, r.e_land2)[k])
        )
    e_numbers = {}

    def e_first():
        for b in range(NF):
            cols = slice(b * FC, (b + 1) * FC)
            links.arrived(e_core + b, r.e_sum.at[b], mate)
            r.e_sum[b] = (r.eg[core, :, cols] + r.e_sum[b].astype(f32)).astype(bf16)

    def e_land(part, step):
        return part.land.at[pl.ds(step + (step > 0), part.down[step][3])]

    def e_start(step):
        for part in parts:
            b, _, send, half, _ = part.down[step]
            e_numbers[part.k, step] = links.start(
                lambda part=part, b=b, send=send, half=half: (
                    r.e_sum.at[pl.ds(send, half), part.rows],
                    e_land(part, step),
                    at_chip[b],
                )
            )

    def e_end(step):
        for part in parts:
            b, keep, _, half, halved = part.down[step]
            number = e_numbers[part.k, step]
            links.arrived(number, e_land(part, step), at_chip[b])
            if not halved:
                links.left(number)
            for i in range(half):
                mine = r.e_sum[keep + i, part.rows, :].astype(f32)
                r.e_sum[keep + i, part.rows, :] = (mine + e_land(part, step)[i].astype(f32)).astype(bf16)

    def e_own():
        for part in parts:
            for i in range(part.n):
                r.e_all[core, part.lo + i, part.rows, :] = r.e_sum[part.lo + i, part.rows, :]

    def e_gather_start(step):
        for part in parts:
            b, at, _, half = part.up[step]
            e_numbers[part.k, step, "up"] = links.start(
                lambda part=part, b=b, at=at, half=half: (
                    r.e_all.at[core, pl.ds(at, half), part.rows],
                    r.e_all.at[core, pl.ds(at, half), part.rows],
                    at_chip[b],
                )
            )

    def e_gather_end(step):
        for part in parts:
            b, _, there, half = part.up[step]
            links.arrived(e_numbers[part.k, step, "up"], r.e_all.at[core, pl.ds(there, half), part.rows], at_chip[b])

    def e_pair_start():
        e_numbers["pair"] = links.start(lambda: (r.e_all.at[core], r.e_all.at[core], mate))

    def e_pair_end():
        links.arrived(e_numbers["pair"], r.e_all.at[1 - core], mate)

    ups = len(parts[0].up)

    class Summed:
        def __init__(self, buffers):
            self.b = buffers
            self.numbers = {}

        def cut(self, k):
            rows, cols = self.b.pair.shape[1:]
            if self.b.by_rows:
                return pl.ds(k * (rows // 2), rows // 2), pl.ds(0, cols)
            return pl.ds(0, rows), pl.ds(k * (cols // 2), cols // 2)

        def send_core(self, halves=(0, 1)):
            b = self.b
            for k in halves:
                self.numbers["core", k] = links.start(
                    lambda k=k: (b.full.at[(pl.ds(0, NS), 1 - core) + self.cut(k)], b.pair.at[(pl.ds(0, NS),) + self.cut(k)], mate)
                )

        def send_section(self, halves=(0, 1)):
            b = self.b
            for k in halves:
                links.arrived(self.numbers["core", k], b.pair.at[(pl.ds(0, NS),) + self.cut(k)], mate)
                links.left(self.numbers["core", k])
                for p in range(NS):
                    mine = b.full[(p, core) + self.cut(k)].astype(f32)
                    b.pair[(p,) + self.cut(k)] = (mine + b.pair[(p,) + self.cut(k)].astype(f32)).astype(bf16)
                for j in range(1, NS):
                    self.numbers["section", k, j] = links.start(
                        lambda k=k, j=j: (b.pair.at[(peers[j],) + self.cut(k)], b.sec.at[(j - 1,) + self.cut(k)], at_section[j])
                    )

        def section_sum(self, halves=(0, 1)):
            b = self.b
            for k in halves:
                total = b.pair[(sec,) + self.cut(k)].astype(f32)
                for j in range(1, NS):
                    there = (j - 1,) + self.cut(k)
                    links.arrived(self.numbers["section", k, j], b.sec.at[there], at_section[j])
                    total = total + b.sec[there].astype(f32)
                b.fin[core, k] = total.astype(bf16)

        def chip_start(self, step, halves=(0, 1)):
            for k in halves:
                bit = step if k == 0 else bits - 1 - step
                self.numbers["chip", k] = links.start(
                    lambda k=k, bit=bit: (self.b.fin.at[core, k], self.b.land.at[step, k], at_chip[bit])
                )

        def chip_end(self, step, halves=(0, 1)):
            for k in halves:
                bit = step if k == 0 else bits - 1 - step
                number = self.numbers["chip", k]
                links.arrived(number, self.b.land.at[step, k], at_chip[bit])
                links.left(number)
                mine = self.b.fin[core, k].astype(f32)
                self.b.fin[core, k] = (mine + self.b.land[step, k].astype(f32)).astype(bf16)

        def pair_start(self, halves=(0, 1)):
            for k in halves:
                self.numbers["pair", k] = links.start(lambda k=k: (self.b.fin.at[core, k], self.b.fin.at[core, k], mate))

        def pair_end(self, halves=(0, 1)):
            for k in halves:
                links.arrived(self.numbers["pair", k], self.b.fin.at[1 - core, k], mate)

    def by_section_rows(full, cols, value):
        n = D // NS // 2
        for p in range(NS):
            for c in range(2):
                full[p, c, :, cols] = value[(2 * p + c) * n : (2 * p + c + 1) * n, :].astype(bf16)

    sum_a2, sum_du, sum_dd, sum_a1 = (Summed(b) for b in (r.t_a2, r.t_du, r.t_dd, r.t_a1))
    out_copies = []

    def send_out(src, dst):
        c = pltpu.make_async_copy(src, dst, r.out_sems.at[len(out_copies)])
        c.start()
        out_copies.append(c)

    def mix_gather(experts, first):
        def step(i, carry):
            rows = pl.ds(pl.multiple_of(i * RP, RP), RP)
            task = jnp.zeros((RP, 1), jnp.int32) + r.v_task[sec, i]
            active = (lane < TASKS * EXPERTS) & (lane // EXPERTS == task)
            ga = jnp.zeros((RP, D), f32) if first else r.acc[rows, :]
            q8 = jnp.zeros((RP, 128), f32) if first else r.q8[rows, :]
            for j in experts:
                pick = onehot(r.pos_pad[rows, j : j + 1] == slot_lane)
                ga = ga + dot(pick, r.slot_out[0] if j == 0 else ga_in(j)[...])
                one = jnp.sum(nt(pick, r.q_out[0] if j == 0 else r.q_in[j]), axis=-1, keepdims=True)
                q8 = q8 + jnp.where(active & (lax.rem(lane, EXPERTS) == peers[j]), one, 0.0)
            if first:
                r.acc[rows, :] = ga
                r.q8[rows, :] = q8
                return carry
            a = r.a4[rows, :]
            gl = (q8 - gates_of(a, task) * jnp.sum(q8, axis=-1, keepdims=True)).astype(bf16)
            ga = ga + nt(gl, r.w_rt[...])
            r.vec[V_R : V_R + 8, :] += tn(gl, a)[0:8, :]
            xhat, scale = normed(r.h3[rows, :].astype(f32))
            r.vec[V_M : V_M + 1, :] += column_sum(ga * xhat)
            r.vec[V_M + 1 : V_M + 2, :] += column_sum(ga)
            g = r.g3[rows, :].astype(f32)
            r.g2[rows, :] = (g + norm_back(ga, xhat, scale, vec.mixture_gain[...])).astype(bf16)
            return carry

        lax.fori_loop(0, IMG, step, 0)

    e_first()
    if bits > 0:
        e_start(0)
    grads_back(1)
    grads_back(2)
    mix_gather((0, 1, 2), True)
    grads_back(3)
    mix_gather((3,), False)

    def e_second():
        if bits > 0:
            e_end(0)
        if bits > 1:
            e_start(1)

    def e_third():
        for step in range(1, bits):
            if step > 1:
                e_start(step)
            e_end(step)
        e_own()
        if ups > 0:
            e_gather_start(0)

    def e_fourth():
        if ups > 0:
            e_gather_end(0)
        if ups > 1:
            e_gather_start(1)

    def e_fifth():
        if ups > 1:
            e_gather_end(1)
        e_pair_start()

    attend_back(
        r.h2, r.g2, r.g1, att2, r.w_p2, r.w_o2, r.qkv2, r.p2, r.ctx2, V_A2, {min(2, IMG - 1): [e_second]}
    )
    for f in range(3):
        cols = slice(f * D, (f + 1) * D)
        by_section_rows(r.t_a2.full, cols, tn(r.a_s[...], r.qkv2[:, cols]))
    by_section_rows(r.t_a2.full, slice(3 * D, 4 * D), tn(r.ctx2[...], r.g2[...]))
    sum_a2.send_core()

    def dense_back(i, carry):
        rows = pl.ds(pl.multiple_of(i * HR, HR), HR)
        g = r.g1[rows, :]
        gf = g.astype(f32)
        xhat, scale = normed(r.h1[rows, :].astype(f32))
        r.a_s[rows, :] = (xhat * vec.dense_gain[...] + vec.dense_shift[...]).astype(bf16)
        ga = jnp.zeros((HR, D), f32)
        for f in range(NF):
            cols = slice(f * FC, (f + 1) * FC)
            gu = (nt(g, r.w_dn[cols, :]) * r.slope[rows, cols].astype(f32)).astype(bf16)
            r.slope[rows, cols] = gu
            r.vec[V_HB + f : V_HB + f + 1, :] += column_sum(gu.astype(f32))
            ga = ga + nt(gu, r.w_up[:, cols])
        r.vec[V_D : V_D + 1, :] += column_sum(ga * xhat)
        r.vec[V_D + 1 : V_D + 2, :] += column_sum(ga)
        r.vec[V_D + 2 : V_D + 3, :] += column_sum(gf)
        r.g0[rows, :] = (gf + norm_back(ga, xhat, scale, vec.dense_gain[...])).astype(bf16)
        at_steps({0: [sum_a2.send_section], 1: [e_third]}, i)
        return carry

    lax.fori_loop(0, 2, dense_back, 0)

    for f in range(NF):
        cols = slice(f * FC, (f + 1) * FC)
        by_section_rows(r.t_du.full, cols, tn(r.a_s[...], r.slope[:, cols]))
    sum_du.send_core()
    for f in range(NF):
        value = tn(r.z[:, f * FC : (f + 1) * FC], r.g1[...])
        n = FC // 2
        for c in range(2):
            r.t_dd.full[f, c] = value[c * n : (c + 1) * n, :].astype(bf16)
    sum_dd.send_core()
    e_fourth()

    for j in range(1, NS):
        links.arrived(w_first + j, w_in(j), at_section[j])

    def block_out(i, carry):
        rows = pl.ds(pl.multiple_of(i * RP, RP), RP)
        total = r.h3[rows, :].astype(f32)
        for j in range(NS):
            pick = onehot(r.pos_pad[rows, j : j + 1] == slot_lane)
            total = total + dot(pick, r.gslot[0] if j == 0 else w_in(j)[...])
        r.a4[rows, :] = total.astype(bf16)
        return carry

    lax.fori_loop(0, IMG, block_out, 0)
    send_out(r.a4, r.o_block)
    sum_a2.section_sum()
    if bits > 0:
        sum_a2.chip_start(0)

    def chips_rest(one, halves=(0, 1)):
        for step in range(1, bits):
            one.chip_end(step - 1, halves)
            one.chip_start(step, halves)

    def chips_last(one, halves=(0, 1)):
        if bits > 0:
            one.chip_end(bits - 1, halves)
        one.pair_start(halves)

    def sections_two():
        for one in (sum_du, sum_dd):
            one.section_sum()
            if bits > 0:
                one.chip_start(0)

    attend_back(
        r.h0, r.g0, r.g3, att1, r.w_p1, r.w_o1, r.qkv1, r.p1, r.ctx1, V_A1,
        {
            0: [sum_du.send_section, sum_dd.send_section],
            1: [lambda: chips_rest(sum_a2)],
            2: [sections_two],
            3: [lambda: chips_last(sum_a2)],
        },
    )
    send_out(r.g3, r.o_grad)
    a1 = r.t_a1.full
    by_section_rows(a1, slice(2 * D, 3 * D), tn(r.a_s[...], r.qkv1[:, 2 * D : 3 * D]))
    by_section_rows(a1, slice(3 * D, 4 * D), tn(r.ctx1[...], r.g0[...]))
    sum_a1.send_core((1,))
    for f in range(2):
        cols = slice(f * D, (f + 1) * D)
        by_section_rows(a1, cols, tn(r.a_s[...], r.qkv1[:, cols]))
    sum_a1.send_core((0,))

    def vec_start(land, device):
        return links.start(lambda: (r.vec, r.vec_land.at[land], device)), land, device

    def vec_end(number, land, device):
        links.arrived(number, r.vec_land.at[land], device)
        links.left(number)

    vec_core = vec_start(0, mate)
    sum_a1.send_section((1,))
    sum_a1.send_section((0,))
    vec_end(*vec_core)
    r.vec[...] += r.vec_land[0]
    vec_section = [vec_start(j, at_section[j]) for j in range(1, NS)]
    chips_rest(sum_du)
    chips_rest(sum_dd)
    e_fifth()
    for one in vec_section:
        vec_end(*one)
    r.vec[...] += r.vec_land[1] + r.vec_land[2] + r.vec_land[3]
    vec_chip = vec_start(NS, at_chip[0]) if bits > 0 else None
    for k in (1, 0):
        sum_a1.section_sum((k,))
        if bits > 0:
            sum_a1.chip_start(0, (k,))
    chips_last(sum_du)
    chips_last(sum_dd)
    for step in range(1, bits):
        for k in (1, 0):
            sum_a1.chip_end(step - 1, (k,))
            sum_a1.chip_start(step, (k,))
        vec_end(*vec_chip)
        r.vec[...] += r.vec_land[NS + step - 1]
        vec_chip = vec_start(NS + step, at_chip[step])
    e_pair_end()
    send_out(r.e_all, r.o_expert)
    for s, dst in ((sum_a2, r.o_a2), (sum_du, r.o_du), (sum_dd, r.o_dd)):
        s.pair_end()
        send_out(s.b.fin, dst)
    for k in (1, 0):
        chips_last(sum_a1, (k,))
    if bits > 0:
        vec_end(*vec_chip)
        r.vec[...] += r.vec_land[NS + bits - 1]
    send_out(r.vec, r.o_vec)
    sum_a1.pair_end()
    send_out(r.t_a1.fin, r.o_a1)
    links.drain()
    for c in out_copies:
        c.wait()
    assert links.used <= NSEM and len(local) <= 32 and len(out_copies) <= 8, links.used


class Bag:
    def __init__(self, **members):
        self.__dict__.update(members)


VECTORS = (
    "first_gain",
    "first_shift",
    "first_bias",
    "dense_gain",
    "dense_shift",
    "hidden_bias",
    "dense_bias",
    "second_gain",
    "second_shift",
    "second_bias",
    "mixture_gain",
    "mixture_shift",
)
SMALL_IN = ("task", "routes", "keep", "router") + VECTORS


def run_blocks(bits, arrays):
    R, D = arrays["patches"].shape[1:]
    FF = arrays["expert_up"].shape[2]
    IMG = R // PATCHES
    RT = IMG * RP
    n = D // 8
    vm = pltpu.VMEM
    scratch = dict(
        pool=vm((max(4 * R, 6 * SL), D), bf16),
        chosen=vm((16, R), f32),
        pos_pad=vm((RT, 16), f32),
        pos_raw=vm((R, 16), f32),
        w_p1=vm((D, 3 * D), bf16),
        w_o1=vm((D, D), bf16),
        w_up=vm((D, FF), bf16),
        w_dn=vm((FF, D), bf16),
        w_p2=vm((D, 3 * D), bf16),
        w_o2=vm((D, D), bf16),
        w_rt=vm((D, 128), bf16),
        rt=vm((4, 128, 128), f32),
        lines=vm((16, FF), f32),
        up=vm((D, FF), bf16),
        down=vm((FF, D), bf16),
        h0=vm((RT, D), bf16),
        h1=vm((RT, D), bf16),
        h2=vm((RT, D), bf16),
        h3=vm((RT, D), bf16),
        g0=vm((RT, D), bf16),
        g1=vm((RT, D), bf16),
        g2=vm((RT, D), bf16),
        g3=vm((RT, D), bf16),
        a_s=vm((RT, D), bf16),
        a4=vm((RT, D), bf16),
        qkv1=vm((RT, 3 * D), bf16),
        qkv2=vm((RT, 3 * D), bf16),
        p1=vm((IMG * HEADS, RP, RP), bf16),
        p2=vm((IMG * HEADS, RP, RP), bf16),
        ctx1=vm((RT, D), bf16),
        ctx2=vm((RT, D), bf16),
        z=vm((RT, FF), bf16),
        slope=vm((RT, FF), bf16),
        slot_out=vm((4, SL, D), bf16),
        slot_in=vm((4, SL, D), bf16),
        gslot=vm((4, SL, D), bf16),
        tslot=vm((4, SL, 128), bf16),
        q_out=vm((4, 16, SL), bf16),
        q_in=vm((4, 16, SL), bf16),
        acc=vm((2 * SL, D), f32),
        q8=vm((RT, 128), f32),
        eg=vm((2, D, FF), f32),
        e_sum=vm((4, D, D), bf16),
        e_land=vm((bits + 1, D // 2, D), bf16),
        e_land2=vm((bits + 1, D // 2, D), bf16),
        e_all=vm((2, 4, D, D), bf16),
        vec=vm((VROWS, D), f32),
        vec_land=vm((4 + max(bits, 1), VROWS, D), f32),
        send=pltpu.SemaphoreType.DMA((NSEM,)),
        recv=pltpu.SemaphoreType.DMA((NSEM,)),
        local=pltpu.SemaphoreType.DMA((32,)),
        out_sems=pltpu.SemaphoreType.DMA((8,)),
    )
    for name in SMALL_IN:
        space = pltpu.SMEM if name == "task" else vm
        scratch["v_" + name] = space(arrays[name].shape, arrays[name].dtype)
    sums = dict(t_a2=False, t_du=False, t_dd=True, t_a1=False)
    fin = {}
    for name, by_rows in sums.items():
        rows, cols = (D // 2, D) if by_rows else (n, FF)
        halved = (rows // 2, cols) if by_rows else (rows, cols // 2)
        if name in ("t_a2", "t_dd"):
            scratch[name + ".full"] = vm((4, 2, rows, cols), bf16)
        scratch[name + ".pair"] = vm((4, rows, cols), bf16)
        scratch[name + ".sec"] = vm((3, rows, cols), bf16)
        scratch[name + ".fin"] = vm((2, 2) + halved, bf16)
        scratch[name + ".land"] = vm((max(bits, 1), 2) + halved, bf16)
        fin[name] = jax.ShapeDtypeStruct((2, 2) + halved, bf16)
    outs = dict(
        o_block=jax.ShapeDtypeStruct((RT, D), bf16),
        o_grad=jax.ShapeDtypeStruct((RT, D), bf16),
        o_expert=jax.ShapeDtypeStruct((2, 4, D, D), bf16),
        o_a2=fin["t_a2"],
        o_du=fin["t_du"],
        o_dd=fin["t_dd"],
        o_a1=fin["t_a1"],
        o_vec=jax.ShapeDtypeStruct((VROWS, D), f32),
    )
    ins = list(arrays)
    names = ins + list(outs) + list(scratch)

    def body(*refs):
        members = {}
        for name, ref in zip(names, refs, strict=True):
            if "." in name:
                outer, inner = name.split(".")
                members.setdefault(outer, Bag(by_rows=sums[outer])).__dict__[inner] = ref
            else:
                members[name] = ref
        for name in ("t_du", "t_a1"):
            members[name].full = members["t_a2"].full
        block_kernel(bits, Bag(**members))

    return pl.pallas_call(
        body,
        out_shape=list(outs.values()),
        in_specs=[pl.BlockSpec(memory_space=pl.ANY)] * len(ins),
        out_specs=[pl.BlockSpec(memory_space=pl.ANY)] * len(outs),
        scratch_shapes=list(scratch.values()),
        compiler_params=pltpu.CompilerParams(
            collective_id=0, has_side_effects=True, vmem_limit_bytes=64 * 2**20 - 2**18
        ),
        name="blocks",
    )(*arrays.values())


FINISHED = ("block", "grad", "expert", "a2", "du", "dd", "a1", "vec")
BIG = ("block", "grad", "p1", "o1", "up", "dn", "p2", "o2", "eup", "edn")


def finish_kernel(r):
    RT, D = r.block.shape
    R = r.o_block.shape[1]
    sec = lax.axis_index("section")
    copies = {}
    for k, name in enumerate(FINISHED):
        copies[name] = pltpu.make_async_copy(getattr(r, name), getattr(r, "v_" + name), r.sems.at[k])
        copies[name].start()
    outs = []

    def send(name):
        c = pltpu.make_async_copy(getattr(r, "w_" + name), getattr(r, "o_" + name), r.sems.at[len(FINISHED) + len(outs)])
        c.start()
        outs.append(c)

    row, col = iota((R, RP), 0), iota((R, RP), 1)
    for name in ("block", "grad"):
        copies[name].wait()
        src, dst = getattr(r, "v_" + name), getattr(r, "w_" + name)
        total = jnp.zeros((R, D), f32)
        for i in range(R // PATCHES):
            pick = onehot((row - i * PATCHES == col) & (col < PATCHES))
            total = total + dot(pick, src[i * RP : (i + 1) * RP, :])
        dst[0] = total.astype(bf16)
        send(name)
    copies["expert"].wait()
    for b in range(4):
        r.w_eup[0, :, b * D : (b + 1) * D] = r.v_expert[0, b].astype(f32)
    send("eup")
    for b in range(4):
        r.w_edn[0, b * D : (b + 1) * D, :] = r.v_expert[1, b].astype(f32)
    send("edn")
    n = D // 8
    for k in ("2", "1"):
        copies["a" + k].wait()
        src, dst_p, dst_o = getattr(r, "v_a" + k), getattr(r, "w_p" + k), getattr(r, "w_o" + k)
        for c in range(2):
            rows = slice(c * n, (c + 1) * n)
            dst_p[rows, 0 : 2 * D] = src[c, 0].astype(f32)
            dst_p[rows, 2 * D : 3 * D] = src[c, 1, :, 0:D].astype(f32)
            dst_o[rows, :] = src[c, 1, :, D : 2 * D].astype(f32)
        send("p" + k)
        send("o" + k)
    copies["du"].wait()
    for c in range(2):
        for k in range(2):
            r.w_up[c * n : (c + 1) * n, k * 2 * D : (k + 1) * 2 * D] = r.v_du[c, k].astype(f32)
    send("up")
    copies["dd"].wait()
    m = r.v_dd.shape[2]
    for c in range(2):
        for k in range(2):
            at = (2 * c + k) * m
            r.w_dn[at : at + m, :] = r.v_dd[c, k].astype(f32)
    send("dn")
    copies["vec"].wait()
    q = D // 4
    mine = jnp.where(iota((D, q), 0) == iota((D, q), 1) + sec * q, 1.0, 0.0)
    cut = jnp.dot(r.v_vec[...], mine, precision=lax.Precision.HIGHEST, preferred_element_type=f32)
    for dst, at in (
        (r.o_g1, V_A1), (r.o_s1, V_A1 + 1), (r.o_b1, V_A1 + 2), (r.o_gd, V_D), (r.o_sd, V_D + 1), (r.o_db, V_D + 2),
        (r.o_g2, V_A2), (r.o_s2, V_A2 + 1), (r.o_b2, V_A2 + 2), (r.o_gm, V_M), (r.o_sm, V_M + 1),
    ):
        dst[...] = cut[at : at + 1, :]
    r.o_rt[...] = cut[V_R : V_R + 8, :]
    r.o_hb[...] = r.v_vec[pl.ds(V_HB + sec, 1), :].reshape(-1)
    for c in outs:
        c.wait()


def finish(parts, shape):
    R, D, FF = shape
    q = D // 4
    s = lambda *dims: jax.ShapeDtypeStruct(dims, f32)
    rows = jax.ShapeDtypeStruct((1, R, D), bf16)
    outs = dict(
        block=rows, grad=rows,
        g1=s(1, q), s1=s(1, q), p1=s(q, 3 * D), o1=s(q, D), b1=s(1, q),
        gd=s(1, q), sd=s(1, q), up=s(q, FF), hb=s(FF // 4), dn=s(FF // 4, D), db=s(1, q),
        g2=s(1, q), s2=s(1, q), p2=s(q, 3 * D), o2=s(q, D), b2=s(1, q),
        gm=s(1, q), sm=s(1, q), rt=s(8, q), eup=s(1, D, FF), edn=s(1, FF, D),
    )
    scratch = {"v_" + name: pltpu.VMEM(part.shape, part.dtype) for name, part in zip(FINISHED, parts)}
    scratch |= {"w_" + name: pltpu.VMEM(outs[name].shape, outs[name].dtype) for name in BIG}
    scratch["sems"] = pltpu.SemaphoreType.DMA((len(FINISHED) + len(BIG),))
    names = list(FINISHED) + ["o_" + name for name in outs] + list(scratch)
    anywhere, near = pl.BlockSpec(memory_space=pltpu.HBM), pl.BlockSpec(memory_space=pltpu.VMEM)

    def body(*refs):
        finish_kernel(Bag(**dict(zip(names, refs, strict=True))))

    return pl.pallas_call(
        body,
        out_shape=list(outs.values()),
        in_specs=[anywhere] * len(FINISHED),
        out_specs=[anywhere if name in BIG else near for name in outs],
        scratch_shapes=list(scratch.values()),
        compiler_params=pltpu.CompilerParams(vmem_limit_bytes=62 * 2**20),
        name="finish",
    )(*parts)


def local(
    patches_in, cotangent, task_ids, routes, keep_mask,
    first_gain, first_shift, first_proj, first_out, first_bias,
    dense_gain, dense_shift, dense_up, hidden_bias, dense_down, dense_bias,
    second_gain, second_shift, second_proj, second_out, second_bias,
    mixture_gain, mixture_shift, router, expert_up, expert_down,
):
    bits = (lax.axis_size("wide") // 2).bit_length() - 1
    arrays = dict(
        patches=patches_in,
        cotangent=cotangent,
        task=task_ids,
        routes=jnp.transpose(routes, (0, 2, 1)),
        keep=jnp.transpose(keep_mask, (0, 2, 1)),
        s_p1=first_proj,
        s_o1=first_out,
        s_up=dense_up,
        s_dn=dense_down,
        s_p2=second_proj,
        s_o2=second_out,
        router=router.T,
        expert_up=expert_up,
        expert_down=expert_down,
        first_gain=first_gain,
        first_shift=first_shift,
        first_bias=first_bias,
        dense_gain=dense_gain,
        dense_shift=dense_shift,
        hidden_bias=hidden_bias,
        dense_bias=dense_bias,
        second_gain=second_gain,
        second_shift=second_shift,
        second_bias=second_bias,
        mixture_gain=mixture_gain,
        mixture_shift=mixture_shift,
    )
    parts = run_blocks(bits, arrays)
    R, D = patches_in.shape[1:]
    outs = list(finish(parts, (R, D, expert_up.shape[2])))
    for at in (2, 3, 6, 7, 8, 12, 13, 14, 17, 18, 19):
        outs[at] = outs[at].reshape(-1)
    outs[20] = outs[20].T
    return tuple(outs)


def solution(mesh):
    rows, vec, mat = P(None, "wide", None), P(), P("section", None)
    cube = P("section", None, None)
    in_specs = (
        rows, rows, P(None, "wide"), rows, rows,
        vec, vec, mat, mat, vec,
        vec, vec, mat, vec, mat, vec,
        vec, vec, mat, mat, vec,
        vec, vec, mat, cube, cube,
    )
    cut, moved = P("section"), P("section", "wide", None)
    out_specs = (
        moved, moved,
        cut, cut, mat, mat, cut,
        cut, cut, mat, cut, mat, cut,
        cut, cut, mat, mat, cut,
        cut, cut, mat, cube, cube,
    )
    return jax.shard_map(local, mesh=mesh, in_specs=in_specs, out_specs=out_specs, check_vma=False)
```

```python
import functools

import jax
import jax.numpy as jnp
from jax import lax
from jax.experimental import pallas as pl
from jax.experimental.pallas import tpu as pltpu
from jax.sharding import PartitionSpec as P

HEADS = 6
HEAD_DIM = 64
PATCHES = 196
EXPERTS = 4
TASKS = 2
CAPACITY = 488
EPSILON = 1e-06
MESH = pl.DeviceIdType.MESH
bf16 = jnp.bfloat16
f32 = jnp.float32

RP = 208
SL = 496
VROWS = 32
NSEM = 200


def dot(left, right):
    return jnp.dot(left, right, preferred_element_type=f32)


def nt(left, right):
    return lax.dot_general(left, right, (((1,), (1,)), ((), ())), preferred_element_type=f32)


def tn(left, right):
    return lax.dot_general(left, right, (((0,), (0,)), ((), ())), preferred_element_type=f32)


def iota(shape, dim):
    return lax.broadcasted_iota(jnp.int32, shape, dim)


def onehot(cond):
    return jnp.where(cond, 1.0, 0.0).astype(bf16)


def normed(x):
    centered = x - jnp.mean(x, axis=-1, keepdims=True)
    scale = lax.rsqrt(jnp.mean(centered * centered, axis=-1, keepdims=True) + EPSILON)
    return centered * scale, scale


def norm_back(grad, xhat, scale, gain):
    inner = grad * gain
    mean_inner = jnp.mean(inner, axis=-1, keepdims=True)
    mean_cross = jnp.mean(inner * xhat, axis=-1, keepdims=True)
    return scale * (inner - mean_inner - xhat * mean_cross)


def gelu_both(u):
    cdf = 0.5 * (1.0 + lax.erf(u * 0.7071067811865476))
    return u * cdf, cdf + u * (jnp.exp(u * u * -0.5) * 0.3989422804014327)


def column_sum(v):
    return jnp.sum(v, axis=0, keepdims=True)


V_A1, V_D, V_HB, V_A2, V_M, V_R = 0, 3, 6, 10, 13, 16


class Links:
    def __init__(self, send_sems, recv_sems):
        self.send_sems, self.recv_sems, self.used, self.sent = send_sems, recv_sems, 0, {}

    def take(self, count=1):
        first = self.used
        self.used += count
        return first

    def copy(self, number, src, dst, device):
        return pltpu.make_async_remote_copy(
            src_ref=src,
            dst_ref=dst,
            send_sem=self.send_sems.at[number],
            recv_sem=self.recv_sems.at[number],
            device_id=device,
            device_id_type=MESH,
        )

    def start(self, name, number=None):
        number = self.take() if number is None else number
        self.copy(number, *name()).start()
        self.sent[number] = name
        return number

    def arrived(self, number, there, device):
        self.copy(number, there, there, device).wait_recv()

    def left(self, number):
        self.copy(number, *self.sent.pop(number)()).wait_send()

    def drain(self):
        for number in list(self.sent):
            self.left(number)


def at_steps(hooks, i):
    for step, actions in hooks.items():

        @pl.when(i == step)
        def _():
            for action in actions:
                action()


def block_kernel(bits, r):
    R, D = r.patches.shape[1:]
    FF = r.expert_up.shape[2]
    xraw = r.h3.at[pl.ds(0, R)]
    IMG = R // PATCHES
    RT = IMG * RP
    FC = D
    NF = FF // FC
    NS = 4
    sec = lax.axis_index("section")
    wide = lax.axis_index("wide")
    core = lax.rem(wide, 2)
    chip = wide // 2
    links = Links(r.send, r.recv)

    sec_hi, sec_lo = sec // 2, lax.rem(sec, 2)

    def flip(bit, by):
        return bit + by - 2 * bit * by

    peers = [flip(sec_hi, j // 2) * 2 + flip(sec_lo, j % 2) for j in range(NS)]
    at_section = [(peer, wide) for peer in peers]
    mate = (sec, wide + 1 - 2 * core)
    bit_of = [lax.rem(chip // (1 << b), 2) for b in range(bits)]
    near_bits = min(bits, 2)
    near = 1 << near_bits
    at_near = []
    for k in range(near):
        other = wide
        for b in range(near_bits):
            if k >> b & 1:
                other = other + (1 - 2 * bit_of[b]) * (2 << b)
        at_near.append((sec, other))
    at_chip = [at_near[1 << b] if b < near_bits else (sec, wide + (1 - 2 * bit_of[b]) * (2 << b)) for b in range(bits)]
    near_index = lax.rem(chip, near)
    near_indices = []
    for k in range(near):
        index = 0
        for b in range(near_bits):
            index = index + flip(bit_of[b], k >> b & 1) * (1 << b)
        near_indices.append(index)

    def peer_of(j):
        return flip(sec_hi, j // 2) * 2 + flip(sec_lo, lax.rem(j, 2))

    local = []

    def fetch(src, dst):
        c = pltpu.make_async_copy(src, dst, r.local.at[len(local)])
        c.start()
        local.append(c)
        return c

    small = [fetch(getattr(r, name), getattr(r, "v_" + name)) for name in SMALL_IN]
    fetch_x = fetch(r.patches.at[sec], xraw)
    fetch_c = [fetch(r.cotangent.at[m], r.pool.at[pl.ds(m * R, R)]) for m in range(NS)]

    r.rt[...] = jnp.zeros(r.rt.shape, f32)

    barrier = pltpu.get_barrier_semaphore()
    partners = at_section[1:] + [mate] + at_near[1:] + at_chip[near_bits:]
    for device in partners:
        pl.semaphore_signal(barrier, inc=1, device_id=device, device_id_type=MESH)
    pl.semaphore_wait(barrier, len(partners))

    shards = [
        (r.s_p1, r.w_p1),
        (r.s_o1, r.w_o1),
        (r.s_up, r.w_up),
        (r.s_dn, r.w_dn),
        (r.s_p2, r.w_p2),
        (r.s_o2, r.w_o2),
    ]
    SPREAD = 3
    direct, passed, spread = {}, {}, {}

    def piece(t, j, c, part=None):
        n = shards[t][0].shape[0]
        h = n // 2
        at, rows = peers[j] * n + c * h, h
        if part is not None:
            rows = h // near
            at = at + part * rows
        return shards[t][1].at[pl.ds(pl.multiple_of(at, 16), rows)]

    def own(t, part=None):
        n = shards[t][0].shape[0]
        at, rows = core * (n // 2), n // 2
        if part is not None:
            rows = rows // near
            at = at + part * rows
        return shards[t][0].at[pl.ds(pl.multiple_of(at, 16), rows)]

    for t in (SPREAD, 0, 1, 2, 4, 5):
        part = near_index if t == SPREAD else None
        for j in range(1, NS):
            direct[t, j] = links.start(
                lambda t=t, j=j, part=part: (own(t, part), piece(t, 0, core, part), at_section[j])
            )
    fetch_w = []
    for shard, whole in shards:
        n = shard.shape[0]
        fetch_w.append(fetch(shard, whole.at[pl.ds(pl.multiple_of(sec * n, n), n)]))
    fetch_e = []
    for f in range(NF):
        cols = pl.ds(f * FC, FC)
        fetch_e.append(fetch(r.expert_up.at[0, :, cols], r.up.at[f]))
        fetch_e.append(fetch(r.expert_down.at[0, cols], r.down.at[f]))

    def spread_on():
        for j in range(1, NS):
            links.arrived(direct[SPREAD, j], piece(SPREAD, j, core, near_index), at_section[j])
            for k in range(1, near):
                spread[j, k] = links.start(
                    lambda j=j, k=k: (piece(SPREAD, j, core, near_index), piece(SPREAD, j, core, near_index), at_near[k])
                )

    def pass_on(*group):
        for t in group:
            for j in range(1, NS):
                if t == SPREAD:
                    for k in range(1, near):
                        links.arrived(spread[j, k], piece(t, j, core, near_indices[k]), at_near[k])
                else:
                    links.arrived(direct[t, j], piece(t, j, core), at_section[j])
                passed[t, j] = links.start(lambda t=t, j=j: (piece(t, j, core), piece(t, j, core), mate))

    def landed(*group):
        for t in group:
            fetch_w[t].wait()
            for j in range(1, NS):
                links.arrived(passed[t, j], piece(t, j, 1 - core), mate)

    for c in small:
        c.wait()
    q = D // NS
    r.rt[sec, 0 : TASKS * EXPERTS, 0:q] = r.v_router[...].astype(f32)
    router_numbers = {}
    for j in range(1, NS):
        router_numbers[j] = links.start(
            lambda j=j: (
                r.rt.at[sec, pl.ds(0, TASKS * EXPERTS)],
                r.rt.at[sec, pl.ds(0, TASKS * EXPERTS)],
                at_section[j],
            )
        )
    vec = Bag()
    for k, name in enumerate(VECTORS):
        line = getattr(r, "v_" + name)
        r.lines[k : k + 1, 0 : line.shape[0]] = line[...].reshape(1, -1)
        setattr(vec, name, r.lines.at[pl.ds(k, 1), pl.ds(0, line.shape[0])])

    def chosen_rows(m_is, expert):
        r0 = jnp.zeros((1, R), jnp.int32)
        r1, k0, k1 = r0, r0, r0
        for m in range(NS):
            mine = jnp.where(m_is == m, 1, 0)
            r0 = r0 + mine * r.v_routes[m, 0:1, :]
            r1 = r1 + mine * r.v_routes[m, 1:2, :]
            k0 = k0 + mine * r.v_keep[m, 0:1, :]
            k1 = k1 + mine * r.v_keep[m, 1:2, :]
        return jnp.where(((r0 == expert) & (k0 == 1)) | ((r1 == expert) & (k1 == 1)), 1.0, 0.0)

    r.chosen[...] = jnp.zeros(r.chosen.shape, f32)
    for j in range(NS):
        r.chosen[j : j + 1, :] = chosen_rows(sec, peers[j])
        r.chosen[4 + j : 5 + j, :] = chosen_rows(peers[j], sec)

    def slots_of(limit, valid):
        chosen = r.chosen[...].astype(bf16)
        column = iota((limit.shape[0], R), 1)
        before = nt(onehot(column < limit), chosen)
        upto = nt(onehot((column <= limit) & valid), chosen)
        return jnp.where(upto > before, before, -1.0)

    def slots_padded(i, carry):
        off = iota((RP, 1), 0)
        r.pos_pad[pl.ds(pl.multiple_of(i * RP, RP), RP), :] = slots_of(i * PATCHES + off, off < PATCHES)
        return carry

    lax.fori_loop(0, IMG, slots_padded, 0)
    RC = R // 7

    def slots_raw(i, carry):
        off = iota((RC, 1), 0)
        r.q8[pl.ds(pl.multiple_of(i * RC, RC), RC), 0:16] = slots_of(i * RC + off, off >= 0)
        return carry

    lax.fori_loop(0, 7, slots_raw, 0)

    fetch_x.wait()
    for c in fetch_c:
        c.wait()
    for i in range(IMG):
        start = (PATCHES * i) // 16 * 16
        gap = PATCHES * i - start
        a, b = iota((RP, RP), 0), iota((RP, RP), 1)
        shift = onehot((b == a + gap) & (a < PATCHES))
        r.h0[i * RP : (i + 1) * RP, :] = dot(shift, xraw[start : start + RP, :]).astype(bf16)
        first = pl.multiple_of(sec * R + start, 16)
        r.g3[i * RP : (i + 1) * RP, :] = dot(shift, r.pool[pl.ds(first, RP), :]).astype(bf16)

    spread_on()

    slot_lane = iota((1, SL), 1).astype(f32)
    for j in range(NS):
        pick = onehot(r.q8[0:R, 4 + j : 5 + j] == slot_lane)
        first = pl.multiple_of(peers[j] * R, 16)
        r.gslot[j] = tn(pick, r.pool[pl.ds(first, R), :]).astype(bf16)
        row = iota((R, 128), 0)
        task = jnp.zeros((R, 128), jnp.int32)
        for i in range(IMG):
            task = jnp.where((row >= i * PATCHES) & (row < (i + 1) * PATCHES), r.v_task[peers[j], i], task)
        task = tn(pick, task.astype(f32).astype(bf16))
        r.tslot[...] = task if j == 0 else jnp.where(iota((SL, 128), 1) == j, task, r.tslot[...])

    low_half = iota((1, 128), 1) < 64
    half_masks = [onehot(low_half), onehot(jnp.logical_not(low_half))]
    low_half_rows = iota((RP, 128), 1) < 64
    key_ok = iota((RP, RP), 0) < PATCHES

    def attend(h_in, h_out, vecs, w_p, w_o, qkv_s, p_s, ctx_s, hooks):
        gain, shift, bias = vecs

        def image(i, carry):
            rows = pl.ds(pl.multiple_of(i * RP, RP), RP)
            x = h_in[rows, :].astype(f32)
            a = (normed(x)[0] * gain[...] + shift[...]).astype(bf16)
            qkv = dot(a, w_p[...]).astype(bf16)
            qkv_s[rows, :] = qkv
            parts = []
            for pair in range(HEADS // 2):
                at = 128 * pair
                q2 = qkv[:, at : at + 128]
                k2 = qkv[:, D + at : D + at + 128]
                v2 = qkv[:, 2 * D + at : 2 * D + at + 128]
                outs = []
                for half in range(2):
                    scores = nt(k2 * half_masks[half], q2)
                    scores = jnp.where(key_ok, scores, -1e30)
                    top = jnp.max(scores, axis=0, keepdims=True)
                    e = jnp.exp((scores - top) * HEAD_DIM**-0.5)
                    p = (e * (1.0 / jnp.sum(e, axis=0, keepdims=True))).astype(bf16)
                    p_s[i * HEADS + 2 * pair + half] = p
                    outs.append(tn(p, v2))
                parts.append(jnp.where(low_half_rows, outs[0], outs[1]).astype(bf16))
            ctx = jnp.concatenate(parts, axis=1)
            ctx_s[rows, :] = ctx
            h_out[rows, :] = (x + dot(ctx, w_o[...]) + bias[...]).astype(bf16)
            at_steps(hooks, i)
            return carry

        lax.fori_loop(0, IMG, image, 0)

    def attend_back(h_in, g_in, g_out, vecs, w_p, w_o, qkv_s, p_s, vrow, hooks, values_done=False):
        gain, shift, _ = vecs

        def image(i, carry):
            rows = pl.ds(pl.multiple_of(i * RP, RP), RP)
            g = g_in[rows, :]
            gf = g.astype(f32)
            xhat, scale = normed(h_in[rows, :].astype(f32))
            if values_done:
                gc = r.z[rows, D : 2 * D]
            else:
                r.a_s[rows, :] = (xhat * gain[...] + shift[...]).astype(bf16)
                gc = nt(g, w_o[...]).astype(bf16)
            qkv = qkv_s[rows, :]
            gq, gk, gv = [], [], []
            for pair in range(HEADS // 2):
                at = 128 * pair
                q2 = qkv[:, at : at + 128]
                k2 = qkv[:, D + at : D + at + 128]
                v2 = qkv[:, 2 * D + at : 2 * D + at + 128]
                gc2 = gc[:, at : at + 128]
                two = []
                for half in range(2):
                    p = p_s[i * HEADS + 2 * pair + half]
                    pf = p.astype(f32)
                    gp = nt(v2 * half_masks[half], gc2)
                    t = pf * gp
                    gs = (t - pf * jnp.sum(t, axis=0, keepdims=True)).astype(bf16)
                    two.append((tn(gs, k2), dot(gs, q2), None if values_done else dot(p, gc2)))
                gq.append((jnp.where(low_half_rows, two[0][0], two[1][0]) * HEAD_DIM**-0.5).astype(bf16))
                gk.append((jnp.where(low_half_rows, two[0][1], two[1][1]) * HEAD_DIM**-0.5).astype(bf16))
                if not values_done:
                    gv.append(jnp.where(low_half_rows, two[0][2], two[1][2]).astype(bf16))
            if values_done:
                gv = [r.z[rows, 0:D]]
            gqkv = jnp.concatenate(gq + gk + gv, axis=1)
            qkv_s[rows, :] = gqkv
            ga = nt(gqkv, w_p[...])
            r.vec[vrow : vrow + 1, :] += column_sum(ga * xhat)
            r.vec[vrow + 1 : vrow + 2, :] += column_sum(ga)
            r.vec[vrow + 2 : vrow + 3, :] += column_sum(gf)
            g_out[rows, :] = (gf + norm_back(ga, xhat, scale, gain[...])).astype(bf16)
            at_steps(hooks, i)
            return carry

        lax.fori_loop(0, IMG, image, 0)

    def values_back(h_in, g_in, vecs, w_o, p_s, hooks):
        gain, shift, _ = vecs

        def image(i, carry):
            rows = pl.ds(pl.multiple_of(i * RP, RP), RP)
            xhat, _ = normed(h_in[rows, :].astype(f32))
            r.a_s[rows, :] = (xhat * gain[...] + shift[...]).astype(bf16)
            gc = nt(g_in[rows, :], w_o[...]).astype(bf16)
            r.z[rows, D : 2 * D] = gc
            for pair in range(HEADS // 2):
                at = 128 * pair
                two = [dot(p_s[i * HEADS + 2 * pair + half], gc[:, at : at + 128]) for half in range(2)]
                r.z[rows, at : at + 128] = jnp.where(low_half_rows, two[0], two[1]).astype(bf16)
            at_steps(hooks, i)
            return carry

        lax.fori_loop(0, IMG, image, 0)

    r.vec[...] = jnp.zeros(r.vec.shape, f32)
    att1 = (vec.first_gain, vec.first_shift, vec.first_bias)
    att2 = (vec.second_gain, vec.second_shift, vec.second_bias)

    pass_on(0, 1)
    landed(0, 1)
    attend(r.h0, r.h1, att1, r.w_p1, r.w_o1, r.qkv1, r.p1, r.ctx1, {IMG - 1: [lambda: pass_on(3, 2)]})
    landed(3, 2)
    HR = RT // 2

    def dense_step(i, carry):
        rows = pl.ds(pl.multiple_of(i * HR, HR), HR)
        x = r.h1[rows, :].astype(f32)
        a = (normed(x)[0] * vec.dense_gain[...] + vec.dense_shift[...]).astype(bf16)
        total = x + vec.dense_bias[...]
        for f in range(NF):
            cols = slice(f * FC, (f + 1) * FC)
            u = dot(a, r.w_up[:, cols]) + vec.hidden_bias[:, cols]
            z, slope = gelu_both(u)
            z = z.astype(bf16)
            r.z[rows, cols] = z
            r.slope[rows, cols] = slope.astype(bf16)
            total = total + dot(z, r.w_dn[cols, :])
        r.h2[rows, :] = total.astype(bf16)
        at_steps({1: [lambda: pass_on(4, 5)]}, i)
        return carry

    lax.fori_loop(0, 2, dense_step, 0)
    landed(4, 5)
    attend(r.h2, r.h3, att2, r.w_p2, r.w_o2, r.qkv2, r.p2, r.ctx2, {})

    for j in range(1, NS):
        links.arrived(router_numbers[j], r.rt.at[peers[j], pl.ds(0, TASKS * EXPERTS)], at_section[j])
    for p in range(NS):
        r.w_rt[p * q : (p + 1) * q, :] = r.rt[p].T[0:q, :].astype(bf16)
    lane = iota((1, 128), 1)

    def gates_of(a, task):
        logits = dot(a, r.w_rt[...])
        active = (lane < TASKS * EXPERTS) & (lane // EXPERTS == task)
        top = jnp.max(jnp.where(active, logits, -1e30), axis=-1, keepdims=True)
        e = jnp.where(active, jnp.exp(jnp.minimum(logits - top, 0.0)), 0.0)
        return e / jnp.sum(e, axis=-1, keepdims=True)

    def mix_rows(i, carry):
        rows = pl.ds(pl.multiple_of(i * RP, RP), RP)
        a = (normed(r.h3[rows, :].astype(f32))[0] * vec.mixture_gain[...] + vec.mixture_shift[...]).astype(bf16)
        r.a_s[rows, :] = a
        return carry

    lax.fori_loop(0, IMG, mix_rows, 0)

    slots_first = links.take(NS)
    for j in (1, 2, 3, 0):
        pick = onehot(r.pos_pad[:, j : j + 1] == slot_lane)
        r.slot_out[j] = tn(pick, r.a_s[...]).astype(bf16)
        if j > 0:
            links.start(lambda j=j: (r.slot_out.at[j], r.slot_in.at[j - 1], at_section[j]), slots_first + j)

    for c in fetch_e:
        c.wait()
    r.eg[...] = jnp.zeros(r.eg.shape, f32)
    ga_first, q_first, w_first = links.take(NS), links.take(NS), links.take(NS)

    def ga_in(j):
        return r.pool.at[pl.ds((j - 1) * SL, SL)]

    def w_in(j):
        return r.pool.at[pl.ds((j + 2) * SL, SL)]

    e_parts = []
    for k in range(2):
        order = list(range(bits))
        if k == 1 and bits > 1:
            order[:2] = [1, 0]
        first = bit_of[order[0]] if bits > 0 else 0
        second = bit_of[order[1]] if bits > 1 else 0
        e_parts.append(
            Bag(k=k, order=order, keep=2 * k + first, send=2 * k + 1 - first, near=second, far=1 - second)
        )
    half_rows = FC // 2
    for part in e_parts if bits > 1 else ():
        part.near_rows = pl.ds(pl.multiple_of(part.near * half_rows, half_rows), half_rows)
        part.far_rows = pl.ds(pl.multiple_of(part.far * half_rows, half_rows), half_rows)

    def expert_step(j, last, own=False):
        a = r.slot_out[0] if own else r.slot_in[j - 1]
        gs = r.gslot[j]
        gates = gates_of(a, jnp.sum(jnp.where(lane == j, r.tslot[...], 0.0), axis=-1, keepdims=True).astype(jnp.int32))
        combine = jnp.sum(jnp.where(lax.rem(lane, EXPERTS) == sec, gates, 0.0), axis=-1, keepdims=True)
        gout = (combine * gs.astype(f32)).astype(bf16)
        for part in e_parts:
            f = part.keep if last else part.send
            z, slope = gelu_both(dot(a, r.up[f]))
            z = z.astype(bf16)
            out = dot(z, r.down[f])
            gv = (nt(gout, r.down[f]) * slope).astype(bf16)
            ga = nt(gv, r.up[f])
            if part.k == 0 and not last:
                r.acc[0:SL, :] = out
                r.acc[SL : 2 * SL, :] = ga
            elif part.k == 0 and not own:
                r.acc[0:SL, :] = out + r.out_half[j - 1].astype(f32)
                r.acc[SL : 2 * SL, :] = ga + r.slot_out[j].astype(f32)
            else:
                r.acc[0:SL, :] += out
                r.acc[SL : 2 * SL, :] += ga
            r.eg[0, f] += tn(a, gv)
            r.eg[1, f] += tn(z, gout)
        if own and not last:
            return
        r.slot_out[j] = r.acc[SL : 2 * SL, :].astype(bf16)
        if not last:
            r.out_half[j - 1] = r.acc[0:SL, :].astype(bf16)
            return
        weighted = combine * r.acc[0:SL, :].astype(bf16).astype(f32)
        q = jnp.sum(gs.astype(f32) * weighted, axis=-1, keepdims=True)
        q_hi = q.astype(bf16).astype(f32)
        lanes = iota((SL, 128), 1)
        q2 = jnp.where(lanes == 0, q_hi, jnp.where(lanes == 1, q - q_hi, 0.0))
        r.q_out[j] = q2.T[0:16, :].astype(bf16)
        r.gslot[j] = weighted.astype(bf16)

    e_numbers = {}

    def e_core_start(last):
        for part in e_parts:
            block = part.keep if last else part.send
            staged = (lambda k=part.k: r.up.at[k]) if last else (lambda k=part.k: r.g0.at[pl.ds(k * D, D)])
            staged()[...] = r.eg[1 - core, block].astype(bf16)
            e_numbers["core", part.k, last] = links.start(
                lambda staged=staged, block=block: (staged(), r.e_sum.at[block], mate)
            )

    def e_core_end(last):
        for part in e_parts:
            block = part.keep if last else part.send
            links.arrived(e_numbers["core", part.k, last], r.e_sum.at[block], mate)
            if not last:
                links.left(e_numbers["core", part.k, last])
            total = r.eg[core, block] + r.e_sum[block].astype(f32)
            if last and bits > 0:
                links.arrived(e_numbers["block", part.k], r.e_land.at[part.k], at_chip[part.order[0]])
                total = total + r.e_land[part.k].astype(f32)
            r.e_sum[block] = total.astype(bf16)

    def e_blocks_start():
        if bits > 0:
            for part in e_parts:
                e_numbers["block", part.k] = links.start(
                    lambda part=part: (r.e_sum.at[part.send], r.e_land.at[part.k], at_chip[part.order[0]])
                )

    def e_step_start(step):
        for part in e_parts:
            which = part.far_rows if step == 1 else part.near_rows
            e_numbers["step", step, part.k] = links.start(
                lambda part=part, which=which: (
                    r.e_sum.at[part.keep, which],
                    r.e_land2.at[step - 1, part.k],
                    at_chip[part.order[step]],
                )
            )

    def e_step_end(step):
        for part in e_parts:
            number = e_numbers["step", step, part.k]
            links.arrived(number, r.e_land2.at[step - 1, part.k], at_chip[part.order[step]])
            if step > 1:
                links.left(number)
            rows = part.near_rows
            mine = r.e_sum[part.keep, rows, :].astype(f32)
            r.e_sum[part.keep, rows, :] = (mine + r.e_land2[step - 1, part.k].astype(f32)).astype(bf16)

    def e_own():
        for part in e_parts:
            if bits > 1:
                rows = part.near_rows
                r.e_all[part.keep, rows, :] = r.e_sum[part.keep, rows, :]
            else:
                r.e_all[part.keep] = r.e_sum[part.keep]
            if bits == 0:
                r.e_all[part.send] = r.e_sum[part.send]

    def e_spread_start(step):
        if bits > step:
            for part in e_parts:
                where = (part.keep, part.near_rows) if step == 1 else (part.keep,)
                e_numbers["up", step, part.k] = links.start(
                    lambda part=part, where=where: (
                        r.e_all.at[where],
                        r.e_all.at[where],
                        at_chip[part.order[step]],
                    )
                )

    def e_spread_end(step):
        if bits > step:
            for part in e_parts:
                where = (part.keep, part.far_rows) if step == 1 else (part.send,)
                links.arrived(e_numbers["up", step, part.k], r.e_all.at[where], at_chip[part.order[step]])

    def e_pair_start():
        e_numbers["pair"] = links.start(lambda: (r.e_all, r.down, mate))

    def e_pair_end():
        links.arrived(e_numbers["pair"], r.down, mate)

    def answer(j):
        links.copy(ga_first + j, r.slot_out.at[j], ga_in(j), (peer_of(j), wide)).start()
        links.copy(q_first + j, r.q_out.at[j], r.q_in.at[j], (peer_of(j), wide)).start()

    expert_step(0, False, True)
    expert_step(0, True, True)

    def others_first(j, carry):
        links.copy(slots_first + j, r.slot_out.at[j], r.slot_in.at[j - 1], (peer_of(j), wide)).wait()
        expert_step(j, False)
        return carry

    lax.fori_loop(1, NS, others_first, 0)
    e_core_start(False)

    def others_last(j, carry):
        expert_step(j, True)
        answer(j)
        at_steps({1: [lambda: e_core_end(False), e_blocks_start]}, j)
        return carry

    lax.fori_loop(1, NS, others_last, 0)

    for j in range(1, NS):
        links.sent.pop(slots_first + j)

    def grads_back(j):
        links.copy(ga_first + j, r.slot_out.at[j], ga_in(j), at_section[j]).wait()
        links.copy(q_first + j, r.q_out.at[j], r.q_in.at[j], at_section[j]).wait()

    e_core_start(True)
    for j in range(1, NS):
        links.start(lambda j=j: (r.gslot.at[j], w_in(j), at_section[j]), w_first + j)

    class Summed:
        def __init__(self, buffers):
            self.b = buffers
            self.numbers = {}

        def cut(self, k):
            rows, cols = self.b.pair.shape[1:]
            if self.b.by_rows:
                return pl.ds(k * (rows // 2), rows // 2), pl.ds(0, cols)
            return pl.ds(0, rows), pl.ds(k * (cols // 2), cols // 2)

        def send_core(self, halves=(0, 1)):
            b = self.b
            for k in halves:
                self.numbers["core", k] = links.start(
                    lambda k=k: (b.full.at[(pl.ds(0, NS), 1 - core) + self.cut(k)], b.pair.at[(pl.ds(0, NS),) + self.cut(k)], mate)
                )

        def send_section(self, halves=(0, 1)):
            b = self.b
            for k in halves:
                links.arrived(self.numbers["core", k], b.pair.at[(pl.ds(0, NS),) + self.cut(k)], mate)
                links.left(self.numbers["core", k])
                for p in range(NS):
                    mine = b.full[(p, core) + self.cut(k)].astype(f32)
                    b.pair[(p,) + self.cut(k)] = (mine + b.pair[(p,) + self.cut(k)].astype(f32)).astype(bf16)
                for j in range(1, NS):
                    self.numbers["section", k, j] = links.start(
                        lambda k=k, j=j: (b.pair.at[(peers[j],) + self.cut(k)], b.sec.at[(j - 1,) + self.cut(k)], at_section[j])
                    )

        def section_sum(self, halves=(0, 1)):
            b = self.b
            for k in halves:
                total = b.pair[(sec,) + self.cut(k)].astype(f32)
                for j in range(1, NS):
                    there = (j - 1,) + self.cut(k)
                    links.arrived(self.numbers["section", k, j], b.sec.at[there], at_section[j])
                    total = total + b.sec[there].astype(f32)
                b.fin[core, k] = total.astype(bf16)

        def chip_start(self, step, halves=(0, 1)):
            for k in halves:
                bit = step if k == 0 else bits - 1 - step
                self.numbers["chip", k] = links.start(
                    lambda k=k, bit=bit: (self.b.fin.at[core, k], self.b.land.at[step, k], at_chip[bit])
                )

        def chip_end(self, step, halves=(0, 1)):
            for k in halves:
                bit = step if k == 0 else bits - 1 - step
                number = self.numbers["chip", k]
                links.arrived(number, self.b.land.at[step, k], at_chip[bit])
                links.left(number)
                mine = self.b.fin[core, k].astype(f32)
                self.b.fin[core, k] = (mine + self.b.land[step, k].astype(f32)).astype(bf16)

        def pair_start(self, halves=(0, 1)):
            for k in halves:
                self.numbers["pair", k] = links.start(lambda k=k: (self.b.fin.at[core, k], self.b.fin.at[core, k], mate))

        def pair_end(self, halves=(0, 1)):
            for k in halves:
                links.arrived(self.numbers["pair", k], self.b.fin.at[1 - core, k], mate)

    def by_section_rows(full, cols, value):
        n = D // NS // 2
        for p in range(NS):
            for c in range(2):
                full[p, c, :, cols] = value[(2 * p + c) * n : (2 * p + c + 1) * n, :].astype(bf16)

    sum_a2, sum_du, sum_dd, sum_a1 = (Summed(b) for b in (r.t_a2, r.t_du, r.t_dd, r.t_a1))
    out_copies = []

    def send_out(src, dst):
        c = pltpu.make_async_copy(src, dst, r.out_sems.at[len(out_copies)])
        c.start()
        out_copies.append(c)

    def mix_gather(experts, first):
        def step(i, carry):
            rows = pl.ds(pl.multiple_of(i * RP, RP), RP)
            task = jnp.zeros((RP, 1), jnp.int32) + r.v_task[sec, i]
            active = (lane < TASKS * EXPERTS) & (lane // EXPERTS == task)
            ga = jnp.zeros((RP, D), f32) if first else r.acc[rows, :]
            q8 = jnp.zeros((RP, 128), f32) if first else r.q8[rows, :]
            for j in experts:
                pick = onehot(r.pos_pad[rows, j : j + 1] == slot_lane)
                ga = ga + dot(pick, r.slot_out[0] if j == 0 else ga_in(j)[...])
                one = jnp.sum(nt(pick, r.q_out[0] if j == 0 else r.q_in[j]), axis=-1, keepdims=True)
                q8 = q8 + jnp.where(active & (lax.rem(lane, EXPERTS) == peers[j]), one, 0.0)
            if first:
                r.acc[rows, :] = ga
                r.q8[rows, :] = q8
                return carry
            a = r.a_s[rows, :]
            gl = (q8 - gates_of(a, task) * jnp.sum(q8, axis=-1, keepdims=True)).astype(bf16)
            ga = ga + nt(gl, r.w_rt[...])
            r.vec[V_R : V_R + 8, :] += tn(gl, a)[0:8, :]
            xhat, scale = normed(r.h3[rows, :].astype(f32))
            r.vec[V_M : V_M + 1, :] += column_sum(ga * xhat)
            r.vec[V_M + 1 : V_M + 2, :] += column_sum(ga)
            g = r.g3[rows, :].astype(f32)
            r.g2[rows, :] = (g + norm_back(ga, xhat, scale, vec.mixture_gain[...])).astype(bf16)
            return carry

        lax.fori_loop(0, IMG, step, 0)

    grads_back(1)
    grads_back(2)
    mix_gather((0, 1, 2), True)
    e_core_end(True)
    if bits > 1:
        e_step_start(1)
    grads_back(3)
    mix_gather((3,), False)

    def e_third():
        for step in range(1, bits):
            if step > 1:
                e_step_start(step)
            e_step_end(step)
        e_own()
        e_spread_start(1)

    def e_fourth():
        e_spread_end(1)
        e_spread_start(0)

    def e_fifth():
        e_spread_end(0)
        e_pair_start()

    attend_back(
        r.h2, r.g2, r.g1, att2, r.w_p2, r.w_o2, r.qkv2, r.p2, V_A2, {1: [e_third]}
    )
    for f in range(3):
        cols = slice(f * D, (f + 1) * D)
        by_section_rows(r.t_a2.full, cols, tn(r.a_s[...], r.qkv2[:, cols]))
    by_section_rows(r.t_a2.full, slice(3 * D, 4 * D), tn(r.ctx2[...], r.g2[...]))
    sum_a2.send_core()

    def dense_back(i, carry):
        rows = pl.ds(pl.multiple_of(i * HR, HR), HR)
        g = r.g1[rows, :]
        gf = g.astype(f32)
        xhat, scale = normed(r.h1[rows, :].astype(f32))
        r.a_s[rows, :] = (xhat * vec.dense_gain[...] + vec.dense_shift[...]).astype(bf16)
        ga = jnp.zeros((HR, D), f32)
        for f in range(NF):
            cols = slice(f * FC, (f + 1) * FC)
            gu = (nt(g, r.w_dn[cols, :]) * r.slope[rows, cols].astype(f32)).astype(bf16)
            r.slope[rows, cols] = gu
            r.vec[V_HB + f : V_HB + f + 1, :] += column_sum(gu.astype(f32))
            ga = ga + nt(gu, r.w_up[:, cols])
        r.vec[V_D : V_D + 1, :] += column_sum(ga * xhat)
        r.vec[V_D + 1 : V_D + 2, :] += column_sum(ga)
        r.vec[V_D + 2 : V_D + 3, :] += column_sum(gf)
        r.g0[rows, :] = (gf + norm_back(ga, xhat, scale, vec.dense_gain[...])).astype(bf16)
        at_steps({0: [sum_a2.send_section, e_fourth]}, i)
        return carry

    lax.fori_loop(0, 2, dense_back, 0)

    for f in range(NF):
        cols = slice(f * FC, (f + 1) * FC)
        by_section_rows(r.t_du.full, cols, tn(r.a_s[...], r.slope[:, cols]))
    sum_du.send_core()
    for f in range(NF):
        value = tn(r.z[:, f * FC : (f + 1) * FC], r.g1[...])
        n = FC // 2
        for c in range(2):
            r.t_dd.full[f, c] = value[c * n : (c + 1) * n, :].astype(bf16)
    sum_dd.send_core()
    sum_du.send_section()

    def chips_first(one, halves=(0, 1)):
        one.section_sum(halves)
        if bits > 0:
            one.chip_start(0, halves)

    def chips_rest(one, halves=(0, 1)):
        for step in range(1, bits):
            one.chip_end(step - 1, halves)
            one.chip_start(step, halves)

    def chips_last(one, halves=(0, 1)):
        if bits > 0:
            one.chip_end(bits - 1, halves)
        one.pair_start(halves)

    a1 = r.t_a1.full
    by_section_rows(a1, slice(3 * D, 4 * D), tn(r.ctx1[...], r.g0[...]))
    values_back(r.h0, r.g0, att1, r.w_o1, r.p1, {1: [sum_dd.send_section]})
    by_section_rows(a1, slice(2 * D, 3 * D), tn(r.a_s[...], r.z[:, 0:D]))
    sum_a1.send_core((1,))
    chips_first(sum_a2)
    attend_back(
        r.h0, r.g0, r.g3, att1, r.w_p1, r.w_o1, r.qkv1, r.p1, V_A1,
        {
            0: [lambda: sum_a1.send_section((1,))],
            2: [lambda: chips_rest(sum_a2), lambda: chips_first(sum_du)],
        },
        True,
    )
    for f in range(2):
        cols = slice(f * D, (f + 1) * D)
        by_section_rows(a1, cols, tn(r.a_s[...], r.qkv1[:, cols]))
    sum_a1.send_core((0,))
    send_out(r.g3, r.o_grad)

    def vec_start(land, device):
        return links.start(lambda: (r.vec, r.vec_land.at[land], device)), land, device

    def vec_end(number, land, device):
        links.arrived(number, r.vec_land.at[land], device)
        links.left(number)

    vec_core = vec_start(0, mate)
    chips_last(sum_a2)
    for j in range(1, NS):
        links.arrived(w_first + j, w_in(j), at_section[j])
    vec_section = []

    def vec_two():
        vec_end(*vec_core)
        r.vec[...] += r.vec_land[0]
        vec_section.extend(vec_start(j, at_section[j]) for j in range(1, NS))

    def block_out(i, carry):
        rows = pl.ds(pl.multiple_of(i * RP, RP), RP)
        total = r.h3[rows, :].astype(f32)
        for j in range(NS):
            pick = onehot(r.pos_pad[rows, j : j + 1] == slot_lane)
            total = total + dot(pick, r.gslot[0] if j == 0 else w_in(j)[...])
        r.h3[rows, :] = total.astype(bf16)
        at_steps({1: [lambda: sum_a1.send_section((0,)), vec_two, lambda: chips_rest(sum_du)]}, i)
        return carry

    lax.fori_loop(0, IMG, block_out, 0)
    send_out(r.h3, r.o_block)
    chips_first(sum_dd)
    chips_first(sum_a1, (1,))
    for one in vec_section:
        vec_end(*one)
    r.vec[...] += r.vec_land[1] + r.vec_land[2] + r.vec_land[3]
    vec_chip = vec_start(NS, at_chip[0]) if bits > 0 else None
    chips_last(sum_du)
    chips_first(sum_a1, (0,))
    e_fifth()
    chips_rest(sum_dd)
    for step in range(1, bits):
        for k in (1, 0):
            sum_a1.chip_end(step - 1, (k,))
            sum_a1.chip_start(step, (k,))
        vec_end(*vec_chip)
        r.vec[...] += r.vec_land[NS + step - 1]
        vec_chip = vec_start(NS + step, at_chip[step])
    chips_last(sum_dd)
    e_pair_end()
    send_out(r.e_all, r.o_expert.at[core])
    send_out(r.down, r.o_expert.at[1 - core])
    for s, dst in ((sum_a2, r.o_a2), (sum_du, r.o_du), (sum_dd, r.o_dd)):
        s.pair_end()
        send_out(s.b.fin, dst)
    for k in (1, 0):
        chips_last(sum_a1, (k,))
    if bits > 0:
        vec_end(*vec_chip)
        r.vec[...] += r.vec_land[NS + bits - 1]
    send_out(r.vec, r.o_vec)
    sum_a1.pair_end()
    send_out(r.t_a1.fin, r.o_a1)
    links.drain()
    for c in out_copies:
        c.wait()
    assert links.used <= NSEM and len(local) <= 40 and len(out_copies) <= 12, links.used


class Bag:
    def __init__(self, **members):
        self.__dict__.update(members)


VECTORS = (
    "first_gain",
    "first_shift",
    "first_bias",
    "dense_gain",
    "dense_shift",
    "hidden_bias",
    "dense_bias",
    "second_gain",
    "second_shift",
    "second_bias",
    "mixture_gain",
    "mixture_shift",
)
SMALL_IN = ("task", "routes", "keep", "router") + VECTORS


def run_blocks(bits, arrays):
    R, D = arrays["patches"].shape[1:]
    FF = arrays["expert_up"].shape[2]
    IMG = R // PATCHES
    RT = IMG * RP
    n = D // 8
    vm = pltpu.VMEM
    scratch = dict(
        pool=vm((max(4 * R, 6 * SL), D), bf16),
        chosen=vm((16, R), f32),
        pos_pad=vm((RT, 16), f32),
        w_p1=vm((D, 3 * D), bf16),
        w_o1=vm((D, D), bf16),
        w_up=vm((D, FF), bf16),
        w_dn=vm((FF, D), bf16),
        w_p2=vm((D, 3 * D), bf16),
        w_o2=vm((D, D), bf16),
        w_rt=vm((D, 128), bf16),
        rt=vm((4, 128, 128), f32),
        lines=vm((16, FF), f32),
        up=vm((FF // D, D, D), bf16),
        down=vm((FF // D, D, D), bf16),
        out_half=vm((3, SL, D), bf16),
        h0=vm((RT, D), bf16),
        h1=vm((RT, D), bf16),
        h2=vm((RT, D), bf16),
        h3=vm((RT, D), bf16),
        g0=vm((RT, D), bf16),
        g1=vm((RT, D), bf16),
        g2=vm((RT, D), bf16),
        g3=vm((RT, D), bf16),
        a_s=vm((RT, D), bf16),
        qkv1=vm((RT, 3 * D), bf16),
        qkv2=vm((RT, 3 * D), bf16),
        p1=vm((IMG * HEADS, RP, RP), bf16),
        p2=vm((IMG * HEADS, RP, RP), bf16),
        ctx1=vm((RT, D), bf16),
        ctx2=vm((RT, D), bf16),
        z=vm((RT, FF), bf16),
        slope=vm((RT, FF), bf16),
        slot_out=vm((4, SL, D), bf16),
        slot_in=vm((3, SL, D), bf16),
        gslot=vm((4, SL, D), bf16),
        tslot=vm((SL, 128), f32),
        q_out=vm((4, 16, SL), bf16),
        q_in=vm((4, 16, SL), bf16),
        acc=vm((2 * SL, D), f32),
        q8=vm((RT, 128), f32),
        eg=vm((2, 4, D, D), f32),
        e_sum=vm((4, D, D), bf16),
        e_land=vm((2, D, D), bf16),
        e_land2=vm((max(bits - 1, 1), 2, D // 2, D), bf16),
        e_all=vm((4, D, D), bf16),
        vec=vm((VROWS, D), f32),
        vec_land=vm((4 + max(bits, 1), VROWS, D), f32),
        send=pltpu.SemaphoreType.DMA((NSEM,)),
        recv=pltpu.SemaphoreType.DMA((NSEM,)),
        local=pltpu.SemaphoreType.DMA((40,)),
        out_sems=pltpu.SemaphoreType.DMA((12,)),
    )
    for name in SMALL_IN:
        space = pltpu.SMEM if name == "task" else vm
        scratch["v_" + name] = space(arrays[name].shape, arrays[name].dtype)
    sums = dict(t_a2=False, t_du=False, t_dd=True, t_a1=False)
    fin = {}
    for name, by_rows in sums.items():
        rows, cols = (D // 2, D) if by_rows else (n, FF)
        halved = (rows // 2, cols) if by_rows else (rows, cols // 2)
        if name in ("t_a2", "t_dd"):
            scratch[name + ".full"] = vm((4, 2, rows, cols), bf16)
        scratch[name + ".pair"] = vm((4, rows, cols), bf16)
        scratch[name + ".sec"] = vm((3, rows, cols), bf16)
        scratch[name + ".fin"] = vm((2, 2) + halved, bf16)
        scratch[name + ".land"] = vm((max(bits, 1), 2) + halved, bf16)
        fin[name] = jax.ShapeDtypeStruct((2, 2) + halved, bf16)
    outs = dict(
        o_block=jax.ShapeDtypeStruct((RT, D), bf16),
        o_grad=jax.ShapeDtypeStruct((RT, D), bf16),
        o_expert=jax.ShapeDtypeStruct((2, 4, D, D), bf16),
        o_a2=fin["t_a2"],
        o_du=fin["t_du"],
        o_dd=fin["t_dd"],
        o_a1=fin["t_a1"],
        o_vec=jax.ShapeDtypeStruct((VROWS, D), f32),
    )
    ins = list(arrays)
    names = ins + list(outs) + list(scratch)

    def body(*refs):
        members = {}
        for name, ref in zip(names, refs, strict=True):
            if "." in name:
                outer, inner = name.split(".")
                members.setdefault(outer, Bag(by_rows=sums[outer])).__dict__[inner] = ref
            else:
                members[name] = ref
        for name in ("t_du", "t_a1"):
            members[name].full = members["t_a2"].full
        block_kernel(bits, Bag(**members))

    return pl.pallas_call(
        body,
        out_shape=list(outs.values()),
        in_specs=[pl.BlockSpec(memory_space=pl.ANY)] * len(ins),
        out_specs=[pl.BlockSpec(memory_space=pl.ANY)] * len(outs),
        scratch_shapes=list(scratch.values()),
        compiler_params=pltpu.CompilerParams(
            collective_id=0, has_side_effects=True, vmem_limit_bytes=64 * 2**20 - 2**18
        ),
        name="blocks",
    )(*arrays.values())


FINISHED = ("block", "grad", "expert", "a2", "du", "dd", "a1", "vec")
BIG = ("block", "grad", "p1", "o1", "up", "dn", "p2", "o2", "eup", "edn")


def finish_kernel(r):
    RT, D = r.block.shape
    R = r.o_block.shape[1]
    sec = lax.axis_index("section")
    copies = {}
    for k, name in enumerate(FINISHED):
        copies[name] = pltpu.make_async_copy(getattr(r, name), getattr(r, "v_" + name), r.sems.at[k])
        copies[name].start()
    outs = []

    def send(name):
        c = pltpu.make_async_copy(getattr(r, "w_" + name), getattr(r, "o_" + name), r.sems.at[len(FINISHED) + len(outs)])
        c.start()
        outs.append(c)

    row, col = iota((R, RP), 0), iota((R, RP), 1)
    for name in ("block", "grad"):
        copies[name].wait()
        src, dst = getattr(r, "v_" + name), getattr(r, "w_" + name)
        total = jnp.zeros((R, D), f32)
        for i in range(R // PATCHES):
            pick = onehot((row - i * PATCHES == col) & (col < PATCHES))
            total = total + dot(pick, src[i * RP : (i + 1) * RP, :])
        dst[0] = total.astype(bf16)
        send(name)
    copies["expert"].wait()
    for b in range(4):
        r.w_eup[0, :, b * D : (b + 1) * D] = r.v_expert[0, b].astype(f32)
    send("eup")
    for b in range(4):
        r.w_edn[0, b * D : (b + 1) * D, :] = r.v_expert[1, b].astype(f32)
    send("edn")
    n = D // 8
    for k in ("2", "1"):
        copies["a" + k].wait()
        src, dst_p, dst_o = getattr(r, "v_a" + k), getattr(r, "w_p" + k), getattr(r, "w_o" + k)
        for c in range(2):
            rows = slice(c * n, (c + 1) * n)
            dst_p[rows, 0 : 2 * D] = src[c, 0].astype(f32)
            dst_p[rows, 2 * D : 3 * D] = src[c, 1, :, 0:D].astype(f32)
            dst_o[rows, :] = src[c, 1, :, D : 2 * D].astype(f32)
        send("p" + k)
        send("o" + k)
    copies["du"].wait()
    for c in range(2):
        for k in range(2):
            r.w_up[c * n : (c + 1) * n, k * 2 * D : (k + 1) * 2 * D] = r.v_du[c, k].astype(f32)
    send("up")
    copies["dd"].wait()
    m = r.v_dd.shape[2]
    for c in range(2):
        for k in range(2):
            at = (2 * c + k) * m
            r.w_dn[at : at + m, :] = r.v_dd[c, k].astype(f32)
    send("dn")
    copies["vec"].wait()
    q = D // 4
    mine = jnp.where(iota((D, q), 0) == iota((D, q), 1) + sec * q, 1.0, 0.0)
    cut = jnp.dot(r.v_vec[...], mine, precision=lax.Precision.HIGHEST, preferred_element_type=f32)
    for dst, at in (
        (r.o_g1, V_A1), (r.o_s1, V_A1 + 1), (r.o_b1, V_A1 + 2), (r.o_gd, V_D), (r.o_sd, V_D + 1), (r.o_db, V_D + 2),
        (r.o_g2, V_A2), (r.o_s2, V_A2 + 1), (r.o_b2, V_A2 + 2), (r.o_gm, V_M), (r.o_sm, V_M + 1),
    ):
        dst[...] = cut[at : at + 1, :]
    r.o_rt[...] = cut[V_R : V_R + 8, :]
    r.o_hb[...] = r.v_vec[pl.ds(V_HB + sec, 1), :].reshape(-1)
    for c in outs:
        c.wait()


def finish(parts, shape):
    R, D, FF = shape
    q = D // 4
    s = lambda *dims: jax.ShapeDtypeStruct(dims, f32)
    rows = jax.ShapeDtypeStruct((1, R, D), bf16)
    outs = dict(
        block=rows, grad=rows,
        g1=s(1, q), s1=s(1, q), p1=s(q, 3 * D), o1=s(q, D), b1=s(1, q),
        gd=s(1, q), sd=s(1, q), up=s(q, FF), hb=s(FF // 4), dn=s(FF // 4, D), db=s(1, q),
        g2=s(1, q), s2=s(1, q), p2=s(q, 3 * D), o2=s(q, D), b2=s(1, q),
        gm=s(1, q), sm=s(1, q), rt=s(8, q), eup=s(1, D, FF), edn=s(1, FF, D),
    )
    scratch = {"v_" + name: pltpu.VMEM(part.shape, part.dtype) for name, part in zip(FINISHED, parts)}
    scratch |= {"w_" + name: pltpu.VMEM(outs[name].shape, outs[name].dtype) for name in BIG}
    scratch["sems"] = pltpu.SemaphoreType.DMA((len(FINISHED) + len(BIG),))
    names = list(FINISHED) + ["o_" + name for name in outs] + list(scratch)
    anywhere, near = pl.BlockSpec(memory_space=pltpu.HBM), pl.BlockSpec(memory_space=pltpu.VMEM)

    def body(*refs):
        finish_kernel(Bag(**dict(zip(names, refs, strict=True))))

    return pl.pallas_call(
        body,
        out_shape=list(outs.values()),
        in_specs=[anywhere] * len(FINISHED),
        out_specs=[anywhere if name in BIG else near for name in outs],
        scratch_shapes=list(scratch.values()),
        compiler_params=pltpu.CompilerParams(vmem_limit_bytes=62 * 2**20),
        name="finish",
    )(*parts)


def local(
    patches_in, cotangent, task_ids, routes, keep_mask,
    first_gain, first_shift, first_proj, first_out, first_bias,
    dense_gain, dense_shift, dense_up, hidden_bias, dense_down, dense_bias,
    second_gain, second_shift, second_proj, second_out, second_bias,
    mixture_gain, mixture_shift, router, expert_up, expert_down,
):
    bits = (lax.axis_size("wide") // 2).bit_length() - 1
    arrays = dict(
        patches=patches_in,
        cotangent=cotangent,
        task=task_ids,
        routes=jnp.transpose(routes, (0, 2, 1)),
        keep=jnp.transpose(keep_mask, (0, 2, 1)),
        s_p1=first_proj,
        s_o1=first_out,
        s_up=dense_up,
        s_dn=dense_down,
        s_p2=second_proj,
        s_o2=second_out,
        router=router.T,
        expert_up=expert_up,
        expert_down=expert_down,
        first_gain=first_gain,
        first_shift=first_shift,
        first_bias=first_bias,
        dense_gain=dense_gain,
        dense_shift=dense_shift,
        hidden_bias=hidden_bias,
        dense_bias=dense_bias,
        second_gain=second_gain,
        second_shift=second_shift,
        second_bias=second_bias,
        mixture_gain=mixture_gain,
        mixture_shift=mixture_shift,
    )
    parts = run_blocks(bits, arrays)
    R, D = patches_in.shape[1:]
    outs = list(finish(parts, (R, D, expert_up.shape[2])))
    for at in (2, 3, 6, 7, 8, 12, 13, 14, 17, 18, 19):
        outs[at] = outs[at].reshape(-1)
    outs[20] = outs[20].T
    return tuple(outs)


def solution(mesh):
    rows, vec, mat = P(None, "wide", None), P(), P("section", None)
    cube = P("section", None, None)
    in_specs = (
        rows, rows, P(None, "wide"), rows, rows,
        vec, vec, mat, mat, vec,
        vec, vec, mat, vec, mat, vec,
        vec, vec, mat, mat, vec,
        vec, vec, mat, cube, cube,
    )
    cut, moved = P("section"), P("section", "wide", None)
    out_specs = (
        moved, moved,
        cut, cut, mat, mat, cut,
        cut, cut, mat, cut, mat, cut,
        cut, cut, mat, mat, cut,
        cut, cut, mat, cube, cube,
    )
    return jax.shard_map(local, mesh=mesh, in_specs=in_specs, out_specs=out_specs, check_vma=False)
```

```python
import functools

import jax
import jax.numpy as jnp
from jax import lax
from jax.experimental import pallas as pl
from jax.experimental.pallas import tpu as pltpu
from jax.sharding import PartitionSpec as P

HEADS = 6
HEAD_DIM = 64
PATCHES = 196
EXPERTS = 4
TASKS = 2
CAPACITY = 488
EPSILON = 1e-06
MESH = pl.DeviceIdType.MESH
bf16 = jnp.bfloat16
f32 = jnp.float32

RP = 208
SL = 496
VROWS = 32
NSEM = 200


def dot(left, right):
    return jnp.dot(left, right, preferred_element_type=f32)


def nt(left, right):
    return lax.dot_general(left, right, (((1,), (1,)), ((), ())), preferred_element_type=f32)


def tn(left, right):
    return lax.dot_general(left, right, (((0,), (0,)), ((), ())), preferred_element_type=f32)


def iota(shape, dim):
    return lax.broadcasted_iota(jnp.int32, shape, dim)


def onehot(cond):
    return jnp.where(cond, 1.0, 0.0).astype(bf16)


def normed(x):
    centered = x - jnp.mean(x, axis=-1, keepdims=True)
    scale = lax.rsqrt(jnp.mean(centered * centered, axis=-1, keepdims=True) + EPSILON)
    return centered * scale, scale


def norm_back(grad, xhat, scale, gain):
    inner = grad * gain
    mean_inner = jnp.mean(inner, axis=-1, keepdims=True)
    mean_cross = jnp.mean(inner * xhat, axis=-1, keepdims=True)
    return scale * (inner - mean_inner - xhat * mean_cross)


def gelu_both(u):
    cdf = 0.5 * (1.0 + lax.erf(u * 0.7071067811865476))
    return u * cdf, cdf + u * (jnp.exp(u * u * -0.5) * 0.3989422804014327)


def column_sum(v):
    return jnp.sum(v, axis=0, keepdims=True)


V_A1, V_D, V_HB, V_A2, V_M, V_R = 0, 3, 6, 10, 13, 16


class Links:
    def __init__(self, send_sems, recv_sems):
        self.send_sems, self.recv_sems, self.used, self.sent = send_sems, recv_sems, 0, {}

    def take(self, count=1):
        first = self.used
        self.used += count
        return first

    def copy(self, number, src, dst, device):
        return pltpu.make_async_remote_copy(
            src_ref=src,
            dst_ref=dst,
            send_sem=self.send_sems.at[number],
            recv_sem=self.recv_sems.at[number],
            device_id=device,
            device_id_type=MESH,
        )

    def start(self, name, number=None):
        number = self.take() if number is None else number
        self.copy(number, *name()).start()
        self.sent[number] = name
        return number

    def arrived(self, number, there, device):
        self.copy(number, there, there, device).wait_recv()

    def left(self, number):
        self.copy(number, *self.sent.pop(number)()).wait_send()

    def drain(self):
        for number in list(self.sent):
            self.left(number)


def at_steps(hooks, i):
    for step, actions in hooks.items():

        @pl.when(i == step)
        def _():
            for action in actions:
                action()


def block_kernel(bits, r):
    R, D = r.patches.shape[1:]
    FF = r.expert_up.shape[2]
    xraw = r.h3.at[pl.ds(0, R)]
    IMG = R // PATCHES
    RT = IMG * RP
    FC = D
    NF = FF // FC
    NS = 4
    sec = lax.axis_index("section")
    wide = lax.axis_index("wide")
    core = lax.rem(wide, 2)
    chip = wide // 2
    links = Links(r.send, r.recv)

    sec_hi, sec_lo = sec // 2, lax.rem(sec, 2)

    def flip(bit, by):
        return bit + by - 2 * bit * by

    peers = [flip(sec_hi, j // 2) * 2 + flip(sec_lo, j % 2) for j in range(NS)]
    at_section = [(peer, wide) for peer in peers]
    mate = (sec, wide + 1 - 2 * core)
    bit_of = [lax.rem(chip // (1 << b), 2) for b in range(bits)]
    near_bits = min(bits, 2)
    near = 1 << near_bits
    at_near = []
    for k in range(near):
        other = wide
        for b in range(near_bits):
            if k >> b & 1:
                other = other + (1 - 2 * bit_of[b]) * (2 << b)
        at_near.append((sec, other))
    at_chip = [at_near[1 << b] if b < near_bits else (sec, wide + (1 - 2 * bit_of[b]) * (2 << b)) for b in range(bits)]
    near_index = lax.rem(chip, near)
    near_indices = []
    for k in range(near):
        index = 0
        for b in range(near_bits):
            index = index + flip(bit_of[b], k >> b & 1) * (1 << b)
        near_indices.append(index)

    def peer_of(j):
        return flip(sec_hi, j // 2) * 2 + flip(sec_lo, lax.rem(j, 2))

    local = []

    def fetch(src, dst):
        c = pltpu.make_async_copy(src, dst, r.local.at[len(local)])
        c.start()
        local.append(c)
        return c

    small = [fetch(getattr(r, name), getattr(r, "v_" + name)) for name in SMALL_IN]
    fetch_x = fetch(r.patches.at[sec], xraw)
    fetch_c = [fetch(r.cotangent.at[m], r.pool.at[pl.ds(m * R, R)]) for m in range(NS)]

    r.rt[...] = jnp.zeros(r.rt.shape, f32)

    barrier = pltpu.get_barrier_semaphore()
    partners = at_section[1:] + [mate] + at_near[1:] + at_chip[near_bits:]
    for device in partners:
        pl.semaphore_signal(barrier, inc=1, device_id=device, device_id_type=MESH)
    pl.semaphore_wait(barrier, len(partners))

    shards = [
        (r.s_p1, r.w_p1),
        (r.s_o1, r.w_o1),
        (r.s_up, r.w_up),
        (r.s_dn, r.w_dn),
        (r.s_p2, r.w_p2),
        (r.s_o2, r.w_o2),
    ]
    SPREAD = 3
    direct, passed, spread = {}, {}, {}

    def piece(t, j, c, part=None):
        n = shards[t][0].shape[0]
        h = n // 2
        at, rows = peers[j] * n + c * h, h
        if part is not None:
            rows = h // near
            at = at + part * rows
        return shards[t][1].at[pl.ds(pl.multiple_of(at, 16), rows)]

    def own(t, part=None):
        n = shards[t][0].shape[0]
        at, rows = core * (n // 2), n // 2
        if part is not None:
            rows = rows // near
            at = at + part * rows
        return shards[t][0].at[pl.ds(pl.multiple_of(at, 16), rows)]

    for t in (SPREAD, 0, 1, 2, 4, 5):
        part = near_index if t == SPREAD else None
        for j in range(1, NS):
            direct[t, j] = links.start(
                lambda t=t, j=j, part=part: (own(t, part), piece(t, 0, core, part), at_section[j])
            )
    fetch_w = []
    for shard, whole in shards:
        n = shard.shape[0]
        fetch_w.append(fetch(shard, whole.at[pl.ds(pl.multiple_of(sec * n, n), n)]))

    def spread_on():
        for j in range(1, NS):
            links.arrived(direct[SPREAD, j], piece(SPREAD, j, core, near_index), at_section[j])
            for k in range(1, near):
                spread[j, k] = links.start(
                    lambda j=j, k=k: (piece(SPREAD, j, core, near_index), piece(SPREAD, j, core, near_index), at_near[k])
                )

    def pass_on(*group):
        for t in group:
            for j in range(1, NS):
                if t == SPREAD:
                    for k in range(1, near):
                        links.arrived(spread[j, k], piece(t, j, core, near_indices[k]), at_near[k])
                else:
                    links.arrived(direct[t, j], piece(t, j, core), at_section[j])
                passed[t, j] = links.start(lambda t=t, j=j: (piece(t, j, core), piece(t, j, core), mate))

    def landed(*group):
        for t in group:
            fetch_w[t].wait()
            for j in range(1, NS):
                links.arrived(passed[t, j], piece(t, j, 1 - core), mate)

    for c in small:
        c.wait()
    q = D // NS
    r.rt[sec, 0 : TASKS * EXPERTS, 0:q] = r.v_router[...].astype(f32)
    vec = Bag()
    for k, name in enumerate(VECTORS):
        line = getattr(r, "v_" + name)
        r.lines[k : k + 1, 0 : line.shape[0]] = line[...].reshape(1, -1)
        setattr(vec, name, r.lines.at[pl.ds(k, 1), pl.ds(0, line.shape[0])])

    def chosen_rows(m_is, expert):
        r0 = jnp.zeros((1, R), jnp.int32)
        r1, k0, k1 = r0, r0, r0
        for m in range(NS):
            mine = jnp.where(m_is == m, 1, 0)
            r0 = r0 + mine * r.v_routes[m, 0:1, :]
            r1 = r1 + mine * r.v_routes[m, 1:2, :]
            k0 = k0 + mine * r.v_keep[m, 0:1, :]
            k1 = k1 + mine * r.v_keep[m, 1:2, :]
        return jnp.where(((r0 == expert) & (k0 == 1)) | ((r1 == expert) & (k1 == 1)), 1.0, 0.0)

    r.chosen[...] = jnp.zeros(r.chosen.shape, f32)
    for j in range(NS):
        r.chosen[j : j + 1, :] = chosen_rows(sec, peers[j])
        r.chosen[4 + j : 5 + j, :] = chosen_rows(peers[j], sec)

    def slots_of(limit, valid):
        chosen = r.chosen[...].astype(bf16)
        column = iota((limit.shape[0], R), 1)
        before = nt(onehot(column < limit), chosen)
        upto = nt(onehot((column <= limit) & valid), chosen)
        return jnp.where(upto > before, before, -1.0)

    def slots_padded(i, carry):
        off = iota((RP, 1), 0)
        r.pos_pad[pl.ds(pl.multiple_of(i * RP, RP), RP), :] = slots_of(i * PATCHES + off, off < PATCHES)
        return carry

    lax.fori_loop(0, IMG, slots_padded, 0)
    RC = R // 7

    def slots_raw(i, carry):
        off = iota((RC, 1), 0)
        r.q8[pl.ds(pl.multiple_of(i * RC, RC), RC), 0:16] = slots_of(i * RC + off, off >= 0)
        return carry

    lax.fori_loop(0, 7, slots_raw, 0)

    fetch_x.wait()
    for c in fetch_c:
        c.wait()
    for i in range(IMG):
        start = (PATCHES * i) // 16 * 16
        gap = PATCHES * i - start
        a, b = iota((RP, RP), 0), iota((RP, RP), 1)
        shift = onehot((b == a + gap) & (a < PATCHES))
        r.h0[i * RP : (i + 1) * RP, :] = dot(shift, xraw[start : start + RP, :]).astype(bf16)
        first = pl.multiple_of(sec * R + start, 16)
        r.g3[i * RP : (i + 1) * RP, :] = dot(shift, r.pool[pl.ds(first, RP), :]).astype(bf16)

    spread_on()

    slot_lane = iota((1, SL), 1).astype(f32)
    for j in range(NS):
        pick = onehot(r.q8[0:R, 4 + j : 5 + j] == slot_lane)
        first = pl.multiple_of(peers[j] * R, 16)
        r.gslot[j] = tn(pick, r.pool[pl.ds(first, R), :]).astype(bf16)
        row = iota((R, 128), 0)
        task = jnp.zeros((R, 128), jnp.int32)
        for i in range(IMG):
            task = jnp.where((row >= i * PATCHES) & (row < (i + 1) * PATCHES), r.v_task[peers[j], i], task)
        task = tn(pick, task.astype(f32).astype(bf16))
        r.tslot[...] = task if j == 0 else jnp.where(iota((SL, 128), 1) == j, task, r.tslot[...])

    low_half = iota((1, 128), 1) < 64
    half_masks = [onehot(low_half), onehot(jnp.logical_not(low_half))]
    low_half_rows = iota((RP, 128), 1) < 64
    key_ok = iota((RP, RP), 0) < PATCHES

    def attend(h_in, h_out, vecs, w_p, w_o, qkv_s, p_s, ctx_s, hooks):
        gain, shift, bias = vecs

        def image(i, carry):
            rows = pl.ds(pl.multiple_of(i * RP, RP), RP)
            x = h_in[rows, :].astype(f32)
            a = (normed(x)[0] * gain[...] + shift[...]).astype(bf16)
            qkv = dot(a, w_p[...]).astype(bf16)
            qkv_s[rows, :] = qkv
            parts = []
            for pair in range(HEADS // 2):
                at = 128 * pair
                q2 = qkv[:, at : at + 128]
                k2 = qkv[:, D + at : D + at + 128]
                v2 = qkv[:, 2 * D + at : 2 * D + at + 128]
                outs = []
                for half in range(2):
                    scores = nt(k2 * half_masks[half], q2)
                    scores = jnp.where(key_ok, scores, -1e30)
                    top = jnp.max(scores, axis=0, keepdims=True)
                    e = jnp.exp((scores - top) * HEAD_DIM**-0.5)
                    p = (e * (1.0 / jnp.sum(e, axis=0, keepdims=True))).astype(bf16)
                    p_s[i * HEADS + 2 * pair + half] = p
                    outs.append(tn(p, v2))
                parts.append(jnp.where(low_half_rows, outs[0], outs[1]).astype(bf16))
            ctx = jnp.concatenate(parts, axis=1)
            ctx_s[rows, :] = ctx
            h_out[rows, :] = (x + dot(ctx, w_o[...]) + bias[...]).astype(bf16)
            at_steps(hooks, i)
            return carry

        lax.fori_loop(0, IMG, image, 0)

    def attend_back(h_in, g_in, g_out, vecs, w_p, w_o, qkv_s, p_s, vrow, hooks, values_done=False):
        gain, shift, _ = vecs

        def image(i, carry):
            rows = pl.ds(pl.multiple_of(i * RP, RP), RP)
            g = g_in[rows, :]
            gf = g.astype(f32)
            xhat, scale = normed(h_in[rows, :].astype(f32))
            if values_done:
                gc = r.z[rows, D : 2 * D]
            else:
                r.a_s[rows, :] = (xhat * gain[...] + shift[...]).astype(bf16)
                gc = nt(g, w_o[...]).astype(bf16)
            qkv = qkv_s[rows, :]
            gq, gk, gv = [], [], []
            for pair in range(HEADS // 2):
                at = 128 * pair
                q2 = qkv[:, at : at + 128]
                k2 = qkv[:, D + at : D + at + 128]
                v2 = qkv[:, 2 * D + at : 2 * D + at + 128]
                gc2 = gc[:, at : at + 128]
                two = []
                for half in range(2):
                    p = p_s[i * HEADS + 2 * pair + half]
                    pf = p.astype(f32)
                    gp = nt(v2 * half_masks[half], gc2)
                    t = pf * gp
                    gs = (t - pf * jnp.sum(t, axis=0, keepdims=True)).astype(bf16)
                    two.append((tn(gs, k2), dot(gs, q2), None if values_done else dot(p, gc2)))
                gq.append((jnp.where(low_half_rows, two[0][0], two[1][0]) * HEAD_DIM**-0.5).astype(bf16))
                gk.append((jnp.where(low_half_rows, two[0][1], two[1][1]) * HEAD_DIM**-0.5).astype(bf16))
                if not values_done:
                    gv.append(jnp.where(low_half_rows, two[0][2], two[1][2]).astype(bf16))
            if values_done:
                gv = [r.z[rows, 0:D]]
            gqkv = jnp.concatenate(gq + gk + gv, axis=1)
            qkv_s[rows, :] = gqkv
            ga = nt(gqkv, w_p[...])
            r.vec[vrow : vrow + 1, :] += column_sum(ga * xhat)
            r.vec[vrow + 1 : vrow + 2, :] += column_sum(ga)
            r.vec[vrow + 2 : vrow + 3, :] += column_sum(gf)
            g_out[rows, :] = (gf + norm_back(ga, xhat, scale, gain[...])).astype(bf16)
            at_steps(hooks, i)
            return carry

        lax.fori_loop(0, IMG, image, 0)

    def values_back(h_in, g_in, vecs, w_o, p_s, hooks):
        gain, shift, _ = vecs

        def image(i, carry):
            rows = pl.ds(pl.multiple_of(i * RP, RP), RP)
            xhat, _ = normed(h_in[rows, :].astype(f32))
            r.a_s[rows, :] = (xhat * gain[...] + shift[...]).astype(bf16)
            gc = nt(g_in[rows, :], w_o[...]).astype(bf16)
            r.z[rows, D : 2 * D] = gc
            for pair in range(HEADS // 2):
                at = 128 * pair
                two = [dot(p_s[i * HEADS + 2 * pair + half], gc[:, at : at + 128]) for half in range(2)]
                r.z[rows, at : at + 128] = jnp.where(low_half_rows, two[0], two[1]).astype(bf16)
            at_steps(hooks, i)
            return carry

        lax.fori_loop(0, IMG, image, 0)

    r.vec[...] = jnp.zeros(r.vec.shape, f32)
    att1 = (vec.first_gain, vec.first_shift, vec.first_bias)
    att2 = (vec.second_gain, vec.second_shift, vec.second_bias)

    pass_on(0, 1)
    landed(0, 1)
    fetch_e = []
    for f in range(NF):
        cols = pl.ds(f * FC, FC)
        fetch_e.append(fetch(r.expert_up.at[0, :, cols], r.up.at[f]))
        fetch_e.append(fetch(r.expert_down.at[0, cols], r.down.at[f]))
    router_numbers = {}
    for j in range(1, NS):
        router_numbers[j] = links.start(
            lambda j=j: (
                r.rt.at[sec, pl.ds(0, TASKS * EXPERTS)],
                r.rt.at[sec, pl.ds(0, TASKS * EXPERTS)],
                at_section[j],
            )
        )
    attend(r.h0, r.h1, att1, r.w_p1, r.w_o1, r.qkv1, r.p1, r.ctx1, {IMG - 1: [lambda: pass_on(3, 2)]})
    landed(3, 2)
    HR = RT // 2

    def dense_step(i, carry):
        rows = pl.ds(pl.multiple_of(i * HR, HR), HR)
        x = r.h1[rows, :].astype(f32)
        a = (normed(x)[0] * vec.dense_gain[...] + vec.dense_shift[...]).astype(bf16)
        total = x + vec.dense_bias[...]
        for f in range(NF):
            cols = slice(f * FC, (f + 1) * FC)
            u = dot(a, r.w_up[:, cols]) + vec.hidden_bias[:, cols]
            z, slope = gelu_both(u)
            z = z.astype(bf16)
            r.z[rows, cols] = z
            r.slope[rows, cols] = slope.astype(bf16)
            total = total + dot(z, r.w_dn[cols, :])
        r.h2[rows, :] = total.astype(bf16)
        at_steps({1: [lambda: pass_on(4, 5)]}, i)
        return carry

    lax.fori_loop(0, 2, dense_step, 0)
    landed(4, 5)
    attend(r.h2, r.h3, att2, r.w_p2, r.w_o2, r.qkv2, r.p2, r.ctx2, {})

    for j in range(1, NS):
        links.arrived(router_numbers[j], r.rt.at[peers[j], pl.ds(0, TASKS * EXPERTS)], at_section[j])
    for p in range(NS):
        r.w_rt[p * q : (p + 1) * q, :] = r.rt[p].T[0:q, :].astype(bf16)
    lane = iota((1, 128), 1)

    def gates_of(a, task):
        logits = dot(a, r.w_rt[...])
        active = (lane < TASKS * EXPERTS) & (lane // EXPERTS == task)
        top = jnp.max(jnp.where(active, logits, -1e30), axis=-1, keepdims=True)
        e = jnp.where(active, jnp.exp(jnp.minimum(logits - top, 0.0)), 0.0)
        return e / jnp.sum(e, axis=-1, keepdims=True)

    def mix_rows(i, carry):
        rows = pl.ds(pl.multiple_of(i * RP, RP), RP)
        a = (normed(r.h3[rows, :].astype(f32))[0] * vec.mixture_gain[...] + vec.mixture_shift[...]).astype(bf16)
        r.a_s[rows, :] = a
        return carry

    lax.fori_loop(0, IMG, mix_rows, 0)

    slots_first = links.take(NS)
    for j in (1, 2, 3, 0):
        pick = onehot(r.pos_pad[:, j : j + 1] == slot_lane)
        r.slot_out[j] = tn(pick, r.a_s[...]).astype(bf16)
        if j > 0:
            links.start(lambda j=j: (r.slot_out.at[j], r.slot_in.at[j - 1], at_section[j]), slots_first + j)

    for c in fetch_e:
        c.wait()
    ga_first, q_first, w_first = links.take(NS), links.take(NS), links.take(NS)

    def ga_in(j):
        return r.pool.at[pl.ds((j - 1) * SL, SL)]

    def w_in(j):
        return r.pool.at[pl.ds((j + 2) * SL, SL)]

    e_parts = []
    for k in range(2):
        order = list(range(bits))
        if k == 1 and bits > 1:
            order[:2] = [1, 0]
        first = bit_of[order[0]] if bits > 0 else 0
        second = bit_of[order[1]] if bits > 1 else 0
        e_parts.append(
            Bag(k=k, order=order, keep=2 * k + first, send=2 * k + 1 - first, near=second, far=1 - second)
        )
    half_rows = FC // 2
    for part in e_parts if bits > 1 else ():
        part.near_rows = pl.ds(pl.multiple_of(part.near * half_rows, half_rows), half_rows)
        part.far_rows = pl.ds(pl.multiple_of(part.far * half_rows, half_rows), half_rows)

    def expert_step(j, last, own=False):
        a = r.slot_out[0] if own else r.slot_in[j - 1]
        gs = r.gslot[j]
        gates = gates_of(a, jnp.sum(jnp.where(lane == j, r.tslot[...], 0.0), axis=-1, keepdims=True).astype(jnp.int32))
        combine = jnp.sum(jnp.where(lax.rem(lane, EXPERTS) == sec, gates, 0.0), axis=-1, keepdims=True)
        gout = (combine * gs.astype(f32)).astype(bf16)
        for part in e_parts:
            f = part.keep if last else part.send
            z, slope = gelu_both(dot(a, r.up[f]))
            z = z.astype(bf16)
            out = dot(z, r.down[f])
            gv = (nt(gout, r.down[f]) * slope).astype(bf16)
            ga = nt(gv, r.up[f])
            if part.k == 0 and not last:
                r.acc[0:SL, :] = out
                r.acc[SL : 2 * SL, :] = ga
            elif part.k == 0 and not own:
                r.acc[0:SL, :] = out + r.out_half[j - 1].astype(f32)
                r.acc[SL : 2 * SL, :] = ga + r.slot_out[j].astype(f32)
            else:
                r.acc[0:SL, :] += out
                r.acc[SL : 2 * SL, :] += ga
            if own:
                r.eg[0, f] = tn(a, gv)
                r.eg[1, f] = tn(z, gout)
            else:
                r.eg[0, f] += tn(a, gv)
                r.eg[1, f] += tn(z, gout)
        if own and not last:
            return
        r.slot_out[j] = r.acc[SL : 2 * SL, :].astype(bf16)
        if not last:
            r.out_half[j - 1] = r.acc[0:SL, :].astype(bf16)
            return
        weighted = combine * r.acc[0:SL, :].astype(bf16).astype(f32)
        q = jnp.sum(gs.astype(f32) * weighted, axis=-1, keepdims=True)
        q_hi = q.astype(bf16).astype(f32)
        lanes = iota((SL, 128), 1)
        q2 = jnp.where(lanes == 0, q_hi, jnp.where(lanes == 1, q - q_hi, 0.0))
        r.q_out[j] = q2.T[0:16, :].astype(bf16)
        r.gslot[j] = weighted.astype(bf16)

    e_numbers = {}

    def e_core_start(last):
        for part in e_parts:
            block = part.keep if last else part.send
            staged = (lambda k=part.k: r.up.at[k]) if last else (lambda k=part.k: r.g0.at[pl.ds(k * D, D)])
            staged()[...] = r.eg[1 - core, block].astype(bf16)
            e_numbers["core", part.k, last] = links.start(
                lambda staged=staged, block=block: (staged(), r.e_sum.at[block], mate)
            )

    def e_core_end(last):
        for part in e_parts:
            block = part.keep if last else part.send
            links.arrived(e_numbers["core", part.k, last], r.e_sum.at[block], mate)
            if not last:
                links.left(e_numbers["core", part.k, last])
            total = r.eg[core, block] + r.e_sum[block].astype(f32)
            if last and bits > 0:
                links.arrived(e_numbers["block", part.k], r.e_land.at[part.k], at_chip[part.order[0]])
                total = total + r.e_land[part.k].astype(f32)
            r.e_sum[block] = total.astype(bf16)

    def e_blocks_start():
        if bits > 0:
            for part in e_parts:
                e_numbers["block", part.k] = links.start(
                    lambda part=part: (r.e_sum.at[part.send], r.e_land.at[part.k], at_chip[part.order[0]])
                )

    def e_step_start(step):
        for part in e_parts:
            which = part.far_rows if step == 1 else part.near_rows
            e_numbers["step", step, part.k] = links.start(
                lambda part=part, which=which: (
                    r.e_sum.at[part.keep, which],
                    r.e_land2.at[step - 1, part.k],
                    at_chip[part.order[step]],
                )
            )

    def e_step_end(step):
        for part in e_parts:
            number = e_numbers["step", step, part.k]
            links.arrived(number, r.e_land2.at[step - 1, part.k], at_chip[part.order[step]])
            if step > 1:
                links.left(number)
            rows = part.near_rows
            mine = r.e_sum[part.keep, rows, :].astype(f32)
            r.e_sum[part.keep, rows, :] = (mine + r.e_land2[step - 1, part.k].astype(f32)).astype(bf16)

    def e_own():
        for part in e_parts:
            if bits > 1:
                rows = part.near_rows
                r.e_all[part.keep, rows, :] = r.e_sum[part.keep, rows, :]
            else:
                r.e_all[part.keep] = r.e_sum[part.keep]
            if bits == 0:
                r.e_all[part.send] = r.e_sum[part.send]

    def e_spread_start(step):
        if bits > step:
            for part in e_parts:
                where = (part.keep, part.near_rows) if step == 1 else (part.keep,)
                e_numbers["up", step, part.k] = links.start(
                    lambda part=part, where=where: (
                        r.e_all.at[where],
                        r.e_all.at[where],
                        at_chip[part.order[step]],
                    )
                )

    def e_spread_end(step):
        if bits > step:
            for part in e_parts:
                where = (part.keep, part.far_rows) if step == 1 else (part.send,)
                links.arrived(e_numbers["up", step, part.k], r.e_all.at[where], at_chip[part.order[step]])

    def e_pair_start():
        e_numbers["pair"] = links.start(lambda: (r.e_all, r.down, mate))

    def e_pair_end():
        links.arrived(e_numbers["pair"], r.down, mate)

    def answer(j):
        links.copy(ga_first + j, r.slot_out.at[j], ga_in(j), (peer_of(j), wide)).start()
        links.copy(q_first + j, r.q_out.at[j], r.q_in.at[j], (peer_of(j), wide)).start()

    expert_step(0, False, True)
    expert_step(0, True, True)

    def others_first(j, carry):
        links.copy(slots_first + j, r.slot_out.at[j], r.slot_in.at[j - 1], (peer_of(j), wide)).wait()
        expert_step(j, False)
        return carry

    lax.fori_loop(1, NS, others_first, 0)
    e_core_start(False)

    def others_last(j, carry):
        expert_step(j, True)
        answer(j)
        at_steps({1: [lambda: e_core_end(False), e_blocks_start]}, j)
        return carry

    lax.fori_loop(1, NS, others_last, 0)

    for j in range(1, NS):
        links.sent.pop(slots_first + j)

    def grads_back(j):
        links.copy(ga_first + j, r.slot_out.at[j], ga_in(j), at_section[j]).wait()
        links.copy(q_first + j, r.q_out.at[j], r.q_in.at[j], at_section[j]).wait()

    e_core_start(True)
    for j in range(1, NS):
        links.start(lambda j=j: (r.gslot.at[j], w_in(j), at_section[j]), w_first + j)

    def split(size, k, first, offset=0):
        v = bit_of[(0 if k == 0 else min(bits, 2) - 1)] if bits > 0 else 0
        which = v if first else 1 - v
        return pl.ds(pl.multiple_of(offset + which * (size // 2), 16), size // 2)

    half_cols, half_rows_of, at_cols, at_rows = [], [], [], []
    for k in range(2 if bits > 0 else 0):
        half_cols.append([split(2 * D, k, first) for first in (False, True)])
        half_rows_of.append([split(FC // 4, k, first) for first in (False, True)])
        at_cols.append([split(2 * D, k, first, 2 * D * k) for first in (False, True)])
        at_rows.append([split(FC // 4, k, first, FC // 4 * k) for first in (False, True)])

    class Summed:
        def __init__(self, buffers, halving=True):
            self.b = buffers
            self.numbers = {}
            self.halving = halving and bits > 0

        def part(self, k, near):
            if not self.halving:
                return ()
            if self.b.by_rows:
                return (half_rows_of[k][1 if near else 0],)
            return (slice(None), half_cols[k][1 if near else 0])

        def back(self, k, near):
            if self.b.by_rows:
                return self.b.sec.at[0, at_rows[k][1 if near else 0]]
            return self.b.sec.at[0, :, at_cols[k][1 if near else 0]]

        def order(self, k):
            return ([0, 1] + list(range(2, bits)) if k == 0 else [1, 0] + list(range(2, bits))) if bits > 1 else [0]

        def cut(self, k):
            rows, cols = self.b.pair.shape[1:]
            if self.b.by_rows:
                return pl.ds(k * (rows // 2), rows // 2), pl.ds(0, cols)
            return pl.ds(0, rows), pl.ds(k * (cols // 2), cols // 2)

        def send_core(self, halves=(0, 1)):
            b = self.b
            for k in halves:
                self.numbers["core", k] = links.start(
                    lambda k=k: (b.full.at[(pl.ds(0, NS), 1 - core) + self.cut(k)], b.pair.at[(pl.ds(0, NS),) + self.cut(k)], mate)
                )

        def send_section(self, halves=(0, 1)):
            b = self.b
            for k in halves:
                links.arrived(self.numbers["core", k], b.pair.at[(pl.ds(0, NS),) + self.cut(k)], mate)
                links.left(self.numbers["core", k])
                for p in range(NS):
                    mine = b.full[(p, core) + self.cut(k)].astype(f32)
                    b.pair[(p,) + self.cut(k)] = (mine + b.pair[(p,) + self.cut(k)].astype(f32)).astype(bf16)
                for j in range(1, NS):
                    self.numbers["section", k, j] = links.start(
                        lambda k=k, j=j: (b.pair.at[(peers[j],) + self.cut(k)], b.sec.at[(j - 1,) + self.cut(k)], at_section[j])
                    )

        def section_sum(self, halves=(0, 1)):
            b = self.b
            for k in halves:
                total = b.pair[(sec,) + self.cut(k)].astype(f32)
                for j in range(1, NS):
                    there = (j - 1,) + self.cut(k)
                    links.arrived(self.numbers["section", k, j], b.sec.at[there], at_section[j])
                    total = total + b.sec[there].astype(f32)
                b.fin[core, k] = total.astype(bf16)

        def chip_start(self, step, halves=(0, 1)):
            for k in halves:
                bit = self.order(k)[step]
                near = step > 0

                def name(k=k, bit=bit, near=near):
                    land = self.b.land.at[(step, k) + self.part(k, True)]
                    return self.b.fin.at[(core, k) + self.part(k, near)], land, at_chip[bit]

                if step == 0 and self.halving:

                    def name(k=k, bit=bit):
                        here = (k,) + self.part(k, False)
                        return self.b.fin.at[(core,) + here], self.b.land.at[(0,) + here], at_chip[bit]

                self.numbers["chip", k] = links.start(name)

        def chip_end(self, step, halves=(0, 1)):
            for k in halves:
                bit = self.order(k)[step]
                number = self.numbers["chip", k]
                here = (k,) + self.part(k, True)
                links.arrived(number, self.b.land.at[(step,) + here], at_chip[bit])
                links.left(number)
                mine = self.b.fin[(core,) + here].astype(f32)
                self.b.fin[(core,) + here] = (mine + self.b.land[(step,) + here].astype(f32)).astype(bf16)

        def chip_spread(self, halves=(0, 1)):
            for k in halves if self.halving else ():
                self.numbers["spread", k] = links.start(
                    lambda k=k: (
                        self.b.fin.at[(core, k) + self.part(k, True)],
                        self.back(k, True),
                        at_chip[self.order(k)[0]],
                    )
                )

        def chip_spread_end(self, halves=(0, 1)):
            for k in halves if self.halving else ():
                links.arrived(self.numbers["spread", k], self.back(k, False), at_chip[self.order(k)[0]])
                self.b.fin[(core, k) + self.part(k, False)] = self.back(k, False)[...]

        def pair_start(self, halves=(0, 1)):
            for k in halves:
                self.numbers["pair", k] = links.start(lambda k=k: (self.b.fin.at[core, k], self.b.fin.at[core, k], mate))

        def pair_end(self, halves=(0, 1)):
            for k in halves:
                links.arrived(self.numbers["pair", k], self.b.fin.at[1 - core, k], mate)

    def by_section_rows(full, cols, value):
        n = D // NS // 2
        for p in range(NS):
            for c in range(2):
                full[p, c, :, cols] = value[(2 * p + c) * n : (2 * p + c + 1) * n, :].astype(bf16)

    sum_a2, sum_du, sum_dd = (Summed(b) for b in (r.t_a2, r.t_du, r.t_dd))
    sum_a1 = Summed(r.t_a1, False)
    out_copies = []

    def send_out(src, dst):
        c = pltpu.make_async_copy(src, dst, r.out_sems.at[len(out_copies)])
        c.start()
        out_copies.append(c)

    def mix_gather(experts, first):
        def step(i, carry):
            rows = pl.ds(pl.multiple_of(i * RP, RP), RP)
            task = jnp.zeros((RP, 1), jnp.int32) + r.v_task[sec, i]
            active = (lane < TASKS * EXPERTS) & (lane // EXPERTS == task)
            ga = jnp.zeros((RP, D), f32) if first else r.acc[rows, :]
            q8 = jnp.zeros((RP, 128), f32) if first else r.q8[rows, :]
            for j in experts:
                pick = onehot(r.pos_pad[rows, j : j + 1] == slot_lane)
                ga = ga + dot(pick, r.slot_out[0] if j == 0 else ga_in(j)[...])
                one = jnp.sum(nt(pick, r.q_out[0] if j == 0 else r.q_in[j]), axis=-1, keepdims=True)
                q8 = q8 + jnp.where(active & (lax.rem(lane, EXPERTS) == peers[j]), one, 0.0)
            if first:
                r.acc[rows, :] = ga
                r.q8[rows, :] = q8
                return carry
            a = r.a_s[rows, :]
            gl = (q8 - gates_of(a, task) * jnp.sum(q8, axis=-1, keepdims=True)).astype(bf16)
            ga = ga + nt(gl, r.w_rt[...])
            r.vec[V_R : V_R + 8, :] += tn(gl, a)[0:8, :]
            xhat, scale = normed(r.h3[rows, :].astype(f32))
            r.vec[V_M : V_M + 1, :] += column_sum(ga * xhat)
            r.vec[V_M + 1 : V_M + 2, :] += column_sum(ga)
            g = r.g3[rows, :].astype(f32)
            r.g2[rows, :] = (g + norm_back(ga, xhat, scale, vec.mixture_gain[...])).astype(bf16)
            return carry

        lax.fori_loop(0, IMG, step, 0)

    grads_back(1)
    grads_back(2)
    mix_gather((0, 1, 2), True)
    e_core_end(True)
    if bits > 1:
        e_step_start(1)
    grads_back(3)
    mix_gather((3,), False)

    def e_third():
        for step in range(1, bits):
            if step > 1:
                e_step_start(step)
            e_step_end(step)
        e_own()
        e_spread_start(1)

    def e_fourth():
        e_spread_end(1)
        e_spread_start(0)

    def e_fifth():
        e_spread_end(0)
        e_pair_start()

    attend_back(
        r.h2, r.g2, r.g1, att2, r.w_p2, r.w_o2, r.qkv2, r.p2, V_A2, {1: [e_third]}
    )
    for f in range(3):
        cols = slice(f * D, (f + 1) * D)
        by_section_rows(r.t_a2.full, cols, tn(r.a_s[...], r.qkv2[:, cols]))
    by_section_rows(r.t_a2.full, slice(3 * D, 4 * D), tn(r.ctx2[...], r.g2[...]))
    sum_a2.send_core()

    def dense_back(i, carry):
        rows = pl.ds(pl.multiple_of(i * HR, HR), HR)
        g = r.g1[rows, :]
        gf = g.astype(f32)
        xhat, scale = normed(r.h1[rows, :].astype(f32))
        r.a_s[rows, :] = (xhat * vec.dense_gain[...] + vec.dense_shift[...]).astype(bf16)
        ga = jnp.zeros((HR, D), f32)
        for f in range(NF):
            cols = slice(f * FC, (f + 1) * FC)
            gu = (nt(g, r.w_dn[cols, :]) * r.slope[rows, cols].astype(f32)).astype(bf16)
            r.slope[rows, cols] = gu
            r.vec[V_HB + f : V_HB + f + 1, :] += column_sum(gu.astype(f32))
            ga = ga + nt(gu, r.w_up[:, cols])
        r.vec[V_D : V_D + 1, :] += column_sum(ga * xhat)
        r.vec[V_D + 1 : V_D + 2, :] += column_sum(ga)
        r.vec[V_D + 2 : V_D + 3, :] += column_sum(gf)
        r.g0[rows, :] = (gf + norm_back(ga, xhat, scale, vec.dense_gain[...])).astype(bf16)
        at_steps({0: [sum_a2.send_section, e_fourth]}, i)
        return carry

    lax.fori_loop(0, 2, dense_back, 0)

    for f in range(NF):
        cols = slice(f * FC, (f + 1) * FC)
        by_section_rows(r.t_du.full, cols, tn(r.a_s[...], r.slope[:, cols]))
    sum_du.send_core()
    for f in range(NF):
        value = tn(r.z[:, f * FC : (f + 1) * FC], r.g1[...])
        n = FC // 2
        for c in range(2):
            r.t_dd.full[f, c] = value[c * n : (c + 1) * n, :].astype(bf16)
    sum_dd.send_core()
    sum_du.send_section()

    def chips_first(one, halves=(0, 1)):
        one.section_sum(halves)
        if bits > 0:
            one.chip_start(0, halves)

    def chips_rest(one, halves=(0, 1)):
        for step in range(1, bits):
            one.chip_end(step - 1, halves)
            one.chip_start(step, halves)

    def chips_spread(one):
        if bits > 0:
            one.chip_end(bits - 1)
        one.chip_spread()

    def chips_last(one, halves=(0, 1)):
        if one.halving:
            one.chip_spread_end(halves)
        elif bits > 0:
            one.chip_end(bits - 1, halves)
        one.pair_start(halves)

    a1 = r.t_a1.full
    by_section_rows(a1, slice(3 * D, 4 * D), tn(r.ctx1[...], r.g0[...]))
    values_back(r.h0, r.g0, att1, r.w_o1, r.p1, {1: [sum_dd.send_section]})
    by_section_rows(a1, slice(2 * D, 3 * D), tn(r.a_s[...], r.z[:, 0:D]))
    sum_a1.send_core((1,))
    chips_first(sum_a2)
    attend_back(
        r.h0, r.g0, r.g3, att1, r.w_p1, r.w_o1, r.qkv1, r.p1, V_A1,
        {
            0: [lambda: sum_a1.send_section((1,))],
            2: [lambda: chips_rest(sum_a2), lambda: chips_first(sum_du)],
        },
        True,
    )
    for f in range(2):
        cols = slice(f * D, (f + 1) * D)
        by_section_rows(a1, cols, tn(r.a_s[...], r.qkv1[:, cols]))
    sum_a1.send_core((0,))
    send_out(r.g3, r.o_grad)
    chips_spread(sum_a2)

    def vec_start(land, device):
        return links.start(lambda: (r.vec, r.vec_land.at[land], device)), land, device

    def vec_end(number, land, device):
        links.arrived(number, r.vec_land.at[land], device)
        links.left(number)

    vec_core = vec_start(0, mate)
    for j in range(1, NS):
        links.arrived(w_first + j, w_in(j), at_section[j])
    vec_section = []

    def vec_two():
        vec_end(*vec_core)
        r.vec[...] += r.vec_land[0]
        vec_section.extend(vec_start(j, at_section[j]) for j in range(1, NS))

    def block_out(i, carry):
        rows = pl.ds(pl.multiple_of(i * RP, RP), RP)
        total = r.h3[rows, :].astype(f32)
        for j in range(NS):
            pick = onehot(r.pos_pad[rows, j : j + 1] == slot_lane)
            total = total + dot(pick, r.gslot[0] if j == 0 else w_in(j)[...])
        r.h3[rows, :] = total.astype(bf16)
        at_steps({1: [lambda: sum_a1.send_section((0,)), vec_two, lambda: chips_rest(sum_du)]}, i)
        return carry

    lax.fori_loop(0, IMG, block_out, 0)
    send_out(r.h3, r.o_block)
    chips_last(sum_a2)
    chips_first(sum_dd)
    chips_first(sum_a1, (1,))
    chips_spread(sum_du)
    for one in vec_section:
        vec_end(*one)
    r.vec[...] += r.vec_land[1] + r.vec_land[2] + r.vec_land[3]
    vec_chip = vec_start(NS, at_chip[0]) if bits > 0 else None
    chips_first(sum_a1, (0,))
    chips_rest(sum_dd)
    chips_last(sum_du)
    e_fifth()
    for step in range(1, bits):
        for k in (1, 0):
            sum_a1.chip_end(step - 1, (k,))
            sum_a1.chip_start(step, (k,))
        vec_end(*vec_chip)
        r.vec[...] += r.vec_land[NS + step - 1]
        vec_chip = vec_start(NS + step, at_chip[step])
        if step == bits - 1:
            chips_spread(sum_dd)
    if bits < 2:
        chips_spread(sum_dd)
    chips_last(sum_dd)
    e_pair_end()
    send_out(r.e_all, r.o_expert.at[core])
    send_out(r.down, r.o_expert.at[1 - core])
    for s, dst in ((sum_a2, r.o_a2), (sum_du, r.o_du), (sum_dd, r.o_dd)):
        s.pair_end()
        send_out(s.b.fin, dst)
    for k in (1, 0):
        chips_last(sum_a1, (k,))
    if bits > 0:
        vec_end(*vec_chip)
        r.vec[...] += r.vec_land[NS + bits - 1]
    send_out(r.vec, r.o_vec)
    sum_a1.pair_end()
    send_out(r.t_a1.fin, r.o_a1)
    links.drain()
    for c in out_copies:
        c.wait()
    assert links.used <= NSEM and len(local) <= 40 and len(out_copies) <= 12, links.used


class Bag:
    def __init__(self, **members):
        self.__dict__.update(members)


VECTORS = (
    "first_gain",
    "first_shift",
    "first_bias",
    "dense_gain",
    "dense_shift",
    "hidden_bias",
    "dense_bias",
    "second_gain",
    "second_shift",
    "second_bias",
    "mixture_gain",
    "mixture_shift",
)
SMALL_IN = ("task", "routes", "keep", "router") + VECTORS


def run_blocks(bits, arrays):
    R, D = arrays["patches"].shape[1:]
    FF = arrays["expert_up"].shape[2]
    IMG = R // PATCHES
    RT = IMG * RP
    n = D // 8
    vm = pltpu.VMEM
    scratch = dict(
        pool=vm((max(4 * R, 6 * SL), D), bf16),
        chosen=vm((16, R), f32),
        pos_pad=vm((RT, 16), f32),
        w_p1=vm((D, 3 * D), bf16),
        w_o1=vm((D, D), bf16),
        w_up=vm((D, FF), bf16),
        w_dn=vm((FF, D), bf16),
        w_p2=vm((D, 3 * D), bf16),
        w_o2=vm((D, D), bf16),
        w_rt=vm((D, 128), bf16),
        rt=vm((4, 128, 128), f32),
        lines=vm((16, FF), f32),
        up=vm((FF // D, D, D), bf16),
        down=vm((FF // D, D, D), bf16),
        out_half=vm((3, SL, D), bf16),
        h0=vm((RT, D), bf16),
        h1=vm((RT, D), bf16),
        h2=vm((RT, D), bf16),
        h3=vm((RT, D), bf16),
        g0=vm((RT, D), bf16),
        g1=vm((RT, D), bf16),
        g2=vm((RT, D), bf16),
        g3=vm((RT, D), bf16),
        a_s=vm((RT, D), bf16),
        qkv1=vm((RT, 3 * D), bf16),
        qkv2=vm((RT, 3 * D), bf16),
        p1=vm((IMG * HEADS, RP, RP), bf16),
        p2=vm((IMG * HEADS, RP, RP), bf16),
        ctx1=vm((RT, D), bf16),
        ctx2=vm((RT, D), bf16),
        z=vm((RT, FF), bf16),
        slope=vm((RT, FF), bf16),
        slot_out=vm((4, SL, D), bf16),
        slot_in=vm((3, SL, D), bf16),
        gslot=vm((4, SL, D), bf16),
        tslot=vm((SL, 128), f32),
        q_out=vm((4, 16, SL), bf16),
        q_in=vm((4, 16, SL), bf16),
        acc=vm((2 * SL, D), f32),
        q8=vm((RT, 128), f32),
        eg=vm((2, 4, D, D), f32),
        e_sum=vm((4, D, D), bf16),
        e_land=vm((2, D, D), bf16),
        e_land2=vm((max(bits - 1, 1), 2, D // 2, D), bf16),
        e_all=vm((4, D, D), bf16),
        vec=vm((VROWS, D), f32),
        vec_land=vm((4 + max(bits, 1), VROWS, D), f32),
        send=pltpu.SemaphoreType.DMA((NSEM,)),
        recv=pltpu.SemaphoreType.DMA((NSEM,)),
        local=pltpu.SemaphoreType.DMA((40,)),
        out_sems=pltpu.SemaphoreType.DMA((12,)),
    )
    for name in SMALL_IN:
        space = pltpu.SMEM if name == "task" else vm
        scratch["v_" + name] = space(arrays[name].shape, arrays[name].dtype)
    sums = dict(t_a2=False, t_du=False, t_dd=True, t_a1=False)
    fin = {}
    for name, by_rows in sums.items():
        rows, cols = (D // 2, D) if by_rows else (n, FF)
        halved = (rows // 2, cols) if by_rows else (rows, cols // 2)
        if name in ("t_a2", "t_dd"):
            scratch[name + ".full"] = vm((4, 2, rows, cols), bf16)
        scratch[name + ".pair"] = vm((4, rows, cols), bf16)
        scratch[name + ".sec"] = vm((3, rows, cols), bf16)
        scratch[name + ".fin"] = vm((2, 2) + halved, bf16)
        scratch[name + ".land"] = vm((max(bits, 1), 2) + halved, bf16)
        fin[name] = jax.ShapeDtypeStruct((2, 2) + halved, bf16)
    outs = dict(
        o_block=jax.ShapeDtypeStruct((RT, D), bf16),
        o_grad=jax.ShapeDtypeStruct((RT, D), bf16),
        o_expert=jax.ShapeDtypeStruct((2, 4, D, D), bf16),
        o_a2=fin["t_a2"],
        o_du=fin["t_du"],
        o_dd=fin["t_dd"],
        o_a1=fin["t_a1"],
        o_vec=jax.ShapeDtypeStruct((VROWS, D), f32),
    )
    ins = list(arrays)
    names = ins + list(outs) + list(scratch)

    def body(*refs):
        members = {}
        for name, ref in zip(names, refs, strict=True):
            if "." in name:
                outer, inner = name.split(".")
                members.setdefault(outer, Bag(by_rows=sums[outer])).__dict__[inner] = ref
            else:
                members[name] = ref
        for name in ("t_du", "t_a1"):
            members[name].full = members["t_a2"].full
        block_kernel(bits, Bag(**members))

    return pl.pallas_call(
        body,
        out_shape=list(outs.values()),
        in_specs=[pl.BlockSpec(memory_space=pl.ANY)] * len(ins),
        out_specs=[pl.BlockSpec(memory_space=pl.ANY)] * len(outs),
        scratch_shapes=list(scratch.values()),
        compiler_params=pltpu.CompilerParams(
            collective_id=0, has_side_effects=True, vmem_limit_bytes=64 * 2**20 - 2**18
        ),
        name="blocks",
    )(*arrays.values())


FINISHED = ("block", "grad", "expert", "a2", "du", "dd", "a1", "vec")
BIG = ("block", "grad", "p1", "o1", "up", "dn", "p2", "o2", "eup", "edn")


def finish_kernel(r):
    RT, D = r.block.shape
    R = r.o_block.shape[1]
    sec = lax.axis_index("section")
    copies = {}
    for k, name in enumerate(FINISHED):
        copies[name] = pltpu.make_async_copy(getattr(r, name), getattr(r, "v_" + name), r.sems.at[k])
        copies[name].start()
    outs = []

    def send(name):
        c = pltpu.make_async_copy(getattr(r, "w_" + name), getattr(r, "o_" + name), r.sems.at[len(FINISHED) + len(outs)])
        c.start()
        outs.append(c)

    row, col = iota((R, RP), 0), iota((R, RP), 1)
    for name in ("block", "grad"):
        copies[name].wait()
        src, dst = getattr(r, "v_" + name), getattr(r, "w_" + name)
        total = jnp.zeros((R, D), f32)
        for i in range(R // PATCHES):
            pick = onehot((row - i * PATCHES == col) & (col < PATCHES))
            total = total + dot(pick, src[i * RP : (i + 1) * RP, :])
        dst[0] = total.astype(bf16)
        send(name)
    copies["expert"].wait()
    for b in range(4):
        r.w_eup[0, :, b * D : (b + 1) * D] = r.v_expert[0, b].astype(f32)
    send("eup")
    for b in range(4):
        r.w_edn[0, b * D : (b + 1) * D, :] = r.v_expert[1, b].astype(f32)
    send("edn")
    n = D // 8
    for k in ("2", "1"):
        copies["a" + k].wait()
        src, dst_p, dst_o = getattr(r, "v_a" + k), getattr(r, "w_p" + k), getattr(r, "w_o" + k)
        for c in range(2):
            rows = slice(c * n, (c + 1) * n)
            dst_p[rows, 0 : 2 * D] = src[c, 0].astype(f32)
            dst_p[rows, 2 * D : 3 * D] = src[c, 1, :, 0:D].astype(f32)
            dst_o[rows, :] = src[c, 1, :, D : 2 * D].astype(f32)
        send("p" + k)
        send("o" + k)
    copies["du"].wait()
    for c in range(2):
        for k in range(2):
            r.w_up[c * n : (c + 1) * n, k * 2 * D : (k + 1) * 2 * D] = r.v_du[c, k].astype(f32)
    send("up")
    copies["dd"].wait()
    m = r.v_dd.shape[2]
    for c in range(2):
        for k in range(2):
            at = (2 * c + k) * m
            r.w_dn[at : at + m, :] = r.v_dd[c, k].astype(f32)
    send("dn")
    copies["vec"].wait()
    q = D // 4
    mine = jnp.where(iota((D, q), 0) == iota((D, q), 1) + sec * q, 1.0, 0.0)
    cut = jnp.dot(r.v_vec[...], mine, precision=lax.Precision.HIGHEST, preferred_element_type=f32)
    for dst, at in (
        (r.o_g1, V_A1), (r.o_s1, V_A1 + 1), (r.o_b1, V_A1 + 2), (r.o_gd, V_D), (r.o_sd, V_D + 1), (r.o_db, V_D + 2),
        (r.o_g2, V_A2), (r.o_s2, V_A2 + 1), (r.o_b2, V_A2 + 2), (r.o_gm, V_M), (r.o_sm, V_M + 1),
    ):
        dst[...] = cut[at : at + 1, :]
    r.o_rt[...] = cut[V_R : V_R + 8, :]
    r.o_hb[...] = r.v_vec[pl.ds(V_HB + sec, 1), :].reshape(-1)
    for c in outs:
        c.wait()


def finish(parts, shape):
    R, D, FF = shape
    q = D // 4
    s = lambda *dims: jax.ShapeDtypeStruct(dims, f32)
    rows = jax.ShapeDtypeStruct((1, R, D), bf16)
    outs = dict(
        block=rows, grad=rows,
        g1=s(1, q), s1=s(1, q), p1=s(q, 3 * D), o1=s(q, D), b1=s(1, q),
        gd=s(1, q), sd=s(1, q), up=s(q, FF), hb=s(FF // 4), dn=s(FF // 4, D), db=s(1, q),
        g2=s(1, q), s2=s(1, q), p2=s(q, 3 * D), o2=s(q, D), b2=s(1, q),
        gm=s(1, q), sm=s(1, q), rt=s(8, q), eup=s(1, D, FF), edn=s(1, FF, D),
    )
    scratch = {"v_" + name: pltpu.VMEM(part.shape, part.dtype) for name, part in zip(FINISHED, parts)}
    scratch |= {"w_" + name: pltpu.VMEM(outs[name].shape, outs[name].dtype) for name in BIG}
    scratch["sems"] = pltpu.SemaphoreType.DMA((len(FINISHED) + len(BIG),))
    names = list(FINISHED) + ["o_" + name for name in outs] + list(scratch)
    anywhere, near = pl.BlockSpec(memory_space=pltpu.HBM), pl.BlockSpec(memory_space=pltpu.VMEM)

    def body(*refs):
        finish_kernel(Bag(**dict(zip(names, refs, strict=True))))

    return pl.pallas_call(
        body,
        out_shape=list(outs.values()),
        in_specs=[anywhere] * len(FINISHED),
        out_specs=[anywhere if name in BIG else near for name in outs],
        scratch_shapes=list(scratch.values()),
        compiler_params=pltpu.CompilerParams(vmem_limit_bytes=62 * 2**20),
        name="finish",
    )(*parts)


def local(
    patches_in, cotangent, task_ids, routes, keep_mask,
    first_gain, first_shift, first_proj, first_out, first_bias,
    dense_gain, dense_shift, dense_up, hidden_bias, dense_down, dense_bias,
    second_gain, second_shift, second_proj, second_out, second_bias,
    mixture_gain, mixture_shift, router, expert_up, expert_down,
):
    bits = (lax.axis_size("wide") // 2).bit_length() - 1
    arrays = dict(
        patches=patches_in,
        cotangent=cotangent,
        task=task_ids,
        routes=jnp.transpose(routes, (0, 2, 1)),
        keep=jnp.transpose(keep_mask, (0, 2, 1)),
        s_p1=first_proj,
        s_o1=first_out,
        s_up=dense_up,
        s_dn=dense_down,
        s_p2=second_proj,
        s_o2=second_out,
        router=router.T,
        expert_up=expert_up,
        expert_down=expert_down,
        first_gain=first_gain,
        first_shift=first_shift,
        first_bias=first_bias,
        dense_gain=dense_gain,
        dense_shift=dense_shift,
        hidden_bias=hidden_bias,
        dense_bias=dense_bias,
        second_gain=second_gain,
        second_shift=second_shift,
        second_bias=second_bias,
        mixture_gain=mixture_gain,
        mixture_shift=mixture_shift,
    )
    parts = run_blocks(bits, arrays)
    R, D = patches_in.shape[1:]
    outs = list(finish(parts, (R, D, expert_up.shape[2])))
    for at in (2, 3, 6, 7, 8, 12, 13, 14, 17, 18, 19):
        outs[at] = outs[at].reshape(-1)
    outs[20] = outs[20].T
    return tuple(outs)


def solution(mesh):
    rows, vec, mat = P(None, "wide", None), P(), P("section", None)
    cube = P("section", None, None)
    in_specs = (
        rows, rows, P(None, "wide"), rows, rows,
        vec, vec, mat, mat, vec,
        vec, vec, mat, vec, mat, vec,
        vec, vec, mat, mat, vec,
        vec, vec, mat, cube, cube,
    )
    cut, moved = P("section"), P("section", "wide", None)
    out_specs = (
        moved, moved,
        cut, cut, mat, mat, cut,
        cut, cut, mat, cut, mat, cut,
        cut, cut, mat, mat, cut,
        cut, cut, mat, cube, cube,
    )
    return jax.shard_map(local, mesh=mesh, in_specs=in_specs, out_specs=out_specs, check_vma=False)
```

```python
import functools

import jax
import jax.numpy as jnp
from jax import lax
from jax.experimental import pallas as pl
from jax.experimental.pallas import tpu as pltpu
from jax.sharding import PartitionSpec as P

HEADS = 6
HEAD_DIM = 64
PATCHES = 196
EXPERTS = 4
TASKS = 2
CAPACITY = 488
EPSILON = 1e-06
MESH = pl.DeviceIdType.MESH
bf16 = jnp.bfloat16
f32 = jnp.float32

RP = 208
SL = 496
VROWS = 24
NSEM = 200


def dot(left, right):
    return jnp.dot(left, right, preferred_element_type=f32)


def nt(left, right):
    return lax.dot_general(left, right, (((1,), (1,)), ((), ())), preferred_element_type=f32)


def tn(left, right):
    return lax.dot_general(left, right, (((0,), (0,)), ((), ())), preferred_element_type=f32)


def iota(shape, dim):
    return lax.broadcasted_iota(jnp.int32, shape, dim)


def onehot(cond):
    return jnp.where(cond, 1.0, 0.0).astype(bf16)


def normed(x):
    centered = x - jnp.mean(x, axis=-1, keepdims=True)
    scale = lax.rsqrt(jnp.mean(centered * centered, axis=-1, keepdims=True) + EPSILON)
    return centered * scale, scale


def norm_back(grad, xhat, scale, gain):
    inner = grad * gain
    mean_inner = jnp.mean(inner, axis=-1, keepdims=True)
    mean_cross = jnp.mean(inner * xhat, axis=-1, keepdims=True)
    return scale * (inner - mean_inner - xhat * mean_cross)


def gelu_both(u):
    cdf = 0.5 * (1.0 + lax.erf(u * 0.7071067811865476))
    return u * cdf, cdf + u * (jnp.exp(u * u * -0.5) * 0.3989422804014327)


def column_sum(v):
    return jnp.sum(v, axis=0, keepdims=True)


V_A1, V_D, V_HB, V_A2, V_M, V_R = 0, 3, 6, 10, 13, 16


class Links:
    def __init__(self, send_sems, recv_sems):
        self.send_sems, self.recv_sems, self.used, self.sent = send_sems, recv_sems, 0, {}

    def take(self, count=1):
        first = self.used
        self.used += count
        return first

    def copy(self, number, src, dst, device):
        return pltpu.make_async_remote_copy(
            src_ref=src,
            dst_ref=dst,
            send_sem=self.send_sems.at[number],
            recv_sem=self.recv_sems.at[number],
            device_id=device,
            device_id_type=MESH,
        )

    def start(self, name, number=None):
        number = self.take() if number is None else number
        self.copy(number, *name()).start()
        self.sent[number] = name
        return number

    def arrived(self, number, there, device):
        self.copy(number, there, there, device).wait_recv()

    def left(self, number):
        self.copy(number, *self.sent.pop(number)()).wait_send()

    def drain(self):
        for number in list(self.sent):
            self.left(number)


def at_steps(hooks, i):
    for step, actions in hooks.items():

        @pl.when(i == step)
        def _():
            for action in actions:
                action()


def block_kernel(bits, r):
    R, D = r.patches.shape[1:]
    FF = r.expert_up.shape[2]
    xraw = r.h3.at[pl.ds(0, R)]
    IMG = R // PATCHES
    RT = IMG * RP
    FC = D
    NF = FF // FC
    NS = 4
    sec = lax.axis_index("section")
    wide = lax.axis_index("wide")
    core = lax.rem(wide, 2)
    chip = wide // 2
    links = Links(r.send, r.recv)

    sec_hi, sec_lo = sec // 2, lax.rem(sec, 2)

    def flip(bit, by):
        return bit + by - 2 * bit * by

    peers = [flip(sec_hi, j // 2) * 2 + flip(sec_lo, j % 2) for j in range(NS)]
    at_section = [(peer, wide) for peer in peers]
    mate = (sec, wide + 1 - 2 * core)
    bit_of = [lax.rem(chip // (1 << b), 2) for b in range(bits)]
    near_bits = min(bits, 2)
    near = 1 << near_bits
    at_near = []
    for k in range(near):
        other = wide
        for b in range(near_bits):
            if k >> b & 1:
                other = other + (1 - 2 * bit_of[b]) * (2 << b)
        at_near.append((sec, other))
    at_chip = [at_near[1 << b] if b < near_bits else (sec, wide + (1 - 2 * bit_of[b]) * (2 << b)) for b in range(bits)]
    near_index = lax.rem(chip, near)
    near_indices = []
    for k in range(near):
        index = 0
        for b in range(near_bits):
            index = index + flip(bit_of[b], k >> b & 1) * (1 << b)
        near_indices.append(index)

    def peer_of(j):
        return flip(sec_hi, j // 2) * 2 + flip(sec_lo, lax.rem(j, 2))

    local = []

    def fetch(src, dst):
        c = pltpu.make_async_copy(src, dst, r.local.at[len(local)])
        c.start()
        local.append(c)
        return c

    small = [fetch(getattr(r, name), getattr(r, "v_" + name)) for name in SMALL_IN]
    fetch_x = fetch(r.patches.at[sec], xraw)
    fetch_c = [fetch(r.cotangent.at[m], r.pool.at[pl.ds(m * R, R)]) for m in range(NS)]

    r.rt[...] = jnp.zeros(r.rt.shape, f32)

    barrier = pltpu.get_barrier_semaphore()
    partners = at_section[1:] + [mate] + at_near[1:] + at_chip[near_bits:]
    for device in partners:
        pl.semaphore_signal(barrier, inc=1, device_id=device, device_id_type=MESH)
    pl.semaphore_wait(barrier, len(partners))

    shards = [
        (r.s_p1, r.w_p1),
        (r.s_o1, r.w_o1),
        (r.s_up, r.w_up),
        (r.s_dn, r.w_dn),
        (r.s_p2, r.w_p2),
        (r.s_o2, r.w_o2),
    ]
    SPREAD = 3
    direct, passed, spread = {}, {}, {}

    def piece(t, j, c, part=None):
        n = shards[t][0].shape[0]
        h = n // 2
        at, rows = peers[j] * n + c * h, h
        if part is not None:
            rows = h // near
            at = at + part * rows
        return shards[t][1].at[pl.ds(pl.multiple_of(at, 16), rows)]

    def own(t, part=None):
        n = shards[t][0].shape[0]
        at, rows = core * (n // 2), n // 2
        if part is not None:
            rows = rows // near
            at = at + part * rows
        return shards[t][0].at[pl.ds(pl.multiple_of(at, 16), rows)]

    for t in (SPREAD, 0, 1, 2, 4, 5):
        part = near_index if t == SPREAD else None
        for j in range(1, NS):
            direct[t, j] = links.start(
                lambda t=t, j=j, part=part: (own(t, part), piece(t, 0, core, part), at_section[j])
            )
    fetch_w = []
    for shard, whole in shards:
        n = shard.shape[0]
        fetch_w.append(fetch(shard, whole.at[pl.ds(pl.multiple_of(sec * n, n), n)]))

    def spread_on():
        for j in range(1, NS):
            links.arrived(direct[SPREAD, j], piece(SPREAD, j, core, near_index), at_section[j])
            for k in range(1, near):
                spread[j, k] = links.start(
                    lambda j=j, k=k: (piece(SPREAD, j, core, near_index), piece(SPREAD, j, core, near_index), at_near[k])
                )

    def pass_on(*group):
        for t in group:
            for j in range(1, NS):
                if t == SPREAD:
                    for k in range(1, near):
                        links.arrived(spread[j, k], piece(t, j, core, near_indices[k]), at_near[k])
                else:
                    links.arrived(direct[t, j], piece(t, j, core), at_section[j])
                passed[t, j] = links.start(lambda t=t, j=j: (piece(t, j, core), piece(t, j, core), mate))

    def landed(*group):
        for t in group:
            fetch_w[t].wait()
            for j in range(1, NS):
                links.arrived(passed[t, j], piece(t, j, 1 - core), mate)

    for c in small:
        c.wait()
    q = D // NS
    r.rt[sec, 0 : TASKS * EXPERTS, 0:q] = r.v_router[...].astype(f32)
    vec = Bag()
    for k, name in enumerate(VECTORS):
        line = getattr(r, "v_" + name)
        r.lines[k : k + 1, 0 : line.shape[0]] = line[...].reshape(1, -1)
        setattr(vec, name, r.lines.at[pl.ds(k, 1), pl.ds(0, line.shape[0])])

    def chosen_rows(m_is, expert):
        r0 = jnp.zeros((1, R), jnp.int32)
        r1, k0, k1 = r0, r0, r0
        for m in range(NS):
            mine = jnp.where(m_is == m, 1, 0)
            r0 = r0 + mine * r.v_routes[m, 0:1, :]
            r1 = r1 + mine * r.v_routes[m, 1:2, :]
            k0 = k0 + mine * r.v_keep[m, 0:1, :]
            k1 = k1 + mine * r.v_keep[m, 1:2, :]
        return jnp.where(((r0 == expert) & (k0 == 1)) | ((r1 == expert) & (k1 == 1)), 1.0, 0.0)

    r.chosen[...] = jnp.zeros(r.chosen.shape, f32)
    for j in range(NS):
        r.chosen[j : j + 1, :] = chosen_rows(sec, peers[j])
        r.chosen[4 + j : 5 + j, :] = chosen_rows(peers[j], sec)

    def slots_of(limit, valid):
        chosen = r.chosen[...].astype(bf16)
        column = iota((limit.shape[0], R), 1)
        before = nt(onehot(column < limit), chosen)
        upto = nt(onehot((column <= limit) & valid), chosen)
        return jnp.where(upto > before, before, -1.0)

    def slots_padded(i, carry):
        off = iota((RP, 1), 0)
        r.pos_pad[pl.ds(pl.multiple_of(i * RP, RP), RP), :] = slots_of(i * PATCHES + off, off < PATCHES)
        return carry

    lax.fori_loop(0, IMG, slots_padded, 0)
    RC = R // 7

    def slots_raw(i, carry):
        off = iota((RC, 1), 0)
        r.q8[pl.ds(pl.multiple_of(i * RC, RC), RC), 0:16] = slots_of(i * RC + off, off >= 0)
        return carry

    lax.fori_loop(0, 7, slots_raw, 0)

    fetch_x.wait()
    for c in fetch_c:
        c.wait()
    for i in range(IMG):
        start = (PATCHES * i) // 16 * 16
        gap = PATCHES * i - start
        a, b = iota((RP, RP), 0), iota((RP, RP), 1)
        shift = onehot((b == a + gap) & (a < PATCHES))
        r.h0[i * RP : (i + 1) * RP, :] = dot(shift, xraw[start : start + RP, :]).astype(bf16)
        first = pl.multiple_of(sec * R + start, 16)
        r.g3[i * RP : (i + 1) * RP, :] = dot(shift, r.pool[pl.ds(first, RP), :]).astype(bf16)

    spread_on()

    slot_lane = iota((1, SL), 1).astype(f32)
    for j in range(NS):
        pick = onehot(r.q8[0:R, 4 + j : 5 + j] == slot_lane)
        first = pl.multiple_of(peers[j] * R, 16)
        r.gslot[j] = tn(pick, r.pool[pl.ds(first, R), :]).astype(bf16)
        row = iota((R, 128), 0)
        task = jnp.zeros((R, 128), jnp.int32)
        for i in range(IMG):
            task = jnp.where((row >= i * PATCHES) & (row < (i + 1) * PATCHES), r.v_task[peers[j], i], task)
        task = tn(pick, task.astype(f32).astype(bf16))
        r.tslot[...] = task if j == 0 else jnp.where(iota((SL, 128), 1) == j, task, r.tslot[...])

    low_half = iota((1, 128), 1) < 64
    half_masks = [onehot(low_half), onehot(jnp.logical_not(low_half))]
    low_half_rows = iota((RP, 128), 1) < 64
    key_ok = iota((RP, RP), 0) < PATCHES

    def attend(h_in, h_out, vecs, w_p, w_o, qkv_s, p_s, ctx_s, hooks):
        gain, shift, bias = vecs

        def image(i, carry):
            rows = pl.ds(pl.multiple_of(i * RP, RP), RP)
            x = h_in[rows, :].astype(f32)
            a = (normed(x)[0] * gain[...] + shift[...]).astype(bf16)
            qkv = dot(a, w_p[...]).astype(bf16)
            qkv_s[rows, :] = qkv
            parts = []
            for pair in range(HEADS // 2):
                at = 128 * pair
                q2 = qkv[:, at : at + 128]
                k2 = qkv[:, D + at : D + at + 128]
                v2 = qkv[:, 2 * D + at : 2 * D + at + 128]
                outs = []
                for half in range(2):
                    scores = nt(k2 * half_masks[half], q2)
                    scores = jnp.where(key_ok, scores, -1e30)
                    top = jnp.max(scores, axis=0, keepdims=True)
                    e = jnp.exp((scores - top) * HEAD_DIM**-0.5)
                    p = (e * (1.0 / jnp.sum(e, axis=0, keepdims=True))).astype(bf16)
                    p_s[i * HEADS + 2 * pair + half] = p
                    outs.append(tn(p, v2))
                parts.append(jnp.where(low_half_rows, outs[0], outs[1]).astype(bf16))
            ctx = jnp.concatenate(parts, axis=1)
            ctx_s[rows, :] = ctx
            h_out[rows, :] = (x + dot(ctx, w_o[...]) + bias[...]).astype(bf16)
            at_steps(hooks, i)
            return carry

        lax.fori_loop(0, IMG, image, 0)

    def attend_back(h_in, g_in, g_out, vecs, w_p, w_o, qkv_s, p_s, vrow, hooks, values_done=False):
        gain, shift, _ = vecs

        def image(i, carry):
            rows = pl.ds(pl.multiple_of(i * RP, RP), RP)
            g = g_in[rows, :]
            gf = g.astype(f32)
            xhat, scale = normed(h_in[rows, :].astype(f32))
            if values_done:
                gc = r.z[rows, D : 2 * D]
            else:
                r.a_s[rows, :] = (xhat * gain[...] + shift[...]).astype(bf16)
                gc = nt(g, w_o[...]).astype(bf16)
            qkv = qkv_s[rows, :]
            gq, gk, gv = [], [], []
            for pair in range(HEADS // 2):
                at = 128 * pair
                q2 = qkv[:, at : at + 128]
                k2 = qkv[:, D + at : D + at + 128]
                v2 = qkv[:, 2 * D + at : 2 * D + at + 128]
                gc2 = gc[:, at : at + 128]
                two = []
                for half in range(2):
                    p = p_s[i * HEADS + 2 * pair + half]
                    pf = p.astype(f32)
                    gp = nt(v2 * half_masks[half], gc2)
                    t = pf * gp
                    gs = (t - pf * jnp.sum(t, axis=0, keepdims=True)).astype(bf16)
                    two.append((tn(gs, k2), dot(gs, q2), None if values_done else dot(p, gc2)))
                gq.append((jnp.where(low_half_rows, two[0][0], two[1][0]) * HEAD_DIM**-0.5).astype(bf16))
                gk.append((jnp.where(low_half_rows, two[0][1], two[1][1]) * HEAD_DIM**-0.5).astype(bf16))
                if not values_done:
                    gv.append(jnp.where(low_half_rows, two[0][2], two[1][2]).astype(bf16))
            if values_done:
                gv = [r.z[rows, 0:D]]
            gqkv = jnp.concatenate(gq + gk + gv, axis=1)
            qkv_s[rows, :] = gqkv
            ga = nt(gqkv, w_p[...])
            r.vec[vrow : vrow + 1, :] += column_sum(ga * xhat)
            r.vec[vrow + 1 : vrow + 2, :] += column_sum(ga)
            r.vec[vrow + 2 : vrow + 3, :] += column_sum(gf)
            g_out[rows, :] = (gf + norm_back(ga, xhat, scale, gain[...])).astype(bf16)
            at_steps(hooks, i)
            return carry

        lax.fori_loop(0, IMG, image, 0)

    def values_back(h_in, g_in, vecs, w_o, p_s, hooks):
        gain, shift, _ = vecs

        def image(i, carry):
            rows = pl.ds(pl.multiple_of(i * RP, RP), RP)
            xhat, _ = normed(h_in[rows, :].astype(f32))
            r.a_s[rows, :] = (xhat * gain[...] + shift[...]).astype(bf16)
            gc = nt(g_in[rows, :], w_o[...]).astype(bf16)
            r.z[rows, D : 2 * D] = gc
            for pair in range(HEADS // 2):
                at = 128 * pair
                two = [dot(p_s[i * HEADS + 2 * pair + half], gc[:, at : at + 128]) for half in range(2)]
                r.z[rows, at : at + 128] = jnp.where(low_half_rows, two[0], two[1]).astype(bf16)
            at_steps(hooks, i)
            return carry

        lax.fori_loop(0, IMG, image, 0)

    r.vec[...] = jnp.zeros(r.vec.shape, f32)
    att1 = (vec.first_gain, vec.first_shift, vec.first_bias)
    att2 = (vec.second_gain, vec.second_shift, vec.second_bias)

    pass_on(0, 1)
    landed(0, 1)
    fetch_e = []
    for f in range(NF):
        cols = pl.ds(f * FC, FC)
        fetch_e.append(fetch(r.expert_up.at[0, :, cols], r.up.at[f]))
        fetch_e.append(fetch(r.expert_down.at[0, cols], r.down.at[f]))
    router_numbers = {}
    for j in range(1, NS):
        router_numbers[j] = links.start(
            lambda j=j: (
                r.rt.at[sec, pl.ds(0, TASKS * EXPERTS)],
                r.rt.at[sec, pl.ds(0, TASKS * EXPERTS)],
                at_section[j],
            )
        )
    attend(r.h0, r.h1, att1, r.w_p1, r.w_o1, r.qkv1, r.p1, r.ctx1, {IMG - 1: [lambda: pass_on(3, 2)]})
    landed(3, 2)
    HR = RT // 2

    def dense_step(i, carry):
        rows = pl.ds(pl.multiple_of(i * HR, HR), HR)
        x = r.h1[rows, :].astype(f32)
        a = (normed(x)[0] * vec.dense_gain[...] + vec.dense_shift[...]).astype(bf16)
        total = x + vec.dense_bias[...]
        for f in range(NF):
            cols = slice(f * FC, (f + 1) * FC)
            u = dot(a, r.w_up[:, cols]) + vec.hidden_bias[:, cols]
            z, slope = gelu_both(u)
            z = z.astype(bf16)
            r.z[rows, cols] = z
            r.slope[rows, cols] = slope.astype(bf16)
            total = total + dot(z, r.w_dn[cols, :])
        r.h2[rows, :] = total.astype(bf16)
        at_steps({1: [lambda: pass_on(4, 5)]}, i)
        return carry

    lax.fori_loop(0, 2, dense_step, 0)
    landed(4, 5)
    attend(r.h2, r.h3, att2, r.w_p2, r.w_o2, r.qkv2, r.p2, r.ctx2, {})

    for j in range(1, NS):
        links.arrived(router_numbers[j], r.rt.at[peers[j], pl.ds(0, TASKS * EXPERTS)], at_section[j])
    for p in range(NS):
        piece_rows = jnp.concatenate([r.rt[p], jnp.zeros((120, 128), f32)], axis=0)
        r.w_rt[p * q : (p + 1) * q, :] = piece_rows.T[0:q, :].astype(bf16)
    lane = iota((1, 128), 1)

    def gates_of(a, task):
        logits = dot(a, r.w_rt[...])
        active = (lane < TASKS * EXPERTS) & (lane // EXPERTS == task)
        top = jnp.max(jnp.where(active, logits, -1e30), axis=-1, keepdims=True)
        e = jnp.where(active, jnp.exp(jnp.minimum(logits - top, 0.0)), 0.0)
        return e / jnp.sum(e, axis=-1, keepdims=True)

    def mix_rows(i, carry):
        rows = pl.ds(pl.multiple_of(i * RP, RP), RP)
        a = (normed(r.h3[rows, :].astype(f32))[0] * vec.mixture_gain[...] + vec.mixture_shift[...]).astype(bf16)
        r.a_s[rows, :] = a
        return carry

    lax.fori_loop(0, IMG, mix_rows, 0)

    slots_first = links.take(NS)
    for j in (1, 2, 3, 0):
        pick = onehot(r.pos_pad[:, j : j + 1] == slot_lane)
        r.slot_out[j] = tn(pick, r.a_s[...]).astype(bf16)
        if j > 0:
            links.start(lambda j=j: (r.slot_out.at[j], r.slot_in.at[j - 1], at_section[j]), slots_first + j)

    for c in fetch_e:
        c.wait()
    ga_first, q_first, w_first = links.take(NS), links.take(NS), links.take(NS)

    def ga_in(j):
        return r.pool.at[pl.ds((j - 1) * SL, SL)]

    def w_in(j):
        return r.pool.at[pl.ds((j + 2) * SL, SL)]

    e_parts = []
    for k in range(2):
        order = list(range(bits))
        if k == 1 and bits > 1:
            order[:2] = [1, 0]
        first = bit_of[order[0]] if bits > 0 else 0
        second = bit_of[order[1]] if bits > 1 else 0
        e_parts.append(
            Bag(k=k, order=order, keep=2 * k + first, send=2 * k + 1 - first, near=second, far=1 - second)
        )
    half_rows = FC // 2
    for part in e_parts if bits > 1 else ():
        part.near_rows = pl.ds(pl.multiple_of(part.near * half_rows, half_rows), half_rows)
        part.far_rows = pl.ds(pl.multiple_of(part.far * half_rows, half_rows), half_rows)

    def expert_step(j, last, own=False):
        a = r.slot_out[0] if own else r.slot_in[j - 1]
        gs = r.gslot[j]
        combine = jnp.sum(jnp.where(lane == j, r.tslot[...], 0.0), axis=-1, keepdims=True)
        if not last:
            gates = gates_of(a, combine.astype(jnp.int32))
            combine = jnp.sum(jnp.where(lax.rem(lane, EXPERTS) == sec, gates, 0.0), axis=-1, keepdims=True)
            r.tslot[...] = jnp.where(lane == j, combine, r.tslot[...])
        gout = (combine * gs.astype(f32)).astype(bf16)
        for part in e_parts:
            f = part.keep if last else part.send
            z, slope = gelu_both(dot(a, r.up[f]))
            z = z.astype(bf16)
            out = dot(z, r.down[f])
            gv = (nt(gout, r.down[f]) * slope).astype(bf16)
            ga = nt(gv, r.up[f])
            if part.k == 0 and not last:
                r.acc[0:SL, :] = out
                r.acc[SL : 2 * SL, :] = ga
            elif part.k == 0 and not own:
                r.acc[0:SL, :] = out + r.out_half[j - 1].astype(f32)
                r.acc[SL : 2 * SL, :] = ga + r.slot_out[j].astype(f32)
            else:
                r.acc[0:SL, :] += out
                r.acc[SL : 2 * SL, :] += ga
            if own:
                r.eg[0, f] = tn(a, gv)
                r.eg[1, f] = tn(z, gout)
            else:
                r.eg[0, f] += tn(a, gv)
                r.eg[1, f] += tn(z, gout)
        if own and not last:
            return
        r.slot_out[j] = r.acc[SL : 2 * SL, :].astype(bf16)
        if not last:
            r.out_half[j - 1] = r.acc[0:SL, :].astype(bf16)
            return
        weighted = combine * r.acc[0:SL, :].astype(bf16).astype(f32)
        q = jnp.sum(gs.astype(f32) * weighted, axis=-1, keepdims=True)
        q_hi = q.astype(bf16).astype(f32)
        lanes = iota((SL, 128), 1)
        q2 = jnp.where(lanes == 0, q_hi, jnp.where(lanes == 1, q - q_hi, 0.0))
        r.q_out[j] = q2.T[0:16, :].astype(bf16)
        r.gslot[j] = weighted.astype(bf16)

    e_numbers = {}

    def e_core_start(last):
        for part in e_parts:
            block = part.keep if last else part.send
            staged = (lambda k=part.k: r.up.at[k]) if last else (lambda k=part.k: r.g0.at[pl.ds(k * D, D)])
            staged()[...] = r.eg[1 - core, block].astype(bf16)
            e_numbers["core", part.k, last] = links.start(
                lambda staged=staged, block=block: (staged(), r.e_sum.at[block], mate)
            )

    def e_core_end(last):
        for part in e_parts:
            block = part.keep if last else part.send
            links.arrived(e_numbers["core", part.k, last], r.e_sum.at[block], mate)
            if not last:
                links.left(e_numbers["core", part.k, last])
            total = r.eg[core, block] + r.e_sum[block].astype(f32)
            if last and bits > 0:
                links.arrived(e_numbers["block", part.k], r.e_land.at[part.k], at_chip[part.order[0]])
                total = total + r.e_land[part.k].astype(f32)
            r.e_sum[block] = total.astype(bf16)

    def e_blocks_start():
        if bits > 0:
            for part in e_parts:
                e_numbers["block", part.k] = links.start(
                    lambda part=part: (r.e_sum.at[part.send], r.e_land.at[part.k], at_chip[part.order[0]])
                )

    def e_step_start(step):
        for part in e_parts:
            which = part.far_rows if step == 1 else part.near_rows
            e_numbers["step", step, part.k] = links.start(
                lambda part=part, which=which: (
                    r.e_sum.at[part.keep, which],
                    r.e_land2.at[step - 1, part.k],
                    at_chip[part.order[step]],
                )
            )

    def e_step_end(step):
        for part in e_parts:
            number = e_numbers["step", step, part.k]
            links.arrived(number, r.e_land2.at[step - 1, part.k], at_chip[part.order[step]])
            if step > 1:
                links.left(number)
            rows = part.near_rows
            mine = r.e_sum[part.keep, rows, :].astype(f32)
            r.e_sum[part.keep, rows, :] = (mine + r.e_land2[step - 1, part.k].astype(f32)).astype(bf16)

    def e_own():
        for part in e_parts:
            if bits > 1:
                rows = part.near_rows
                r.e_all[part.keep, rows, :] = r.e_sum[part.keep, rows, :]
            else:
                r.e_all[part.keep] = r.e_sum[part.keep]
            if bits == 0:
                r.e_all[part.send] = r.e_sum[part.send]

    def e_spread_start(step):
        if bits > step:
            for part in e_parts:
                where = (part.keep, part.near_rows) if step == 1 else (part.keep,)
                e_numbers["up", step, part.k] = links.start(
                    lambda part=part, where=where: (
                        r.e_all.at[where],
                        r.e_all.at[where],
                        at_chip[part.order[step]],
                    )
                )

    def e_spread_end(step):
        if bits > step:
            for part in e_parts:
                where = (part.keep, part.far_rows) if step == 1 else (part.send,)
                links.arrived(e_numbers["up", step, part.k], r.e_all.at[where], at_chip[part.order[step]])

    def e_pair_start():
        e_numbers["pair"] = links.start(lambda: (r.e_all, r.down, mate))

    def e_pair_end():
        links.arrived(e_numbers["pair"], r.down, mate)

    def answer(j):
        links.copy(ga_first + j, r.slot_out.at[j], ga_in(j), (peer_of(j), wide)).start()
        links.copy(q_first + j, r.q_out.at[j], r.q_in.at[j], (peer_of(j), wide)).start()

    expert_step(0, False, True)
    expert_step(0, True, True)

    def others_first(j, carry):
        links.copy(slots_first + j, r.slot_out.at[j], r.slot_in.at[j - 1], (peer_of(j), wide)).wait()
        expert_step(j, False)
        return carry

    lax.fori_loop(1, NS, others_first, 0)
    e_core_start(False)

    def others_last(i, carry):
        j = lax.rem(i + 1, 3) + 1
        expert_step(j, True)
        answer(j)
        at_steps({1: [lambda: e_core_end(False), e_blocks_start]}, i)
        return carry

    lax.fori_loop(1, NS, others_last, 0)

    for j in range(1, NS):
        links.sent.pop(slots_first + j)

    def grads_back(j):
        links.copy(ga_first + j, r.slot_out.at[j], ga_in(j), at_section[j]).wait()
        links.copy(q_first + j, r.q_out.at[j], r.q_in.at[j], at_section[j]).wait()

    e_core_start(True)

    def split(size, k, first, offset=0):
        v = bit_of[(0 if k == 0 else min(bits, 2) - 1)] if bits > 0 else 0
        which = v if first else 1 - v
        return pl.ds(pl.multiple_of(offset + which * (size // 2), 16), size // 2)

    half_cols, half_rows_of, at_cols, at_rows = [], [], [], []
    for k in range(2 if bits > 0 else 0):
        half_cols.append([split(2 * D, k, first) for first in (False, True)])
        half_rows_of.append([split(FC // 4, k, first) for first in (False, True)])
        at_cols.append([split(2 * D, k, first, 2 * D * k) for first in (False, True)])
        at_rows.append([split(FC // 4, k, first, FC // 4 * k) for first in (False, True)])

    class Summed:
        def __init__(self, buffers, halving=True):
            self.b = buffers
            self.numbers = {}
            self.halving = halving and bits > 0

        def part(self, k, near):
            if not self.halving:
                return ()
            if self.b.by_rows:
                return (half_rows_of[k][1 if near else 0],)
            return (slice(None), half_cols[k][1 if near else 0])

        def back(self, k, near):
            if self.b.by_rows:
                return self.b.sec.at[0, at_rows[k][1 if near else 0]]
            return self.b.sec.at[0, :, at_cols[k][1 if near else 0]]

        def order(self, k):
            return ([0, 1] + list(range(2, bits)) if k == 0 else [1, 0] + list(range(2, bits))) if bits > 1 else [0]

        def cut(self, k):
            rows, cols = self.b.pair.shape[1:]
            if self.b.by_rows:
                return pl.ds(k * (rows // 2), rows // 2), pl.ds(0, cols)
            return pl.ds(0, rows), pl.ds(k * (cols // 2), cols // 2)

        def send_core(self, halves=(0, 1)):
            b = self.b
            for k in halves:
                self.numbers["core", k] = links.start(
                    lambda k=k: (b.full.at[(pl.ds(0, NS), 1 - core) + self.cut(k)], b.pair.at[(pl.ds(0, NS),) + self.cut(k)], mate)
                )

        def send_section(self, halves=(0, 1)):
            b = self.b
            for k in halves:
                links.arrived(self.numbers["core", k], b.pair.at[(pl.ds(0, NS),) + self.cut(k)], mate)
                links.left(self.numbers["core", k])
                for p in range(NS):
                    mine = b.full[(p, core) + self.cut(k)].astype(f32)
                    b.pair[(p,) + self.cut(k)] = (mine + b.pair[(p,) + self.cut(k)].astype(f32)).astype(bf16)
                for j in range(1, NS):
                    self.numbers["section", k, j] = links.start(
                        lambda k=k, j=j: (b.pair.at[(peers[j],) + self.cut(k)], b.sec.at[(j - 1,) + self.cut(k)], at_section[j])
                    )

        def section_sum(self, halves=(0, 1)):
            b = self.b
            for k in halves:
                total = b.pair[(sec,) + self.cut(k)].astype(f32)
                for j in range(1, NS):
                    there = (j - 1,) + self.cut(k)
                    links.arrived(self.numbers["section", k, j], b.sec.at[there], at_section[j])
                    total = total + b.sec[there].astype(f32)
                b.fin[core, k] = total.astype(bf16)

        def chip_start(self, step, halves=(0, 1)):
            for k in halves:
                bit = self.order(k)[step]
                near = step > 0

                def name(k=k, bit=bit, near=near):
                    land = self.b.land.at[(step, k) + self.part(k, True)]
                    return self.b.fin.at[(core, k) + self.part(k, near)], land, at_chip[bit]

                if step == 0 and self.halving:

                    def name(k=k, bit=bit):
                        here = (k,) + self.part(k, False)
                        return self.b.fin.at[(core,) + here], self.b.land.at[(0,) + here], at_chip[bit]

                self.numbers["chip", k] = links.start(name)

        def chip_end(self, step, halves=(0, 1)):
            for k in halves:
                bit = self.order(k)[step]
                number = self.numbers["chip", k]
                here = (k,) + self.part(k, True)
                links.arrived(number, self.b.land.at[(step,) + here], at_chip[bit])
                links.left(number)
                mine = self.b.fin[(core,) + here].astype(f32)
                self.b.fin[(core,) + here] = (mine + self.b.land[(step,) + here].astype(f32)).astype(bf16)

        def chip_spread(self, halves=(0, 1)):
            for k in halves if self.halving else ():
                self.numbers["spread", k] = links.start(
                    lambda k=k: (
                        self.b.fin.at[(core, k) + self.part(k, True)],
                        self.back(k, True),
                        at_chip[self.order(k)[0]],
                    )
                )

        def chip_spread_end(self, halves=(0, 1)):
            for k in halves if self.halving else ():
                links.arrived(self.numbers["spread", k], self.back(k, False), at_chip[self.order(k)[0]])
                self.b.fin[(core, k) + self.part(k, False)] = self.back(k, False)[...]

        def pair_start(self, halves=(0, 1)):
            for k in halves:
                self.numbers["pair", k] = links.start(lambda k=k: (self.b.fin.at[core, k], self.b.fin.at[core, k], mate))

        def pair_end(self, halves=(0, 1)):
            for k in halves:
                links.arrived(self.numbers["pair", k], self.b.fin.at[1 - core, k], mate)

    def by_section_rows(full, cols, value):
        n = D // NS // 2
        for p in range(NS):
            for c in range(2):
                full[p, c, :, cols] = value[(2 * p + c) * n : (2 * p + c + 1) * n, :].astype(bf16)

    sum_a2, sum_du, sum_dd = (Summed(b) for b in (r.t_a2, r.t_du, r.t_dd))
    sum_a1 = Summed(r.t_a1, False)
    out_copies = []

    def send_out(src, dst):
        c = pltpu.make_async_copy(src, dst, r.out_sems.at[len(out_copies)])
        c.start()
        out_copies.append(c)

    def mix_gather(experts, first):
        def step(i, carry):
            rows = pl.ds(pl.multiple_of(i * RP, RP), RP)
            task = jnp.zeros((RP, 1), jnp.int32) + r.v_task[sec, i]
            active = (lane < TASKS * EXPERTS) & (lane // EXPERTS == task)
            ga = jnp.zeros((RP, D), f32) if first else r.acc[rows, :]
            q8 = jnp.zeros((RP, 128), f32) if first else r.q8[rows, :]
            for j in experts:
                pick = onehot(r.pos_pad[rows, j : j + 1] == slot_lane)
                ga = ga + dot(pick, r.slot_out[0] if j == 0 else ga_in(j)[...])
                one = jnp.sum(nt(pick, r.q_out[0] if j == 0 else r.q_in[j]), axis=-1, keepdims=True)
                q8 = q8 + jnp.where(active & (lax.rem(lane, EXPERTS) == peers[j]), one, 0.0)
            if first:
                r.acc[rows, :] = ga
                r.q8[rows, :] = q8
                return carry
            a = r.a_s[rows, :]
            gl = (q8 - gates_of(a, task) * jnp.sum(q8, axis=-1, keepdims=True)).astype(bf16)
            ga = ga + nt(gl, r.w_rt[...])
            r.vec[V_R : V_R + 8, :] += tn(gl, a)[0:8, :]
            xhat, scale = normed(r.h3[rows, :].astype(f32))
            r.vec[V_M : V_M + 1, :] += column_sum(ga * xhat)
            r.vec[V_M + 1 : V_M + 2, :] += column_sum(ga)
            g = r.g3[rows, :].astype(f32)
            r.g2[rows, :] = (g + norm_back(ga, xhat, scale, vec.mixture_gain[...])).astype(bf16)
            return carry

        lax.fori_loop(0, IMG, step, 0)

    grads_back(3)
    mix_gather((0, 3), True)
    e_core_end(True)
    if bits > 1:
        e_step_start(1)
    grads_back(1)
    grads_back(2)
    for j in range(1, NS):
        links.start(lambda j=j: (r.gslot.at[j], w_in(j), at_section[j]), w_first + j)
    mix_gather((1, 2), False)

    def e_third():
        for step in range(1, bits):
            if step > 1:
                e_step_start(step)
            e_step_end(step)
        e_own()
        e_spread_start(1)

    def e_fourth():
        e_spread_end(1)
        e_spread_start(0)

    def e_fifth():
        e_spread_end(0)
        e_pair_start()

    attend_back(
        r.h2, r.g2, r.g1, att2, r.w_p2, r.w_o2, r.qkv2, r.p2, V_A2, {1: [e_third]}
    )
    for f in range(3):
        cols = slice(f * D, (f + 1) * D)
        by_section_rows(r.t_a2.full, cols, tn(r.a_s[...], r.qkv2[:, cols]))
    by_section_rows(r.t_a2.full, slice(3 * D, 4 * D), tn(r.ctx2[...], r.g2[...]))
    sum_a2.send_core()

    def dense_back(i, carry):
        rows = pl.ds(pl.multiple_of(i * HR, HR), HR)
        g = r.g1[rows, :]
        gf = g.astype(f32)
        xhat, scale = normed(r.h1[rows, :].astype(f32))
        r.a_s[rows, :] = (xhat * vec.dense_gain[...] + vec.dense_shift[...]).astype(bf16)
        ga = jnp.zeros((HR, D), f32)
        for f in range(NF):
            cols = slice(f * FC, (f + 1) * FC)
            gu = (nt(g, r.w_dn[cols, :]) * r.slope[rows, cols].astype(f32)).astype(bf16)
            r.slope[rows, cols] = gu
            r.vec[V_HB + f : V_HB + f + 1, :] += column_sum(gu.astype(f32))
            ga = ga + nt(gu, r.w_up[:, cols])
        r.vec[V_D : V_D + 1, :] += column_sum(ga * xhat)
        r.vec[V_D + 1 : V_D + 2, :] += column_sum(ga)
        r.vec[V_D + 2 : V_D + 3, :] += column_sum(gf)
        r.g0[rows, :] = (gf + norm_back(ga, xhat, scale, vec.dense_gain[...])).astype(bf16)
        at_steps({0: [sum_a2.send_section, e_fourth]}, i)
        return carry

    lax.fori_loop(0, 2, dense_back, 0)

    for f in range(NF):
        cols = slice(f * FC, (f + 1) * FC)
        by_section_rows(r.t_du.full, cols, tn(r.a_s[...], r.slope[:, cols]))
    sum_du.send_core()
    for f in range(NF):
        value = tn(r.z[:, f * FC : (f + 1) * FC], r.g1[...])
        n = FC // 2
        for c in range(2):
            r.t_dd.full[f, c] = value[c * n : (c + 1) * n, :].astype(bf16)
    sum_dd.send_core()
    sum_du.send_section()

    def chips_first(one, halves=(0, 1)):
        one.section_sum(halves)
        if bits > 0:
            one.chip_start(0, halves)

    def chips_rest(one, halves=(0, 1)):
        for step in range(1, bits):
            one.chip_end(step - 1, halves)
            one.chip_start(step, halves)

    def chips_spread(one):
        if bits > 0:
            one.chip_end(bits - 1)
        one.chip_spread()

    def chips_last(one, halves=(0, 1)):
        if one.halving:
            one.chip_spread_end(halves)
        elif bits > 0:
            one.chip_end(bits - 1, halves)
        one.pair_start(halves)

    a1 = r.t_a1.full
    by_section_rows(a1, slice(3 * D, 4 * D), tn(r.ctx1[...], r.g0[...]))
    values_back(r.h0, r.g0, att1, r.w_o1, r.p1, {1: [sum_dd.send_section]})
    by_section_rows(a1, slice(2 * D, 3 * D), tn(r.a_s[...], r.z[:, 0:D]))
    sum_a1.send_core((1,))
    chips_first(sum_a2)
    attend_back(
        r.h0, r.g0, r.g3, att1, r.w_p1, r.w_o1, r.qkv1, r.p1, V_A1,
        {
            0: [lambda: sum_a1.send_section((1,))],
            2: [lambda: chips_rest(sum_a2), lambda: chips_first(sum_du)],
        },
        True,
    )
    for f in range(2):
        cols = slice(f * D, (f + 1) * D)
        by_section_rows(a1, cols, tn(r.a_s[...], r.qkv1[:, cols]))
    sum_a1.send_core((0,))
    send_out(r.g3, r.o_grad)
    chips_spread(sum_a2)

    def vec_start(land, device):
        return links.start(lambda: (r.vec, r.vec_land.at[land], device)), land, device

    def vec_end(number, land, device):
        links.arrived(number, r.vec_land.at[land], device)
        links.left(number)

    vec_core = vec_start(0, mate)
    for j in range(1, NS):
        links.arrived(w_first + j, w_in(j), at_section[j])
    vec_section = []

    def vec_two():
        vec_end(*vec_core)
        r.vec[...] += r.vec_land[0]
        vec_section.extend(vec_start(j, at_section[j]) for j in range(1, NS))

    def block_out(i, carry):
        rows = pl.ds(pl.multiple_of(i * RP, RP), RP)
        total = r.h3[rows, :].astype(f32)
        for j in range(NS):
            pick = onehot(r.pos_pad[rows, j : j + 1] == slot_lane)
            total = total + dot(pick, r.gslot[0] if j == 0 else w_in(j)[...])
        r.h3[rows, :] = total.astype(bf16)
        at_steps({1: [lambda: sum_a1.send_section((0,)), vec_two, lambda: chips_rest(sum_du)]}, i)
        return carry

    lax.fori_loop(0, IMG, block_out, 0)
    send_out(r.h3, r.o_block)
    chips_last(sum_a2)
    chips_first(sum_dd)
    chips_first(sum_a1, (1,))
    chips_spread(sum_du)
    for one in vec_section:
        vec_end(*one)
    r.vec[...] += r.vec_land[1] + r.vec_land[2] + r.vec_land[3]
    vec_chip = vec_start(NS, at_chip[0]) if bits > 0 else None
    chips_first(sum_a1, (0,))
    chips_rest(sum_dd)
    chips_last(sum_du)
    e_fifth()
    for step in range(1, bits):
        for k in (1, 0):
            sum_a1.chip_end(step - 1, (k,))
            sum_a1.chip_start(step, (k,))
        vec_end(*vec_chip)
        r.vec[...] += r.vec_land[NS + step - 1]
        vec_chip = vec_start(NS + step, at_chip[step])
        if step == bits - 1:
            chips_spread(sum_dd)
    if bits < 2:
        chips_spread(sum_dd)
    chips_last(sum_dd)
    e_pair_end()
    send_out(r.e_all, r.o_expert.at[core])
    send_out(r.down, r.o_expert.at[1 - core])
    for s, dst in ((sum_a2, r.o_a2), (sum_du, r.o_du), (sum_dd, r.o_dd)):
        s.pair_end()
        send_out(s.b.fin, dst)
    for k in (1, 0):
        chips_last(sum_a1, (k,))
    if bits > 0:
        vec_end(*vec_chip)
        r.vec[...] += r.vec_land[NS + bits - 1]
    send_out(r.vec, r.o_vec)
    sum_a1.pair_end()
    send_out(r.t_a1.fin, r.o_a1)
    links.drain()
    for c in out_copies:
        c.wait()
    assert links.used <= NSEM and len(local) <= 40 and len(out_copies) <= 12, links.used


class Bag:
    def __init__(self, **members):
        self.__dict__.update(members)


VECTORS = (
    "first_gain",
    "first_shift",
    "first_bias",
    "dense_gain",
    "dense_shift",
    "hidden_bias",
    "dense_bias",
    "second_gain",
    "second_shift",
    "second_bias",
    "mixture_gain",
    "mixture_shift",
)
SMALL_IN = ("task", "routes", "keep", "router") + VECTORS


def run_blocks(bits, arrays):
    R, D = arrays["patches"].shape[1:]
    FF = arrays["expert_up"].shape[2]
    IMG = R // PATCHES
    RT = IMG * RP
    n = D // 8
    vm = pltpu.VMEM
    scratch = dict(
        pool=vm((max(4 * R, 6 * SL), D), bf16),
        chosen=vm((16, R), f32),
        pos_pad=vm((RT, 16), f32),
        w_p1=vm((D, 3 * D), bf16),
        w_o1=vm((D, D), bf16),
        w_up=vm((D, FF), bf16),
        w_dn=vm((FF, D), bf16),
        w_p2=vm((D, 3 * D), bf16),
        w_o2=vm((D, D), bf16),
        w_rt=vm((D, 128), bf16),
        rt=vm((4, 8, 128), f32),
        lines=vm((16, FF), f32),
        up=vm((FF // D, D, D), bf16),
        down=vm((FF // D, D, D), bf16),
        out_half=vm((3, SL, D), bf16),
        h0=vm((RT, D), bf16),
        h1=vm((RT, D), bf16),
        h2=vm((RT, D), bf16),
        h3=vm((RT, D), bf16),
        g0=vm((RT, D), bf16),
        g1=vm((RT, D), bf16),
        g2=vm((RT, D), bf16),
        g3=vm((RT, D), bf16),
        a_s=vm((RT, D), bf16),
        qkv1=vm((RT, 3 * D), bf16),
        qkv2=vm((RT, 3 * D), bf16),
        p1=vm((IMG * HEADS, RP, RP), bf16),
        p2=vm((IMG * HEADS, RP, RP), bf16),
        ctx1=vm((RT, D), bf16),
        ctx2=vm((RT, D), bf16),
        z=vm((RT, FF), bf16),
        slope=vm((RT, FF), bf16),
        slot_out=vm((4, SL, D), bf16),
        slot_in=vm((3, SL, D), bf16),
        gslot=vm((4, SL, D), bf16),
        tslot=vm((SL, 128), f32),
        q_out=vm((4, 16, SL), bf16),
        q_in=vm((4, 16, SL), bf16),
        acc=vm((2 * SL, D), f32),
        q8=vm((RT, 128), f32),
        eg=vm((2, 4, D, D), f32),
        e_sum=vm((4, D, D), bf16),
        e_land=vm((2, D, D), bf16),
        e_land2=vm((max(bits - 1, 1), 2, D // 2, D), bf16),
        e_all=vm((4, D, D), bf16),
        vec=vm((VROWS, D), f32),
        vec_land=vm((4 + max(bits, 1), VROWS, D), f32),
        send=pltpu.SemaphoreType.DMA((NSEM,)),
        recv=pltpu.SemaphoreType.DMA((NSEM,)),
        local=pltpu.SemaphoreType.DMA((40,)),
        out_sems=pltpu.SemaphoreType.DMA((12,)),
    )
    for name in SMALL_IN:
        space = pltpu.SMEM if name == "task" else vm
        scratch["v_" + name] = space(arrays[name].shape, arrays[name].dtype)
    sums = dict(t_a2=False, t_du=False, t_dd=True, t_a1=False)
    fin = {}
    for name, by_rows in sums.items():
        rows, cols = (D // 2, D) if by_rows else (n, FF)
        halved = (rows // 2, cols) if by_rows else (rows, cols // 2)
        if name in ("t_a2", "t_dd"):
            scratch[name + ".full"] = vm((4, 2, rows, cols), bf16)
        scratch[name + ".pair"] = vm((4, rows, cols), bf16)
        scratch[name + ".sec"] = vm((3, rows, cols), bf16)
        scratch[name + ".fin"] = vm((2, 2) + halved, bf16)
        scratch[name + ".land"] = vm((max(bits, 1), 2) + halved, bf16)
        fin[name] = jax.ShapeDtypeStruct((2, 2) + halved, bf16)
    outs = dict(
        o_block=jax.ShapeDtypeStruct((RT, D), bf16),
        o_grad=jax.ShapeDtypeStruct((RT, D), bf16),
        o_expert=jax.ShapeDtypeStruct((2, 4, D, D), bf16),
        o_a2=fin["t_a2"],
        o_du=fin["t_du"],
        o_dd=fin["t_dd"],
        o_a1=fin["t_a1"],
        o_vec=jax.ShapeDtypeStruct((VROWS, D), f32),
    )
    ins = list(arrays)
    names = ins + list(outs) + list(scratch)

    def body(*refs):
        members = {}
        for name, ref in zip(names, refs, strict=True):
            if "." in name:
                outer, inner = name.split(".")
                members.setdefault(outer, Bag(by_rows=sums[outer])).__dict__[inner] = ref
            else:
                members[name] = ref
        for name in ("t_du", "t_a1"):
            members[name].full = members["t_a2"].full
        block_kernel(bits, Bag(**members))

    return pl.pallas_call(
        body,
        out_shape=list(outs.values()),
        in_specs=[pl.BlockSpec(memory_space=pl.ANY)] * len(ins),
        out_specs=[pl.BlockSpec(memory_space=pl.ANY)] * len(outs),
        scratch_shapes=list(scratch.values()),
        compiler_params=pltpu.CompilerParams(
            collective_id=0, has_side_effects=True, vmem_limit_bytes=64 * 2**20 - 2**17
        ),
        name="blocks",
    )(*arrays.values())


FINISHED = ("block", "grad", "expert", "a2", "du", "dd", "a1", "vec")
BIG = ("block", "grad", "p1", "o1", "up", "dn", "p2", "o2", "eup", "edn")


def finish_kernel(r):
    RT, D = r.block.shape
    R = r.o_block.shape[1]
    sec = lax.axis_index("section")
    copies = {}
    for k, name in enumerate(FINISHED):
        copies[name] = pltpu.make_async_copy(getattr(r, name), getattr(r, "v_" + name), r.sems.at[k])
        copies[name].start()
    outs = []

    def send(name):
        c = pltpu.make_async_copy(getattr(r, "w_" + name), getattr(r, "o_" + name), r.sems.at[len(FINISHED) + len(outs)])
        c.start()
        outs.append(c)

    row, col = iota((R, RP), 0), iota((R, RP), 1)
    for name in ("block", "grad"):
        copies[name].wait()
        src, dst = getattr(r, "v_" + name), getattr(r, "w_" + name)
        total = jnp.zeros((R, D), f32)
        for i in range(R // PATCHES):
            pick = onehot((row - i * PATCHES == col) & (col < PATCHES))
            total = total + dot(pick, src[i * RP : (i + 1) * RP, :])
        dst[0] = total.astype(bf16)
        send(name)
    copies["expert"].wait()
    for b in range(4):
        r.w_eup[0, :, b * D : (b + 1) * D] = r.v_expert[0, b].astype(f32)
    send("eup")
    for b in range(4):
        r.w_edn[0, b * D : (b + 1) * D, :] = r.v_expert[1, b].astype(f32)
    send("edn")
    n = D // 8
    for k in ("2", "1"):
        copies["a" + k].wait()
        src, dst_p, dst_o = getattr(r, "v_a" + k), getattr(r, "w_p" + k), getattr(r, "w_o" + k)
        for c in range(2):
            rows = slice(c * n, (c + 1) * n)
            dst_p[rows, 0 : 2 * D] = src[c, 0].astype(f32)
            dst_p[rows, 2 * D : 3 * D] = src[c, 1, :, 0:D].astype(f32)
            dst_o[rows, :] = src[c, 1, :, D : 2 * D].astype(f32)
        send("p" + k)
        send("o" + k)
    copies["du"].wait()
    for c in range(2):
        for k in range(2):
            r.w_up[c * n : (c + 1) * n, k * 2 * D : (k + 1) * 2 * D] = r.v_du[c, k].astype(f32)
    send("up")
    copies["dd"].wait()
    m = r.v_dd.shape[2]
    for c in range(2):
        for k in range(2):
            at = (2 * c + k) * m
            r.w_dn[at : at + m, :] = r.v_dd[c, k].astype(f32)
    send("dn")
    copies["vec"].wait()
    q = D // 4
    mine = jnp.where(iota((D, q), 0) == iota((D, q), 1) + sec * q, 1.0, 0.0)
    cut = jnp.dot(r.v_vec[...], mine, precision=lax.Precision.HIGHEST, preferred_element_type=f32)
    for dst, at in (
        (r.o_g1, V_A1), (r.o_s1, V_A1 + 1), (r.o_b1, V_A1 + 2), (r.o_gd, V_D), (r.o_sd, V_D + 1), (r.o_db, V_D + 2),
        (r.o_g2, V_A2), (r.o_s2, V_A2 + 1), (r.o_b2, V_A2 + 2), (r.o_gm, V_M), (r.o_sm, V_M + 1),
    ):
        dst[...] = cut[at : at + 1, :]
    r.o_rt[...] = cut[V_R : V_R + 8, :]
    r.o_hb[...] = r.v_vec[pl.ds(V_HB + sec, 1), :].reshape(-1)
    for c in outs:
        c.wait()


def finish(parts, shape):
    R, D, FF = shape
    q = D // 4
    s = lambda *dims: jax.ShapeDtypeStruct(dims, f32)
    rows = jax.ShapeDtypeStruct((1, R, D), bf16)
    outs = dict(
        block=rows, grad=rows,
        g1=s(1, q), s1=s(1, q), p1=s(q, 3 * D), o1=s(q, D), b1=s(1, q),
        gd=s(1, q), sd=s(1, q), up=s(q, FF), hb=s(FF // 4), dn=s(FF // 4, D), db=s(1, q),
        g2=s(1, q), s2=s(1, q), p2=s(q, 3 * D), o2=s(q, D), b2=s(1, q),
        gm=s(1, q), sm=s(1, q), rt=s(8, q), eup=s(1, D, FF), edn=s(1, FF, D),
    )
    scratch = {"v_" + name: pltpu.VMEM(part.shape, part.dtype) for name, part in zip(FINISHED, parts)}
    scratch |= {"w_" + name: pltpu.VMEM(outs[name].shape, outs[name].dtype) for name in BIG}
    scratch["sems"] = pltpu.SemaphoreType.DMA((len(FINISHED) + len(BIG),))
    names = list(FINISHED) + ["o_" + name for name in outs] + list(scratch)
    anywhere, near = pl.BlockSpec(memory_space=pltpu.HBM), pl.BlockSpec(memory_space=pltpu.VMEM)

    def body(*refs):
        finish_kernel(Bag(**dict(zip(names, refs, strict=True))))

    return pl.pallas_call(
        body,
        out_shape=list(outs.values()),
        in_specs=[anywhere] * len(FINISHED),
        out_specs=[anywhere if name in BIG else near for name in outs],
        scratch_shapes=list(scratch.values()),
        compiler_params=pltpu.CompilerParams(vmem_limit_bytes=62 * 2**20),
        name="finish",
    )(*parts)


def local(
    patches_in, cotangent, task_ids, routes, keep_mask,
    first_gain, first_shift, first_proj, first_out, first_bias,
    dense_gain, dense_shift, dense_up, hidden_bias, dense_down, dense_bias,
    second_gain, second_shift, second_proj, second_out, second_bias,
    mixture_gain, mixture_shift, router, expert_up, expert_down,
):
    bits = (lax.axis_size("wide") // 2).bit_length() - 1
    arrays = dict(
        patches=patches_in,
        cotangent=cotangent,
        task=task_ids,
        routes=jnp.transpose(routes, (0, 2, 1)),
        keep=jnp.transpose(keep_mask, (0, 2, 1)),
        s_p1=first_proj,
        s_o1=first_out,
        s_up=dense_up,
        s_dn=dense_down,
        s_p2=second_proj,
        s_o2=second_out,
        router=router.T,
        expert_up=expert_up,
        expert_down=expert_down,
        first_gain=first_gain,
        first_shift=first_shift,
        first_bias=first_bias,
        dense_gain=dense_gain,
        dense_shift=dense_shift,
        hidden_bias=hidden_bias,
        dense_bias=dense_bias,
        second_gain=second_gain,
        second_shift=second_shift,
        second_bias=second_bias,
        mixture_gain=mixture_gain,
        mixture_shift=mixture_shift,
    )
    parts = run_blocks(bits, arrays)
    R, D = patches_in.shape[1:]
    outs = list(finish(parts, (R, D, expert_up.shape[2])))
    for at in (2, 3, 6, 7, 8, 12, 13, 14, 17, 18, 19):
        outs[at] = outs[at].reshape(-1)
    outs[20] = outs[20].T
    return tuple(outs)


def solution(mesh):
    rows, vec, mat = P(None, "wide", None), P(), P("section", None)
    cube = P("section", None, None)
    in_specs = (
        rows, rows, P(None, "wide"), rows, rows,
        vec, vec, mat, mat, vec,
        vec, vec, mat, vec, mat, vec,
        vec, vec, mat, mat, vec,
        vec, vec, mat, cube, cube,
    )
    cut, moved = P("section"), P("section", "wide", None)
    out_specs = (
        moved, moved,
        cut, cut, mat, mat, cut,
        cut, cut, mat, cut, mat, cut,
        cut, cut, mat, mat, cut,
        cut, cut, mat, cube, cube,
    )
    return jax.shard_map(local, mesh=mesh, in_specs=in_specs, out_specs=out_specs, check_vma=False)
```
